32 devices in a mesh: dom: 16 (over z, y, x), rep: 2 (over core).
Axes of the slice: x: 2, y: 2, z: 4, core: 2. Of those that a mesh axis runs over, the one named last changes fastest.
Arguments:
- features: bfloat16 [8192, 256], P('dom'), may hold values from -6 to 6
- weight: bfloat16 [256, 256], replicated, may hold values from -0.375 to 0.375
- grad_out: bfloat16 [8192, 256], P('dom'), may hold values from -6 to 6
- tiles: bfloat16 [16, 16, 512, 512], P('dom', 'rep'), may hold values from -0.125 to 0.125
- tile_mask: int32 [16, 16], P('dom', 'rep'), may hold values from 0 to 1, as said below
Outputs:
- activated: bfloat16 [8192, 256], P('dom')
- feature_grad: bfloat16 [8192, 256], P('dom')
- weight_grad: float32 [256, 256], replicated
The draws below stay inside these ranges and needn't reach their ends.
Inputs may be any that keep to these rules, and one draw needn't show every extreme that they name: `tile_mask`: the diagonal tiles (offset 0) are always present; other tiles are sparse, more frequent near the diagonal (small offsets or offsets near 16), and some row blocks hold many more tiles than others.
All inputs are finite; a program needn't handle non-finite values.
Results may differ from the reference program's by a relative error of at most 0.007.
Values may be sent and summed in bfloat16 or wider, within the bound.
A program may use at most 64 MiB of HBM per device.

```python
import jax
import jax.numpy as jnp
from jax import lax

ROWS_DEV = 512
HIDDEN_SIZE = 256
BLOCKS = 16
NODES = 8192


def draw_tile_mask(key, part):
    key = jax.random.fold_in(key, 11)
    heavy_key, roll_key = jax.random.split(key)
    offsets = jnp.arange(BLOCKS, dtype=jnp.int32)
    distance = jnp.minimum(offsets, BLOCKS - offsets)
    safe_distance = jnp.maximum(distance, 1)
    chance = 500 // (safe_distance * safe_distance) + 40
    heavy = jnp.where(jax.random.randint(heavy_key, (BLOCKS, 1), 0, 4) == 0, 3, 1).astype(jnp.int32)
    roll = jax.random.randint(roll_key, (BLOCKS, BLOCKS), 0, 1000)
    present = (roll < chance[None, :] * heavy).astype(jnp.int32)
    return jnp.where(distance[None, :] == 0, 1, present).astype(jnp.int32)


def level_of(key, dims, shards, least, largest):
    gain, own = 1.0, jax.random.fold_in(key, 6)
    for position, shards_of in shards:
        heights = jnp.exp(jax.random.uniform(jax.random.fold_in(own, position), (shards_of,), jnp.float32, least / len(shards), largest / len(shards)))
        gain = gain * jnp.repeat(heights, dims[position] // shards_of).reshape([-1 if axis == position else 1 for axis in range(len(dims))])
    return gain


def bell_draw(stream_key, dims, deviation, bound, pieces=(), kind=jnp.bfloat16):
    entries = deviation * jax.random.normal(stream_key, dims, jnp.float32)
    if pieces:
        entries = entries * level_of(stream_key, dims, pieces, -0.22, 0.18)
    return jnp.clip(entries, -bound, bound).astype(kind)


def setup_inputs(seed: int = 0) -> dict:
    key_list = jax.random.split(jax.random.key(seed), 6)
    features = bell_draw(key_list[0], (NODES, HIDDEN_SIZE), 1.0, 6.0, ((0, 16),))
    weight = bell_draw(key_list[1], (HIDDEN_SIZE, HIDDEN_SIZE), HIDDEN_SIZE ** -0.5, 0.375)
    grad_out = bell_draw(key_list[2], (NODES, HIDDEN_SIZE), 1.0, 6.0, ((0, 16),))
    tiles = bell_draw(key_list[3], (BLOCKS, BLOCKS, ROWS_DEV, ROWS_DEV), (4 * ROWS_DEV) ** -0.5, 0.125, ((0, 16), (1, 2)))
    tile_mask = draw_tile_mask(jax.random.fold_in(key_list[5], 71), 0)
    return {"features": features, "weight": weight, "grad_out": grad_out, "tiles": tiles, "tile_mask": tile_mask}


def reference(features, weight, grad_out, tiles, tile_mask):
    projected = jnp.dot(features, weight, preferred_element_type=jnp.float32).astype(jnp.bfloat16)
    blocks = projected.reshape(BLOCKS, ROWS_DEV, HIDDEN_SIZE)
    offsets = jnp.arange(BLOCKS, dtype=jnp.int32)

    def row_sum(i):
        columns = ((i - offsets) % BLOCKS).astype(jnp.int32)
        weight_flag = tile_mask[i].astype(jnp.float32)
        tile_block = tiles[i].astype(jnp.float32) * weight_flag[:, None, None]
        return jnp.einsum('orc,ocf->rf', tile_block, blocks[columns].astype(jnp.float32))

    total = lax.map(row_sum, offsets).reshape(NODES, HIDDEN_SIZE)
    gate_value = jax.nn.sigmoid(total)
    activated = (total * gate_value).astype(jnp.bfloat16)
    score_grad = (grad_out.astype(jnp.float32) * gate_value * (1.0 + total * (1.0 - gate_value))).astype(jnp.bfloat16)
    score_blocks = score_grad.reshape(BLOCKS, ROWS_DEV, HIDDEN_SIZE)

    def column_sum(j):
        row_ids = ((j + offsets) % BLOCKS).astype(jnp.int32)
        weight_flag = tile_mask[row_ids, offsets].astype(jnp.float32)
        tile_block = tiles[row_ids, offsets].astype(jnp.float32) * weight_flag[:, None, None]
        return jnp.einsum('orc,orf->cf', tile_block, score_blocks[row_ids].astype(jnp.float32))

    node_grad = lax.map(column_sum, offsets).reshape(NODES, HIDDEN_SIZE).astype(jnp.bfloat16)
    feature_grad = jnp.dot(node_grad, weight.T, preferred_element_type=jnp.float32).astype(jnp.bfloat16)
    weight_grad = jnp.dot(features.T, node_grad, preferred_element_type=jnp.float32) * (NODES ** -0.5)
    return activated, feature_grad, weight_grad
```

```python
import functools

import jax
import jax.numpy as jnp
from jax import lax
from jax.experimental import pallas as pl
from jax.experimental.pallas import tpu as pltpu
from jax.sharding import PartitionSpec as P

MESH = pl.DeviceIdType.MESH
F32 = jnp.float32
BF16 = jnp.bfloat16


def shifted_2(block, axis, distance):
    devices = range(lax.axis_size(axis))
    route = [((i - distance) % len(devices), i) for i in devices]
    return lax.ppermute(block, axis, route)


def tile_product(tile, weight_flag, operand, transposed):
    if transposed:
        contraction = (((0,), (0,)), ((), ()))
        out_rows = tile.shape[1]
    else:
        contraction = (((1,), (0,)), ((), ()))
        out_rows = tile.shape[0]

    def compute():
        return lax.dot_general(tile, operand, contraction, preferred_element_type=jnp.float32)

    def skipped():
        return jnp.zeros((out_rows, operand.shape[1]), jnp.float32)

    return lax.cond(weight_flag > 0, compute, skipped)


def ring_shards(features, weight, grad_out, tiles, tile_mask):
    domains = lax.axis_size("dom")
    replicas = lax.axis_size("rep")
    sections = domains // replicas
    replica = lax.axis_index("rep")
    bit_count = replicas.bit_length() - 1
    rows_here = features.shape[0]
    hidden = features.shape[1]
    projected = jnp.dot(features, weight, preferred_element_type=jnp.float32).astype(jnp.bfloat16)
    current = projected
    for level in range(bit_count):
        shifted = shifted_2(current, "dom", sections << level)
        current = jnp.where(replica >> level & 1 == 1, shifted, current)
    partial_value = jnp.zeros((rows_here, hidden), jnp.float32)
    for section in range(sections):
        if section > 0:
            current = shifted_2(current, "dom", 1)
        partial_value = partial_value + tile_product(
            tiles[0, section], tile_mask[0, section], current, False
        )
    total = lax.psum(partial_value, "rep")
    gate_value = jax.nn.sigmoid(total)
    activated = (total * gate_value).astype(jnp.bfloat16)
    score_grad = (
        grad_out.astype(jnp.float32) * gate_value * (1.0 + total * (1.0 - gate_value))
    ).astype(jnp.bfloat16)
    carried = tile_product(tiles[0, sections - 1], tile_mask[0, sections - 1], score_grad, True)
    for section in range(sections - 2, -1, -1):
        carried = shifted_2(carried, "dom", -1)
        carried = carried + tile_product(tiles[0, section], tile_mask[0, section], score_grad, True)
    for level in range(bit_count):
        shifted = shifted_2(carried, "dom", -(sections << level))
        carried = jnp.where(replica >> level & 1 == 1, shifted, carried)
    node_grad = lax.psum(carried, "rep").astype(jnp.bfloat16)
    feature_grad = lax.dot_general(
        node_grad, weight, (((1,), (1,)), ((), ())), preferred_element_type=jnp.float32
    ).astype(jnp.bfloat16)
    scaling = (rows_here * domains) ** (-0.5)
    weight_term = lax.dot_general(
        features, node_grad, (((0,), (0,)), ((), ())), preferred_element_type=jnp.float32
    )
    weight_grad = lax.psum(weight_term, "dom") * scaling
    return (activated, feature_grad, weight_grad)


def layer_kernel(
    domains, scaling,
    x_ref, w_ref, g_ref, tiles_hbm, mask_ref,
    act_ref, fg_ref, wg_ref,
    tiles, xs, ps, from_b, from_a, from_z, part, part_in, ax, st, ws, w_in, w_full, fg_half,
    tile_sem, x_recv, x_recv_p, x_send_z, x_send_a, x_send_b, x_send_p,
    part_send, part_recv,
    p_recv_p, p_send_p, b_send, b_recv, a_send, a_recv, z_send, z_recv,
    w_send, w_recv, last_send, last_recv,
):
    layers = domains // 4
    levels = 2 + layers.bit_length() - 1
    sections = domains // 2
    half = x_ref.shape[0] // 2
    hidden = x_ref.shape[1]
    d = lax.axis_index("dom")
    c = lax.axis_index("rep")
    other = 1 - c
    step_a, step_b = 1 + c, 2 - c
    z = d // 4
    a = (d // step_a) % 2
    b = (d // step_b) % 2

    def block_at(z_, b_, a_):
        return z_ * 4 + b_ * step_b + a_ * step_a

    dev_a, dev_b = block_at(z, b, 1 - a), block_at(z, 1 - b, a)
    far = []
    for level in range(1, layers.bit_length() - 1):
        dist = 1 << level
        far.append(block_at(z + dist * (1 - 2 * ((z // dist) % 2)), b, a))
    dev_z1 = block_at(z + (1 - 2 * (z % 2)), b, a)

    def copy_to(src, dst, send, recv, dom, rep):
        return pltpu.make_async_remote_copy(
            src_ref=src, dst_ref=dst, send_sem=send, recv_sem=recv,
            device_id=(dom, rep), device_id_type=MESH,
        )

    barrier = pltpu.get_barrier_semaphore()
    for dom, rep in [(dev_a, c), (dev_b, c), (d, other)] + [(f, c) for f in far]:
        pl.semaphore_signal(barrier, inc=1, device_id=(dom, rep), device_id_type=MESH)

    @pl.when(z > 0)
    def _():
        pl.semaphore_signal(barrier, inc=1, device_id=(d - 4, c), device_id_type=MESH)

    @pl.when(z < layers - 1)
    def _():
        pl.semaphore_signal(barrier, inc=1, device_id=(d + 4, c), device_id_type=MESH)

    ends = jnp.where(z > 0, 1, 0) + jnp.where(z < layers - 1, 1, 0)
    pl.semaphore_wait(barrier, 3 + len(far) + ends)

    def owner(j):
        return ((d - j + domains) % domains) // sections

    def x_copy_z(j, z_, up):
        return copy_to(xs.at[j, c], xs.at[j, c], x_send_z.at[up, z_], x_recv.at[j], d - 4 + 8 * up, c)

    def x_copy_a(j, z_):
        return copy_to(xs.at[j, c], xs.at[j, c], x_send_a.at[z_], x_recv.at[j], dev_a, c)

    def x_copy_b(j, z_, a_):
        return copy_to(xs.at[j, c], xs.at[j, c], x_send_b.at[z_, a_], x_recv.at[j], dev_b, c)

    def x_copy_p(j):
        return copy_to(xs.at[j, c], xs.at[j, c], x_send_p.at[j], x_recv_p.at[j], d, other)

    def x_arrive(j):
        copy_to(xs.at[j, c], xs.at[j, c], x_send_p.at[j], x_recv.at[j], d, other).wait_recv()

        @pl.when(owner(j) != c)
        def _():
            x_copy_p(j).start()

    xs[d, 0] = x_ref[pl.ds(0, half), :]
    xs[d, 1] = x_ref[pl.ds(half, half), :]

    @pl.when(z > 0)
    def _():
        x_copy_z(d, z, 0).start()

    @pl.when(z < layers - 1)
    def _():
        x_copy_z(d, z, 1).start()

    x_copy_b(d, z, a).start()
    x_copy_a(d, z).start()
    tile_copy = pltpu.make_async_copy(tiles_hbm.at[0], tiles, tile_sem)
    tile_copy.start()

    def layer_of(n):
        return z + ((n + 1) // 2) * (2 * ((n + 1) % 2) - 1)

    def in_range(z_):
        return jnp.logical_and(z_ >= 0, z_ < layers)

    def from_layer(n):
        z_ = layer_of(n)

        @pl.when(in_range(z_))
        def _():
            j = block_at(z_, b, a)
            x_arrive(j)

            @pl.when(jnp.logical_and(z_ < z, z < layers - 1))
            def _():
                x_copy_z(j, z_, 1).start()

            @pl.when(jnp.logical_and(z_ > z, z > 0))
            def _():
                x_copy_z(j, z_, 0).start()

            x_copy_b(j, z_, a).start()
            x_copy_a(j, z_).start()

    def from_a_side(n):
        z_ = layer_of(n)

        @pl.when(in_range(z_))
        def _():
            j = block_at(z_, b, 1 - a)
            x_arrive(j)
            x_copy_b(j, z_, 1 - a).start()

    def from_b_side(n):
        z_ = layer_of(n)

        @pl.when(in_range(z_))
        def _():
            x_arrive(block_at(z_, 1 - b, a))
            x_arrive(block_at(z_, 1 - b, 1 - a))

    visits = 2 * layers - 1

    def gather_step(n, carry):
        @pl.when(n < visits)
        def _():
            from_layer(n)

        @pl.when(n >= 2)
        def _():
            from_a_side(n - 2)

        return carry

    lax.fori_loop(1, visits + 2, gather_step, 0)

    def gather_end(n, carry):
        from_b_side(n)
        return carry

    lax.fori_loop(0, visits, gather_end, 0)

    def wait_partner_x(j, carry):
        @pl.when(jnp.logical_and(owner(j) == c, j != d))
        def _():
            copy_to(xs.at[j, other], xs.at[j, other], x_send_p.at[j], x_recv_p.at[j], d, other).wait_recv()

        return carry

    lax.fori_loop(0, domains, wait_partner_x, 0)
    tile_copy.wait()

    def flag(o):
        return jnp.where(mask_ref[0, o] > 0, 1.0, 0.0)

    def part_copy(r):
        return copy_to(part.at[r], part_in.at[r], part_send.at[r], part_recv.at[r], d, other)

    for r in range(2):
        part[r] = jnp.zeros((half, hidden), F32)

        def forward(o, carry, r=r):
            j = (d - c * sections - o + 2 * domains) % domains
            m = flag(o).astype(BF16)
            rows = pl.ds(r * half, half)
            part[r] += jnp.dot(
                tiles[o, rows, pl.ds(0, half)], xs[j, 0] * m, preferred_element_type=F32
            ) + jnp.dot(tiles[o, rows, pl.ds(half, half)], xs[j, 1] * m, preferred_element_type=F32)
            return carry

        lax.fori_loop(0, sections, forward, 0)
        part_copy(r).start()

    for r in range(2):
        part_copy(r).wait_recv()
        rows = pl.ds(r * half, half)
        ax_here = (part[r] + part_in[r]).astype(BF16)
        ax[rows, :] = ax_here
        total = jnp.dot(ax_here, w_ref[...], preferred_element_type=F32)
        gate = jax.nn.sigmoid(total)
        act_ref[rows, :] = (total * gate).astype(BF16)
        score = g_ref[rows, :].astype(F32) * gate * (1.0 + total * (1.0 - gate))
        st[:, rows] = jnp.transpose(score).astype(BF16)

    quarter = hidden // 2
    w_peers = [dev_a, dev_b, dev_z1] + far
    w_peers = w_peers[:levels]

    def w_copy(level):
        return copy_to(
            ws.at[level], w_in.at[level], w_send.at[level], w_recv.at[level], w_peers[level], c
        )

    ws[0] = jnp.dot(
        st[pl.ds(pl.multiple_of(c * quarter, quarter), quarter), :], ax[...],
        preferred_element_type=F32,
    )

    def target_layer(t):
        return jnp.where(t % 2 == 0, layers - 1 - t // 2, t // 2)

    def piece(k):
        z_ = target_layer(k // 4)
        q = k % 4
        b_ = jnp.where(q < 2, 1 - b, b)
        a_ = jnp.where(q % 2 == 0, 1 - a, a)
        return z_, b_, a_, block_at(z_, b_, a_)

    def p_copy(j):
        return copy_to(ps.at[j, other], ps.at[j, other], p_send_p.at[j], p_recv_p.at[j], d, other)

    def b_copy(z_, a_):
        return copy_to(
            ps.at[block_at(z_, 1 - b, a_), c], from_b.at[z_, a_], b_send.at[z_, a_], b_recv.at[z_, a_],
            dev_b, c,
        )

    def a_copy(z_):
        return copy_to(
            ps.at[block_at(z_, b, 1 - a), c], from_a.at[z_], a_send.at[z_], a_recv.at[z_], dev_a, c
        )

    def z_copy(z_, up):
        return copy_to(
            ps.at[block_at(z_, b, a), c], from_z.at[up, z_], z_send.at[z_], z_recv.at[up, z_],
            d - 4 + 8 * up, c,
        )

    def backward(k, carry):
        z_, b_, a_, j = piece(k)

        @pl.when(owner(j) == c)
        def _():
            o = (d - j + domains) % domains - c * sections
            m = flag(o)
            for h in range(2):
                ps[j, h] = (
                    jnp.dot(st[...], tiles[o, :, pl.ds(h * half, half)], preferred_element_type=F32) * m
                ).astype(BF16)
            p_copy(j).start()

            @pl.when(b_ != b)
            def _():
                b_copy(z_, a_).start()

        return carry

    lax.fori_loop(0, domains, backward, 0)

    def relay_partner(k, carry):
        z_, b_, a_, j = piece(k)

        @pl.when(owner(j) != c)
        def _():
            copy_to(ps.at[j, c], ps.at[j, c], p_send_p.at[j], p_recv_p.at[j], d, other).wait_recv()

            @pl.when(b_ != b)
            def _():
                b_copy(z_, a_).start()

        return carry

    lax.fori_loop(0, domains, relay_partner, 0)
    w_copy(0).start()

    def stage_a(t):
        z_ = target_layer(t)
        b_copy(z_, 1 - a).wait_recv()
        j = block_at(z_, b, 1 - a)
        ps[j, c] = (ps[j, c].astype(F32) + from_b[z_, 1 - a].astype(F32)).astype(BF16)
        a_copy(z_).start()

    def stage_z(t):
        z_ = target_layer(t)
        b_copy(z_, a).wait_recv()
        a_copy(z_).wait_recv()
        j = block_at(z_, b, a)

        def mine():
            return ps[j, c].astype(F32) + from_b[z_, a].astype(F32) + from_a[z_].astype(F32)

        @pl.when(z_ == z)
        def _():
            part[0] = mine()

        @pl.when(z_ > z)
        def _():
            @pl.when(z > 0)
            def _():
                z_copy(z_, 1).wait_recv()
                ps[j, c] = (mine() + from_z[1, z_].astype(F32)).astype(BF16)

            @pl.when(z == 0)
            def _():
                ps[j, c] = mine().astype(BF16)

            z_copy(z_, 1).start()

        @pl.when(z_ < z)
        def _():
            @pl.when(z < layers - 1)
            def _():
                z_copy(z_, 0).wait_recv()
                ps[j, c] = (mine() + from_z[0, z_].astype(F32)).astype(BF16)

            @pl.when(z == layers - 1)
            def _():
                ps[j, c] = mine().astype(BF16)

            z_copy(z_, 0).start()

    for r in range(2):
        part_copy(r).wait_send()

    stages = max(layers + 1, levels)
    for t in range(stages):
        if t < layers:
            stage_a(t)
        if 1 <= t <= layers:
            stage_z(t - 1)
        if t < levels:
            w_copy(t).wait_recv()
            ws[t + 1] = ws[t] + w_in[t]
            if t + 1 < levels:
                w_copy(t + 1).start()

    w_full[c] = ws[levels]
    w_last = copy_to(w_full.at[c], w_full.at[c], last_send.at[0], last_recv.at[0], d, other)
    w_last.start()

    @pl.when(z > 0)
    def _():
        z_copy(z, 1).wait_recv()
        part[0] += from_z[1, z].astype(F32)

    @pl.when(z < layers - 1)
    def _():
        z_copy(z, 0).wait_recv()
        part[0] += from_z[0, z].astype(F32)

    node = jnp.transpose(part[0]).astype(BF16)
    fg_half[c] = lax.dot_general(
        node, w_ref[...], (((1,), (1,)), ((), ())), preferred_element_type=F32
    ).astype(BF16)
    f_last = copy_to(fg_half.at[c], fg_half.at[c], last_send.at[1], last_recv.at[1], d, other)
    f_last.start()

    copy_to(w_full.at[other], w_full.at[other], last_send.at[0], last_recv.at[0], d, other).wait_recv()
    for h in range(2):
        wg_ref[:, pl.ds(h * quarter, quarter)] = jnp.transpose(w_full[h]) * scaling

    def drain_p(j, carry):
        @pl.when(jnp.logical_and(owner(j) != c, j != d))
        def _():
            x_copy_p(j).wait_send()

        @pl.when(owner(j) == c)
        def _():
            p_copy(j).wait_send()

        return carry

    lax.fori_loop(0, domains, drain_p, 0)

    def drain(z_, carry):
        @pl.when(jnp.logical_and(z_ <= z, z < layers - 1))
        def _():
            x_copy_z(block_at(z_, b, a), z_, 1).wait_send()

        @pl.when(jnp.logical_and(z_ >= z, z > 0))
        def _():
            x_copy_z(block_at(z_, b, a), z_, 0).wait_send()

        x_copy_a(block_at(z_, b, a), z_).wait_send()
        a_copy(z_).wait_send()
        for a_ in range(2):
            x_copy_b(block_at(z_, b, a_), z_, a_).wait_send()
            b_copy(z_, a_).wait_send()

        @pl.when(z_ > z)
        def _():
            z_copy(z_, 1).wait_send()

        @pl.when(z_ < z)
        def _():
            z_copy(z_, 0).wait_send()

        return carry

    lax.fori_loop(0, layers, drain, 0)
    for level in range(levels):
        w_copy(level).wait_send()
    copy_to(fg_half.at[other], fg_half.at[other], last_send.at[1], last_recv.at[1], d, other).wait_recv()
    for h in range(2):
        fg_ref[pl.ds(h * half, half), :] = fg_half[h]
    w_last.wait_send()
    f_last.wait_send()


def kernel_shards(features, weight, grad_out, tiles, tile_mask):
    domains = lax.axis_size("dom")
    layers = domains // 4
    levels = 2 + layers.bit_length() - 1
    sections = tiles.shape[1]
    rows, hidden = features.shape
    half, quarter = rows // 2, hidden // 2
    dma = pltpu.SemaphoreType.DMA
    vmem = pl.BlockSpec(memory_space=pltpu.VMEM)
    return pl.pallas_call(
        functools.partial(layer_kernel, domains, float((rows * domains) ** (-0.5))),
        out_shape=(
            jax.ShapeDtypeStruct((rows, hidden), BF16),
            jax.ShapeDtypeStruct((rows, hidden), BF16),
            jax.ShapeDtypeStruct((hidden, hidden), F32),
        ),
        in_specs=[
            vmem, vmem, vmem,
            pl.BlockSpec(memory_space=pl.ANY),
            pl.BlockSpec(memory_space=pltpu.SMEM),
        ],
        out_specs=(vmem, vmem, vmem),
        scratch_shapes=[
            pltpu.VMEM(tiles.shape[1:], BF16),
            pltpu.VMEM((domains, 2, half, hidden), BF16),
            pltpu.VMEM((domains, 2, hidden, half), BF16),
            pltpu.VMEM((layers, 2, hidden, half), BF16),
            pltpu.VMEM((layers, hidden, half), BF16),
            pltpu.VMEM((2, layers, hidden, half), BF16),
            pltpu.VMEM((2, half, hidden), F32),
            pltpu.VMEM((2, half, hidden), F32),
            pltpu.VMEM((rows, hidden), BF16),
            pltpu.VMEM((hidden, rows), BF16),
            pltpu.VMEM((levels + 1, quarter, hidden), F32),
            pltpu.VMEM((levels, quarter, hidden), F32),
            pltpu.VMEM((2, quarter, hidden), F32),
            pltpu.VMEM((2, half, hidden), BF16),
            dma,
            dma((domains,)), dma((domains,)),
            dma((2, layers)), dma((layers,)), dma((layers, 2)), dma((domains,)),
            dma((2,)), dma((2,)),
            dma((domains,)), dma((domains,)),
            dma((layers, 2)), dma((layers, 2)),
            dma((layers,)), dma((layers,)),
            dma((layers,)), dma((2, layers)),
            dma((levels,)), dma((levels,)),
            dma((2,)), dma((2,)),
        ],
        compiler_params=pltpu.CompilerParams(
            collective_id=0, has_side_effects=True, vmem_limit_bytes=40 * 1024 * 1024
        ),
        cost_estimate=pl.CostEstimate(
            flops=4 * sections * rows * rows * hidden,
            bytes_accessed=2 * sections * rows * rows,
            transcendentals=rows * hidden,
        ),
    )(features, weight, grad_out, tiles, tile_mask)


def solution(mesh):
    domains, replicas = mesh.shape["dom"], mesh.shape["rep"]
    paired = replicas == 2 and domains >= 8 and domains & (domains - 1) == 0
    placed = (P("dom", None), P(), P("dom", None), P("dom", "rep", None, None), P("dom", "rep"))
    return jax.shard_map(
        kernel_shards if paired else ring_shards,
        mesh=mesh,
        in_specs=placed,
        out_specs=(P("dom", None), P("dom", None), P()),
        check_vma=False,
    )
```

```python
import functools

import jax
import jax.numpy as jnp
from jax import lax
from jax.experimental import pallas as pl
from jax.experimental.pallas import tpu as pltpu
from jax.sharding import PartitionSpec as P

MESH = pl.DeviceIdType.MESH
F32 = jnp.float32
BF16 = jnp.bfloat16


def shifted_2(block, axis, distance):
    devices = range(lax.axis_size(axis))
    route = [((i - distance) % len(devices), i) for i in devices]
    return lax.ppermute(block, axis, route)


def tile_product(tile, weight_flag, operand, transposed):
    if transposed:
        contraction = (((0,), (0,)), ((), ()))
        out_rows = tile.shape[1]
    else:
        contraction = (((1,), (0,)), ((), ()))
        out_rows = tile.shape[0]

    def compute():
        return lax.dot_general(tile, operand, contraction, preferred_element_type=jnp.float32)

    def skipped():
        return jnp.zeros((out_rows, operand.shape[1]), jnp.float32)

    return lax.cond(weight_flag > 0, compute, skipped)


def ring_shards(features, weight, grad_out, tiles, tile_mask):
    domains = lax.axis_size("dom")
    replicas = lax.axis_size("rep")
    sections = domains // replicas
    replica = lax.axis_index("rep")
    bit_count = replicas.bit_length() - 1
    rows_here = features.shape[0]
    hidden = features.shape[1]
    projected = jnp.dot(features, weight, preferred_element_type=jnp.float32).astype(jnp.bfloat16)
    current = projected
    for level in range(bit_count):
        shifted = shifted_2(current, "dom", sections << level)
        current = jnp.where(replica >> level & 1 == 1, shifted, current)
    partial_value = jnp.zeros((rows_here, hidden), jnp.float32)
    for section in range(sections):
        if section > 0:
            current = shifted_2(current, "dom", 1)
        partial_value = partial_value + tile_product(
            tiles[0, section], tile_mask[0, section], current, False
        )
    total = lax.psum(partial_value, "rep")
    gate_value = jax.nn.sigmoid(total)
    activated = (total * gate_value).astype(jnp.bfloat16)
    score_grad = (
        grad_out.astype(jnp.float32) * gate_value * (1.0 + total * (1.0 - gate_value))
    ).astype(jnp.bfloat16)
    carried = tile_product(tiles[0, sections - 1], tile_mask[0, sections - 1], score_grad, True)
    for section in range(sections - 2, -1, -1):
        carried = shifted_2(carried, "dom", -1)
        carried = carried + tile_product(tiles[0, section], tile_mask[0, section], score_grad, True)
    for level in range(bit_count):
        shifted = shifted_2(carried, "dom", -(sections << level))
        carried = jnp.where(replica >> level & 1 == 1, shifted, carried)
    node_grad = lax.psum(carried, "rep").astype(jnp.bfloat16)
    feature_grad = lax.dot_general(
        node_grad, weight, (((1,), (1,)), ((), ())), preferred_element_type=jnp.float32
    ).astype(jnp.bfloat16)
    scaling = (rows_here * domains) ** (-0.5)
    weight_term = lax.dot_general(
        features, node_grad, (((0,), (0,)), ((), ())), preferred_element_type=jnp.float32
    )
    weight_grad = lax.psum(weight_term, "dom") * scaling
    return (activated, feature_grad, weight_grad)


def layer_kernel(
    domains, scaling,
    x_hbm, w_hbm, g_hbm, tiles_hbm, mask_ref,
    act_ref, fg_ref, wg_ref,
    w_ref, g_ref, tiles, xs, ps, from_b, from_a, from_z, part, part_in, ax, st, ws, w_in, w_full, fg_half,
    own_sem, tile_sem, x_recv, x_recv_p, x_send_z, x_send_a, x_send_b, x_send_p,
    part_send, part_recv,
    p_recv_p, p_send_p, b_send, b_recv, a_send, a_recv, z_send, z_recv,
    w_send, w_recv, last_send, last_recv,
):
    layers = domains // 4
    levels = 2 + layers.bit_length() - 1
    sections = domains // 2
    half = x_hbm.shape[0] // 2
    hidden = x_hbm.shape[1]
    d = lax.axis_index("dom")
    c = lax.axis_index("rep")
    other = 1 - c
    step_a, step_b = 1 + c, 2 - c
    z = d // 4
    a = (d // step_a) % 2
    b = (d // step_b) % 2

    def block_at(z_, b_, a_):
        return z_ * 4 + b_ * step_b + a_ * step_a

    dev_a, dev_b = block_at(z, b, 1 - a), block_at(z, 1 - b, a)
    far = []
    for level in range(1, layers.bit_length() - 1):
        dist = 1 << level
        far.append(block_at(z + dist * (1 - 2 * ((z // dist) % 2)), b, a))
    dev_z1 = block_at(z + (1 - 2 * (z % 2)), b, a)

    def copy_to(src, dst, send, recv, dom, rep):
        return pltpu.make_async_remote_copy(
            src_ref=src, dst_ref=dst, send_sem=send, recv_sem=recv,
            device_id=(dom, rep), device_id_type=MESH,
        )

    own_copies = [
        pltpu.make_async_copy(x_hbm.at[pl.ds(h * half, half)], xs.at[d, h], own_sem.at[h])
        for h in range(2)
    ]
    tile_copies = [
        pltpu.make_async_copy(w_hbm, w_ref, tile_sem.at[0]),
        pltpu.make_async_copy(g_hbm, g_ref, tile_sem.at[1]),
        pltpu.make_async_copy(tiles_hbm.at[0], tiles, tile_sem.at[2]),
    ]
    for copy in own_copies + tile_copies:
        copy.start()

    barrier = pltpu.get_barrier_semaphore()
    for dom, rep in [(dev_a, c), (dev_b, c), (d, other)] + [(f, c) for f in far]:
        pl.semaphore_signal(barrier, inc=1, device_id=(dom, rep), device_id_type=MESH)

    @pl.when(z > 0)
    def _():
        pl.semaphore_signal(barrier, inc=1, device_id=(d - 4, c), device_id_type=MESH)

    @pl.when(z < layers - 1)
    def _():
        pl.semaphore_signal(barrier, inc=1, device_id=(d + 4, c), device_id_type=MESH)

    ends = jnp.where(z > 0, 1, 0) + jnp.where(z < layers - 1, 1, 0)
    pl.semaphore_wait(barrier, 3 + len(far) + ends)

    def owner(j):
        return ((d - j + domains) % domains) // sections

    def x_copy_z(j, z_, up):
        return copy_to(xs.at[j, c], xs.at[j, c], x_send_z.at[up, z_], x_recv.at[j], d - 4 + 8 * up, c)

    def x_copy_a(j, z_):
        return copy_to(xs.at[j, c], xs.at[j, c], x_send_a.at[z_], x_recv.at[j], dev_a, c)

    def x_copy_b(j, z_, a_):
        return copy_to(xs.at[j, c], xs.at[j, c], x_send_b.at[z_, a_], x_recv.at[j], dev_b, c)

    def x_copy_p(j):
        return copy_to(xs.at[j, c], xs.at[j, c], x_send_p.at[j], x_recv_p.at[j], d, other)

    def x_arrive(j):
        copy_to(xs.at[j, c], xs.at[j, c], x_send_p.at[j], x_recv.at[j], d, other).wait_recv()

        @pl.when(owner(j) != c)
        def _():
            x_copy_p(j).start()

    for copy in own_copies:
        copy.wait()

    @pl.when(z > 0)
    def _():
        x_copy_z(d, z, 0).start()

    @pl.when(z < layers - 1)
    def _():
        x_copy_z(d, z, 1).start()

    x_copy_b(d, z, a).start()
    x_copy_a(d, z).start()

    def layer_of(n):
        return z + ((n + 1) // 2) * (2 * ((n + 1) % 2) - 1)

    def in_range(z_):
        return jnp.logical_and(z_ >= 0, z_ < layers)

    def from_layer(n):
        z_ = layer_of(n)

        @pl.when(in_range(z_))
        def _():
            j = block_at(z_, b, a)
            x_arrive(j)

            @pl.when(jnp.logical_and(z_ < z, z < layers - 1))
            def _():
                x_copy_z(j, z_, 1).start()

            @pl.when(jnp.logical_and(z_ > z, z > 0))
            def _():
                x_copy_z(j, z_, 0).start()

            x_copy_b(j, z_, a).start()
            x_copy_a(j, z_).start()

    def from_a_side(n):
        z_ = layer_of(n)

        @pl.when(in_range(z_))
        def _():
            j = block_at(z_, b, 1 - a)
            x_arrive(j)
            x_copy_b(j, z_, 1 - a).start()

    def from_b_side(n):
        z_ = layer_of(n)

        @pl.when(in_range(z_))
        def _():
            x_arrive(block_at(z_, 1 - b, a))
            x_arrive(block_at(z_, 1 - b, 1 - a))

    def flag(o):
        return jnp.where(mask_ref[0, o] > 0, 1.0, 0.0)

    def product(j):
        o = (d - j + domains) % domains - c * sections
        m = flag(o).astype(BF16)
        x_top, x_low = xs[j, 0] * m, xs[j, 1] * m
        for r in range(2):
            rows = pl.ds(r * half, half)
            part[r] += jnp.dot(
                tiles[o, rows, pl.ds(0, half)], x_top, preferred_element_type=F32
            ) + jnp.dot(tiles[o, rows, pl.ds(half, half)], x_low, preferred_element_type=F32)

    def products(n):
        z_ = layer_of(n)

        def one(q, carry):
            j = z_ * 4 + q

            @pl.when(owner(j) == c)
            def _():
                @pl.when(j != d)
                def _():
                    copy_to(
                        xs.at[j, other], xs.at[j, other], x_send_p.at[j], x_recv_p.at[j], d, other
                    ).wait_recv()

                product(j)

            return carry

        @pl.when(in_range(z_))
        def _():
            lax.fori_loop(0, 4, one, 0)

    visits = 2 * layers - 1
    for copy in tile_copies:
        copy.wait()
    for r in range(2):
        part[r] = jnp.zeros((half, hidden), F32)

    def gather_step(n, carry):
        for lag, step in enumerate((from_layer, from_a_side, from_b_side)):
            at = n - 2 * lag

            @pl.when(jnp.logical_and(at >= (1 if lag == 0 else 0), at < visits))
            def _():
                step(at)

        @pl.when(n >= 5)
        def _():
            products(n - 5)

        return carry

    lax.fori_loop(1, visits + 5, gather_step, 0)

    def part_copy(r):
        return copy_to(part.at[r], part_in.at[r], part_send.at[r], part_recv.at[r], d, other)

    for r in range(2):
        part_copy(r).start()

    for r in range(2):
        part_copy(r).wait_recv()
        rows = pl.ds(r * half, half)
        ax_here = (part[r] + part_in[r]).astype(BF16)
        ax[rows, :] = ax_here
        total = jnp.dot(ax_here, w_ref[...], preferred_element_type=F32)
        gate = jax.nn.sigmoid(total)
        act_ref[rows, :] = (total * gate).astype(BF16)
        score = g_ref[rows, :].astype(F32) * gate * (1.0 + total * (1.0 - gate))
        st[:, rows] = jnp.transpose(score).astype(BF16)

    quarter = hidden // 2
    w_peers = [dev_a, dev_b, dev_z1] + far
    w_peers = w_peers[:levels]

    def w_copy(level):
        return copy_to(
            ws.at[level], w_in.at[level], w_send.at[level], w_recv.at[level], w_peers[level], c
        )

    ws[0] = jnp.dot(
        st[pl.ds(pl.multiple_of(c * quarter, quarter), quarter), :], ax[...],
        preferred_element_type=F32,
    )

    def target_layer(t):
        return jnp.where(t % 2 == 0, layers - 1 - t // 2, t // 2)

    def piece(k):
        z_ = target_layer(k // 4)
        q = k % 4
        b_ = jnp.where(q < 2, 1 - b, b)
        a_ = jnp.where(q % 2 == 0, 1 - a, a)
        return z_, b_, a_, block_at(z_, b_, a_)

    def p_copy(j):
        return copy_to(ps.at[j, other], ps.at[j, other], p_send_p.at[j], p_recv_p.at[j], d, other)

    def b_copy(z_, a_):
        return copy_to(
            ps.at[block_at(z_, 1 - b, a_), c], from_b.at[z_, a_], b_send.at[z_, a_], b_recv.at[z_, a_],
            dev_b, c,
        )

    def a_copy(z_):
        return copy_to(
            ps.at[block_at(z_, b, 1 - a), c], from_a.at[z_], a_send.at[z_], a_recv.at[z_], dev_a, c
        )

    def z_copy(z_, up):
        return copy_to(
            ps.at[block_at(z_, b, a), c], from_z.at[up, z_], z_send.at[z_], z_recv.at[up, z_],
            d - 4 + 8 * up, c,
        )

    def backward(k, carry):
        z_, b_, a_, j = piece(k)

        @pl.when(owner(j) == c)
        def _():
            o = (d - j + domains) % domains - c * sections
            m = flag(o)
            for h in range(2):
                ps[j, h] = (
                    jnp.dot(st[...], tiles[o, :, pl.ds(h * half, half)], preferred_element_type=F32) * m
                ).astype(BF16)
            p_copy(j).start()

            @pl.when(b_ != b)
            def _():
                b_copy(z_, a_).start()

        return carry

    lax.fori_loop(0, domains, backward, 0)

    def relay_partner(k, carry):
        z_, b_, a_, j = piece(k)

        @pl.when(owner(j) != c)
        def _():
            copy_to(ps.at[j, c], ps.at[j, c], p_send_p.at[j], p_recv_p.at[j], d, other).wait_recv()

            @pl.when(b_ != b)
            def _():
                b_copy(z_, a_).start()

        return carry

    lax.fori_loop(0, domains, relay_partner, 0)
    w_copy(0).start()

    def stage_a(t):
        z_ = target_layer(t)
        b_copy(z_, 1 - a).wait_recv()
        j = block_at(z_, b, 1 - a)
        ps[j, c] = (ps[j, c].astype(F32) + from_b[z_, 1 - a].astype(F32)).astype(BF16)
        a_copy(z_).start()

    def stage_z(t):
        z_ = target_layer(t)
        b_copy(z_, a).wait_recv()
        a_copy(z_).wait_recv()
        j = block_at(z_, b, a)

        def mine():
            return ps[j, c].astype(F32) + from_b[z_, a].astype(F32) + from_a[z_].astype(F32)

        @pl.when(z_ == z)
        def _():
            part[0] = mine()

        @pl.when(jnp.logical_and(z_ > z, z == 0))
        def _():
            ps[j, c] = mine().astype(BF16)
            z_copy(z_, 1).start()

        @pl.when(jnp.logical_and(z_ < z, z == layers - 1))
        def _():
            ps[j, c] = mine().astype(BF16)
            z_copy(z_, 0).start()

    def stage_relay(t):
        z_ = target_layer(t)
        j = block_at(z_, b, a)

        def pass_on(up):
            z_copy(z_, up).wait_recv()
            ps[j, c] = (
                ps[j, c].astype(F32) + from_b[z_, a].astype(F32) + from_a[z_].astype(F32)
                + from_z[up, z_].astype(F32)
            ).astype(BF16)
            z_copy(z_, up).start()

        @pl.when(jnp.logical_and(z_ > z, z > 0))
        def _():
            pass_on(1)

        @pl.when(jnp.logical_and(z_ < z, z < layers - 1))
        def _():
            pass_on(0)

    for r in range(2):
        part_copy(r).wait_send()

    stages = max(layers + 2, levels)
    for t in range(stages):
        if t < layers:
            stage_a(t)
        if 1 <= t <= layers:
            stage_z(t - 1)
        if 2 <= t <= layers + 1:
            stage_relay(t - 2)
        if t < levels:
            w_copy(t).wait_recv()
            ws[t + 1] = ws[t] + w_in[t]
            if t + 1 < levels:
                w_copy(t + 1).start()

    w_full[c] = ws[levels]
    w_last = copy_to(w_full.at[c], w_full.at[c], last_send.at[0], last_recv.at[0], d, other)
    w_last.start()

    @pl.when(z > 0)
    def _():
        z_copy(z, 1).wait_recv()
        part[0] += from_z[1, z].astype(F32)

    @pl.when(z < layers - 1)
    def _():
        z_copy(z, 0).wait_recv()
        part[0] += from_z[0, z].astype(F32)

    node = jnp.transpose(part[0]).astype(BF16)
    fg_half[c] = lax.dot_general(
        node, w_ref[...], (((1,), (1,)), ((), ())), preferred_element_type=F32
    ).astype(BF16)
    f_last = copy_to(fg_half.at[c], fg_half.at[c], last_send.at[1], last_recv.at[1], d, other)
    f_last.start()

    copy_to(w_full.at[other], w_full.at[other], last_send.at[0], last_recv.at[0], d, other).wait_recv()
    for h in range(2):
        wg_ref[:, pl.ds(h * quarter, quarter)] = jnp.transpose(w_full[h]) * scaling

    def drain_p(j, carry):
        @pl.when(jnp.logical_and(owner(j) != c, j != d))
        def _():
            x_copy_p(j).wait_send()

        @pl.when(owner(j) == c)
        def _():
            p_copy(j).wait_send()

        return carry

    lax.fori_loop(0, domains, drain_p, 0)

    def drain(z_, carry):
        @pl.when(jnp.logical_and(z_ <= z, z < layers - 1))
        def _():
            x_copy_z(block_at(z_, b, a), z_, 1).wait_send()

        @pl.when(jnp.logical_and(z_ >= z, z > 0))
        def _():
            x_copy_z(block_at(z_, b, a), z_, 0).wait_send()

        x_copy_a(block_at(z_, b, a), z_).wait_send()
        a_copy(z_).wait_send()
        for a_ in range(2):
            x_copy_b(block_at(z_, b, a_), z_, a_).wait_send()
            b_copy(z_, a_).wait_send()

        @pl.when(z_ > z)
        def _():
            z_copy(z_, 1).wait_send()

        @pl.when(z_ < z)
        def _():
            z_copy(z_, 0).wait_send()

        return carry

    lax.fori_loop(0, layers, drain, 0)
    for level in range(levels):
        w_copy(level).wait_send()
    copy_to(fg_half.at[other], fg_half.at[other], last_send.at[1], last_recv.at[1], d, other).wait_recv()
    for h in range(2):
        fg_ref[pl.ds(h * half, half), :] = fg_half[h]
    w_last.wait_send()
    f_last.wait_send()


def kernel_shards(features, weight, grad_out, tiles, tile_mask):
    domains = lax.axis_size("dom")
    layers = domains // 4
    levels = 2 + layers.bit_length() - 1
    sections = tiles.shape[1]
    rows, hidden = features.shape
    half, quarter = rows // 2, hidden // 2
    dma = pltpu.SemaphoreType.DMA
    vmem = pl.BlockSpec(memory_space=pltpu.VMEM)
    return pl.pallas_call(
        functools.partial(layer_kernel, domains, float((rows * domains) ** (-0.5))),
        out_shape=(
            jax.ShapeDtypeStruct((rows, hidden), BF16),
            jax.ShapeDtypeStruct((rows, hidden), BF16),
            jax.ShapeDtypeStruct((hidden, hidden), F32),
        ),
        in_specs=[pl.BlockSpec(memory_space=pl.ANY)] * 4 + [pl.BlockSpec(memory_space=pltpu.SMEM)],
        out_specs=(vmem, vmem, vmem),
        scratch_shapes=[
            pltpu.VMEM(weight.shape, BF16),
            pltpu.VMEM((rows, hidden), BF16),
            pltpu.VMEM(tiles.shape[1:], BF16),
            pltpu.VMEM((domains, 2, half, hidden), BF16),
            pltpu.VMEM((domains, 2, hidden, half), BF16),
            pltpu.VMEM((layers, 2, hidden, half), BF16),
            pltpu.VMEM((layers, hidden, half), BF16),
            pltpu.VMEM((2, layers, hidden, half), BF16),
            pltpu.VMEM((2, half, hidden), F32),
            pltpu.VMEM((2, half, hidden), F32),
            pltpu.VMEM((rows, hidden), BF16),
            pltpu.VMEM((hidden, rows), BF16),
            pltpu.VMEM((levels + 1, quarter, hidden), F32),
            pltpu.VMEM((levels, quarter, hidden), F32),
            pltpu.VMEM((2, quarter, hidden), F32),
            pltpu.VMEM((2, half, hidden), BF16),
            dma((2,)), dma((3,)),
            dma((domains,)), dma((domains,)),
            dma((2, layers)), dma((layers,)), dma((layers, 2)), dma((domains,)),
            dma((2,)), dma((2,)),
            dma((domains,)), dma((domains,)),
            dma((layers, 2)), dma((layers, 2)),
            dma((layers,)), dma((layers,)),
            dma((layers,)), dma((2, layers)),
            dma((levels,)), dma((levels,)),
            dma((2,)), dma((2,)),
        ],
        compiler_params=pltpu.CompilerParams(
            collective_id=0, has_side_effects=True, vmem_limit_bytes=63 * 1024 * 1024
        ),
        cost_estimate=pl.CostEstimate(
            flops=4 * sections * rows * rows * hidden,
            bytes_accessed=2 * sections * rows * rows,
            transcendentals=rows * hidden,
        ),
    )(features, weight, grad_out, tiles, tile_mask)


def solution(mesh):
    domains, replicas = mesh.shape["dom"], mesh.shape["rep"]
    paired = replicas == 2 and domains >= 8 and domains & (domains - 1) == 0
    placed = (P("dom", None), P(), P("dom", None), P("dom", "rep", None, None), P("dom", "rep"))
    return jax.shard_map(
        kernel_shards if paired else ring_shards,
        mesh=mesh,
        in_specs=placed,
        out_specs=(P("dom", None), P("dom", None), P()),
        check_vma=False,
    )
```

```python
import functools

import jax
import jax.numpy as jnp
from jax import lax
from jax.experimental import pallas as pl
from jax.experimental.pallas import tpu as pltpu
from jax.sharding import PartitionSpec as P

MESH = pl.DeviceIdType.MESH
F32 = jnp.float32
BF16 = jnp.bfloat16


def shifted_2(block, axis, distance):
    devices = range(lax.axis_size(axis))
    route = [((i - distance) % len(devices), i) for i in devices]
    return lax.ppermute(block, axis, route)


def tile_product(tile, weight_flag, operand, transposed):
    if transposed:
        contraction = (((0,), (0,)), ((), ()))
        out_rows = tile.shape[1]
    else:
        contraction = (((1,), (0,)), ((), ()))
        out_rows = tile.shape[0]

    def compute():
        return lax.dot_general(tile, operand, contraction, preferred_element_type=jnp.float32)

    def skipped():
        return jnp.zeros((out_rows, operand.shape[1]), jnp.float32)

    return lax.cond(weight_flag > 0, compute, skipped)


def ring_shards(features, weight, grad_out, tiles, tile_mask):
    domains = lax.axis_size("dom")
    replicas = lax.axis_size("rep")
    sections = domains // replicas
    replica = lax.axis_index("rep")
    bit_count = replicas.bit_length() - 1
    rows_here = features.shape[0]
    hidden = features.shape[1]
    projected = jnp.dot(features, weight, preferred_element_type=jnp.float32).astype(jnp.bfloat16)
    current = projected
    for level in range(bit_count):
        shifted = shifted_2(current, "dom", sections << level)
        current = jnp.where(replica >> level & 1 == 1, shifted, current)
    partial_value = jnp.zeros((rows_here, hidden), jnp.float32)
    for section in range(sections):
        if section > 0:
            current = shifted_2(current, "dom", 1)
        partial_value = partial_value + tile_product(
            tiles[0, section], tile_mask[0, section], current, False
        )
    total = lax.psum(partial_value, "rep")
    gate_value = jax.nn.sigmoid(total)
    activated = (total * gate_value).astype(jnp.bfloat16)
    score_grad = (
        grad_out.astype(jnp.float32) * gate_value * (1.0 + total * (1.0 - gate_value))
    ).astype(jnp.bfloat16)
    carried = tile_product(tiles[0, sections - 1], tile_mask[0, sections - 1], score_grad, True)
    for section in range(sections - 2, -1, -1):
        carried = shifted_2(carried, "dom", -1)
        carried = carried + tile_product(tiles[0, section], tile_mask[0, section], score_grad, True)
    for level in range(bit_count):
        shifted = shifted_2(carried, "dom", -(sections << level))
        carried = jnp.where(replica >> level & 1 == 1, shifted, carried)
    node_grad = lax.psum(carried, "rep").astype(jnp.bfloat16)
    feature_grad = lax.dot_general(
        node_grad, weight, (((1,), (1,)), ((), ())), preferred_element_type=jnp.float32
    ).astype(jnp.bfloat16)
    scaling = (rows_here * domains) ** (-0.5)
    weight_term = lax.dot_general(
        features, node_grad, (((0,), (0,)), ((), ())), preferred_element_type=jnp.float32
    )
    weight_grad = lax.psum(weight_term, "dom") * scaling
    return (activated, feature_grad, weight_grad)


def layer_kernel(
    domains, scaling,
    x_hbm, w_hbm, g_hbm, tiles_hbm, mask_ref,
    act_ref, fg_ref, wg_ref,
    w_ref, g_ref, tiles, xs, ps, from_b, from_a, from_z, part, part_in, ax, st, ws, w_in, w_cross, w_cross_in, w_full, fg_half,
    own_sem, tile_sem, x_recv, x_recv_p, x_send_z, x_send_a, x_send_b, x_send_p,
    part_send, part_recv,
    p_recv_p, p_send_p, b_send, b_recv, a_send, a_recv, z_send, z_recv,
    w_send, w_recv, last_send, last_recv,
):
    layers = domains // 4
    folds = layers.bit_length() - 1
    sections = domains // 2
    half = x_hbm.shape[0] // 2
    hidden = x_hbm.shape[1]
    d = lax.axis_index("dom")
    c = lax.axis_index("rep")
    other = 1 - c
    step_a, step_b = 1 + c, 2 - c
    z = d // 4
    a = (d // step_a) % 2
    b = (d // step_b) % 2

    def block_at(z_, b_, a_):
        return z_ * 4 + b_ * step_b + a_ * step_a

    dev_a, dev_b = block_at(z, b, 1 - a), block_at(z, 1 - b, a)
    dev_fold = [block_at(z + (1 << f) * (1 - 2 * ((z // (1 << f)) % 2)), b, a) for f in range(folds)]
    far = dev_fold[1:]

    def copy_to(src, dst, send, recv, dom, rep):
        return pltpu.make_async_remote_copy(
            src_ref=src, dst_ref=dst, send_sem=send, recv_sem=recv,
            device_id=(dom, rep), device_id_type=MESH,
        )

    own_copies = [
        pltpu.make_async_copy(x_hbm.at[pl.ds(h * half, half)], xs.at[d, h], own_sem.at[h])
        for h in range(2)
    ]
    tile_copies = [
        pltpu.make_async_copy(w_hbm, w_ref, tile_sem.at[0]),
        pltpu.make_async_copy(g_hbm, g_ref, tile_sem.at[1]),
        pltpu.make_async_copy(tiles_hbm.at[0], tiles, tile_sem.at[2]),
    ]
    for copy in own_copies + tile_copies:
        copy.start()

    barrier = pltpu.get_barrier_semaphore()
    for dom, rep in [(dev_a, c), (dev_b, c), (d, other)] + [(f, c) for f in far]:
        pl.semaphore_signal(barrier, inc=1, device_id=(dom, rep), device_id_type=MESH)

    @pl.when(z > 0)
    def _():
        pl.semaphore_signal(barrier, inc=1, device_id=(d - 4, c), device_id_type=MESH)

    @pl.when(z < layers - 1)
    def _():
        pl.semaphore_signal(barrier, inc=1, device_id=(d + 4, c), device_id_type=MESH)

    ends = jnp.where(z > 0, 1, 0) + jnp.where(z < layers - 1, 1, 0)
    pl.semaphore_wait(barrier, 3 + len(far) + ends)

    def owner(j):
        return ((d - j + domains) % domains) // sections

    def x_copy_z(j, z_, up):
        return copy_to(xs.at[j, c], xs.at[j, c], x_send_z.at[up, z_], x_recv.at[j], d - 4 + 8 * up, c)

    def x_copy_a(j, z_):
        return copy_to(xs.at[j, c], xs.at[j, c], x_send_a.at[z_], x_recv.at[j], dev_a, c)

    def x_copy_b(j, z_, a_):
        return copy_to(xs.at[j, c], xs.at[j, c], x_send_b.at[z_, a_], x_recv.at[j], dev_b, c)

    def x_copy_p(j):
        return copy_to(xs.at[j, c], xs.at[j, c], x_send_p.at[j], x_recv_p.at[j], d, other)

    def x_arrive(j):
        copy_to(xs.at[j, c], xs.at[j, c], x_send_p.at[j], x_recv.at[j], d, other).wait_recv()

        @pl.when(owner(j) != c)
        def _():
            x_copy_p(j).start()

    for copy in own_copies:
        copy.wait()

    @pl.when(z > 0)
    def _():
        x_copy_z(d, z, 0).start()

    @pl.when(z < layers - 1)
    def _():
        x_copy_z(d, z, 1).start()

    x_copy_b(d, z, a).start()
    x_copy_a(d, z).start()

    def layer_of(n):
        return z + ((n + 1) // 2) * (2 * ((n + 1) % 2) - 1)

    def in_range(z_):
        return jnp.logical_and(z_ >= 0, z_ < layers)

    def from_layer(n):
        z_ = layer_of(n)

        @pl.when(in_range(z_))
        def _():
            j = block_at(z_, b, a)
            x_arrive(j)

            @pl.when(jnp.logical_and(z_ < z, z < layers - 1))
            def _():
                x_copy_z(j, z_, 1).start()

            @pl.when(jnp.logical_and(z_ > z, z > 0))
            def _():
                x_copy_z(j, z_, 0).start()

            x_copy_b(j, z_, a).start()
            x_copy_a(j, z_).start()

    def from_a_side(n):
        z_ = layer_of(n)

        @pl.when(in_range(z_))
        def _():
            j = block_at(z_, b, 1 - a)
            x_arrive(j)
            x_copy_b(j, z_, 1 - a).start()

    def from_b_side(n):
        z_ = layer_of(n)

        @pl.when(in_range(z_))
        def _():
            x_arrive(block_at(z_, 1 - b, a))
            x_arrive(block_at(z_, 1 - b, 1 - a))

    def flag(o):
        return jnp.where(mask_ref[0, o] > 0, 1.0, 0.0)

    def product(j):
        o = (d - j + domains) % domains - c * sections
        m = flag(o).astype(BF16)
        x_top, x_low = xs[j, 0] * m, xs[j, 1] * m
        for r in range(2):
            rows = pl.ds(r * half, half)
            part[r] += jnp.dot(
                tiles[o, rows, pl.ds(0, half)], x_top, preferred_element_type=F32
            ) + jnp.dot(tiles[o, rows, pl.ds(half, half)], x_low, preferred_element_type=F32)

    def products(n):
        z_ = layer_of(n)

        def one(q, carry):
            j = z_ * 4 + q

            @pl.when(owner(j) == c)
            def _():
                @pl.when(j != d)
                def _():
                    copy_to(
                        xs.at[j, other], xs.at[j, other], x_send_p.at[j], x_recv_p.at[j], d, other
                    ).wait_recv()

                product(j)

            return carry

        @pl.when(in_range(z_))
        def _():
            lax.fori_loop(0, 4, one, 0)

    visits = 2 * layers - 1
    for copy in tile_copies:
        copy.wait()
    for r in range(2):
        part[r] = jnp.zeros((half, hidden), F32)

    def gather_step(n, carry):
        for lag, step in enumerate((from_layer, from_a_side, from_b_side)):
            at = n - 2 * lag

            @pl.when(jnp.logical_and(at >= (1 if lag == 0 else 0), at < visits))
            def _():
                step(at)

        @pl.when(n >= 5)
        def _():
            products(n - 5)

        return carry

    lax.fori_loop(1, visits + 5, gather_step, 0)

    def part_copy(r):
        return copy_to(part.at[r], part_in.at[r], part_send.at[r], part_recv.at[r], d, other)

    for r in range(2):
        part_copy(r).start()

    for r in range(2):
        part_copy(r).wait_recv()
        rows = pl.ds(r * half, half)
        ax_here = (part[r] + part_in[r]).astype(BF16)
        ax[rows, :] = ax_here
        total = jnp.dot(ax_here, w_ref[...], preferred_element_type=F32)
        gate = jax.nn.sigmoid(total)
        act_ref[rows, :] = (total * gate).astype(BF16)
        score = g_ref[rows, :].astype(F32) * gate * (1.0 + total * (1.0 - gate))
        st[:, rows] = jnp.transpose(score).astype(BF16)

    quarter = hidden // 2
    sizes, bases = [quarter], [0]
    for f in range(folds):
        sizes.append(sizes[-1] // 2)
        bases.append(bases[-1] + ((z // (1 << f)) % 2) * sizes[-1])

    def fold_copy(f):
        there = bases[f] + (1 - (z // (1 << f)) % 2) * sizes[f + 1]
        rows = pl.ds(pl.multiple_of(there, sizes[f + 1]), sizes[f + 1])
        return copy_to(
            ws.at[rows], w_in.at[f, pl.ds(0, sizes[f + 1])], w_send.at[f], w_recv.at[f], dev_fold[f], c
        )

    def cross_copy(i):
        return copy_to(
            w_cross.at[i], w_cross_in.at[i], w_send.at[folds + i], w_recv.at[folds + i],
            (dev_a, dev_b)[i], c,
        )

    def unfold_copy(f):
        rows = pl.ds(pl.multiple_of(bases[f + 1], sizes[f + 1]), sizes[f + 1])
        return copy_to(
            w_full.at[c, rows], w_full.at[c, rows], w_send.at[folds + 2 + f], w_recv.at[folds + 2 + f],
            dev_fold[f], c,
        )

    def weight_step(s):
        if s < folds:
            fold_copy(s).wait_recv()
            rows = pl.ds(pl.multiple_of(bases[s + 1], sizes[s + 1]), sizes[s + 1])
            ws[rows, :] += w_in[s, pl.ds(0, sizes[s + 1])]
            if s + 1 < folds:
                fold_copy(s + 1).start()
            else:
                w_cross[0] = ws[rows, :]
                cross_copy(0).start()
        elif s < folds + 2:
            i = s - folds
            cross_copy(i).wait_recv()
            if i == 0:
                w_cross[1] = w_cross[0] + w_cross_in[0]
                cross_copy(1).start()
            else:
                rows = pl.ds(pl.multiple_of(bases[folds], sizes[folds]), sizes[folds])
                w_full[c, rows] = w_cross[1] + w_cross_in[1]
                unfold_copy(folds - 1).start()
        else:
            f = 2 * folds + 1 - s
            unfold_copy(f).wait_recv()
            if f > 0:
                unfold_copy(f - 1).start()

    weight_steps = 2 * folds + 2

    ws[...] = jnp.dot(
        st[pl.ds(pl.multiple_of(c * quarter, quarter), quarter), :], ax[...],
        preferred_element_type=F32,
    )

    def target_layer(t):
        return jnp.where(t % 2 == 0, layers - 1 - t // 2, t // 2)

    def piece(k):
        z_ = target_layer(k // 4)
        q = k % 4
        b_ = jnp.where(q < 2, 1 - b, b)
        a_ = jnp.where(q % 2 == 0, 1 - a, a)
        return z_, b_, a_, block_at(z_, b_, a_)

    def p_copy(j):
        return copy_to(ps.at[j, other], ps.at[j, other], p_send_p.at[j], p_recv_p.at[j], d, other)

    def b_copy(z_, a_):
        return copy_to(
            ps.at[block_at(z_, 1 - b, a_), c], from_b.at[z_, a_], b_send.at[z_, a_], b_recv.at[z_, a_],
            dev_b, c,
        )

    def a_copy(z_):
        return copy_to(
            ps.at[block_at(z_, b, 1 - a), c], from_a.at[z_], a_send.at[z_], a_recv.at[z_], dev_a, c
        )

    def z_copy(z_, up):
        return copy_to(
            ps.at[block_at(z_, b, a), c], from_z.at[up, z_], z_send.at[z_], z_recv.at[up, z_],
            d - 4 + 8 * up, c,
        )

    def backward(k, carry):
        z_, b_, a_, j = piece(k)

        @pl.when(owner(j) == c)
        def _():
            o = (d - j + domains) % domains - c * sections
            m = flag(o)
            for h in range(2):
                ps[j, h] = (
                    jnp.dot(st[...], tiles[o, :, pl.ds(h * half, half)], preferred_element_type=F32) * m
                ).astype(BF16)
            p_copy(j).start()

            @pl.when(jnp.logical_and(b_ != b, k < 8))
            def _():
                b_copy(z_, a_).start()

        return carry

    lax.fori_loop(0, domains, backward, 0)

    def relay_partner(k, carry):
        z_, b_, a_, j = piece(k)

        @pl.when(owner(j) != c)
        def _():
            copy_to(ps.at[j, c], ps.at[j, c], p_send_p.at[j], p_recv_p.at[j], d, other).wait_recv()

            @pl.when(jnp.logical_and(b_ != b, k < 8))
            def _():
                b_copy(z_, a_).start()

        return carry

    lax.fori_loop(0, domains, relay_partner, 0)
    fold_copy(0).start()

    def stage_a(t):
        z_ = target_layer(t)
        b_copy(z_, 1 - a).wait_recv()
        j = block_at(z_, b, 1 - a)
        ps[j, c] = (ps[j, c].astype(F32) + from_b[z_, 1 - a].astype(F32)).astype(BF16)
        a_copy(z_).start()

    def stage_z(t):
        z_ = target_layer(t)
        b_copy(z_, a).wait_recv()
        a_copy(z_).wait_recv()
        j = block_at(z_, b, a)

        def mine():
            return ps[j, c].astype(F32) + from_b[z_, a].astype(F32) + from_a[z_].astype(F32)

        @pl.when(z_ == z)
        def _():
            part[0] = mine()

        @pl.when(jnp.logical_and(z_ > z, z == 0))
        def _():
            ps[j, c] = mine().astype(BF16)
            z_copy(z_, 1).start()

        @pl.when(jnp.logical_and(z_ < z, z == layers - 1))
        def _():
            ps[j, c] = mine().astype(BF16)
            z_copy(z_, 0).start()

    def stage_relay(t):
        z_ = target_layer(t)
        j = block_at(z_, b, a)

        def pass_on(up):
            z_copy(z_, up).wait_recv()
            ps[j, c] = (
                ps[j, c].astype(F32) + from_b[z_, a].astype(F32) + from_a[z_].astype(F32)
                + from_z[up, z_].astype(F32)
            ).astype(BF16)
            z_copy(z_, up).start()

        @pl.when(jnp.logical_and(z_ > z, z > 0))
        def _():
            pass_on(1)

        @pl.when(jnp.logical_and(z_ < z, z < layers - 1))
        def _():
            pass_on(0)

    for r in range(2):
        part_copy(r).wait_send()

    stages = max(layers + 2, weight_steps)
    for t in range(stages):
        if t < layers:
            stage_a(t)
        if t + 2 < layers:
            b_copy(target_layer(t + 2), 1 - a).start()
            b_copy(target_layer(t + 2), a).start()
        if 1 <= t <= layers:
            stage_z(t - 1)
        if 2 <= t <= layers + 1:
            stage_relay(t - 2)
        if t < weight_steps:
            weight_step(t)

    w_last = copy_to(w_full.at[c], w_full.at[c], last_send.at[0], last_recv.at[0], d, other)
    w_last.start()

    @pl.when(z > 0)
    def _():
        z_copy(z, 1).wait_recv()
        part[0] += from_z[1, z].astype(F32)

    @pl.when(z < layers - 1)
    def _():
        z_copy(z, 0).wait_recv()
        part[0] += from_z[0, z].astype(F32)

    node = jnp.transpose(part[0]).astype(BF16)
    fg_half[c] = lax.dot_general(
        node, w_ref[...], (((1,), (1,)), ((), ())), preferred_element_type=F32
    ).astype(BF16)
    f_last = copy_to(fg_half.at[c], fg_half.at[c], last_send.at[1], last_recv.at[1], d, other)
    f_last.start()

    copy_to(w_full.at[other], w_full.at[other], last_send.at[0], last_recv.at[0], d, other).wait_recv()
    for h in range(2):
        wg_ref[:, pl.ds(h * quarter, quarter)] = jnp.transpose(w_full[h]) * scaling

    def drain_p(j, carry):
        @pl.when(jnp.logical_and(owner(j) != c, j != d))
        def _():
            x_copy_p(j).wait_send()

        @pl.when(owner(j) == c)
        def _():
            p_copy(j).wait_send()

        return carry

    lax.fori_loop(0, domains, drain_p, 0)

    def drain(z_, carry):
        @pl.when(jnp.logical_and(z_ <= z, z < layers - 1))
        def _():
            x_copy_z(block_at(z_, b, a), z_, 1).wait_send()

        @pl.when(jnp.logical_and(z_ >= z, z > 0))
        def _():
            x_copy_z(block_at(z_, b, a), z_, 0).wait_send()

        x_copy_a(block_at(z_, b, a), z_).wait_send()
        a_copy(z_).wait_send()
        for a_ in range(2):
            x_copy_b(block_at(z_, b, a_), z_, a_).wait_send()
            b_copy(z_, a_).wait_send()

        @pl.when(z_ > z)
        def _():
            z_copy(z_, 1).wait_send()

        @pl.when(z_ < z)
        def _():
            z_copy(z_, 0).wait_send()

        return carry

    lax.fori_loop(0, layers, drain, 0)
    for f in range(folds):
        fold_copy(f).wait_send()
        unfold_copy(f).wait_send()
    for i in range(2):
        cross_copy(i).wait_send()
    copy_to(fg_half.at[other], fg_half.at[other], last_send.at[1], last_recv.at[1], d, other).wait_recv()
    for h in range(2):
        fg_ref[pl.ds(h * half, half), :] = fg_half[h]
    w_last.wait_send()
    f_last.wait_send()


def kernel_shards(features, weight, grad_out, tiles, tile_mask):
    domains = lax.axis_size("dom")
    layers = domains // 4
    folds = layers.bit_length() - 1
    sections = tiles.shape[1]
    rows, hidden = features.shape
    half, quarter = rows // 2, hidden // 2
    dma = pltpu.SemaphoreType.DMA
    vmem = pl.BlockSpec(memory_space=pltpu.VMEM)
    return pl.pallas_call(
        functools.partial(layer_kernel, domains, float((rows * domains) ** (-0.5))),
        out_shape=(
            jax.ShapeDtypeStruct((rows, hidden), BF16),
            jax.ShapeDtypeStruct((rows, hidden), BF16),
            jax.ShapeDtypeStruct((hidden, hidden), F32),
        ),
        in_specs=[pl.BlockSpec(memory_space=pltpu.HBM)] * 4 + [pl.BlockSpec(memory_space=pltpu.SMEM)],
        out_specs=(vmem, vmem, vmem),
        scratch_shapes=[
            pltpu.VMEM(weight.shape, BF16),
            pltpu.VMEM((rows, hidden), BF16),
            pltpu.VMEM(tiles.shape[1:], BF16),
            pltpu.VMEM((domains, 2, half, hidden), BF16),
            pltpu.VMEM((domains, 2, hidden, half), BF16),
            pltpu.VMEM((layers, 2, hidden, half), BF16),
            pltpu.VMEM((layers, hidden, half), BF16),
            pltpu.VMEM((2, layers, hidden, half), BF16),
            pltpu.VMEM((2, half, hidden), F32),
            pltpu.VMEM((2, half, hidden), F32),
            pltpu.VMEM((rows, hidden), BF16),
            pltpu.VMEM((hidden, rows), BF16),
            pltpu.VMEM((quarter, hidden), F32),
            pltpu.VMEM((folds, quarter // 2, hidden), F32),
            pltpu.VMEM((2, quarter // layers, hidden), F32),
            pltpu.VMEM((2, quarter // layers, hidden), F32),
            pltpu.VMEM((2, quarter, hidden), F32),
            pltpu.VMEM((2, half, hidden), BF16),
            dma((2,)), dma((3,)),
            dma((domains,)), dma((domains,)),
            dma((2, layers)), dma((layers,)), dma((layers, 2)), dma((domains,)),
            dma((2,)), dma((2,)),
            dma((domains,)), dma((domains,)),
            dma((layers, 2)), dma((layers, 2)),
            dma((layers,)), dma((layers,)),
            dma((layers,)), dma((2, layers)),
            dma((2 * folds + 2,)), dma((2 * folds + 2,)),
            dma((2,)), dma((2,)),
        ],
        compiler_params=pltpu.CompilerParams(
            collective_id=0, has_side_effects=True, vmem_limit_bytes=48 * 1024 * 1024
        ),
        cost_estimate=pl.CostEstimate(
            flops=4 * sections * rows * rows * hidden,
            bytes_accessed=2 * sections * rows * rows,
            transcendentals=rows * hidden,
        ),
    )(features, weight, grad_out, tiles, tile_mask)


def solution(mesh):
    domains, replicas = mesh.shape["dom"], mesh.shape["rep"]
    paired = replicas == 2 and domains >= 8 and domains & (domains - 1) == 0
    placed = (P("dom", None), P(), P("dom", None), P("dom", "rep", None, None), P("dom", "rep"))
    return jax.shard_map(
        kernel_shards if paired else ring_shards,
        mesh=mesh,
        in_specs=placed,
        out_specs=(P("dom", None), P("dom", None), P()),
        check_vma=False,
    )
```

```python
import functools

import jax
import jax.numpy as jnp
from jax import lax
from jax.experimental import pallas as pl
from jax.experimental.pallas import tpu as pltpu
from jax.sharding import PartitionSpec as P

MESH = pl.DeviceIdType.MESH
F32 = jnp.float32
BF16 = jnp.bfloat16


def shifted_2(block, axis, distance):
    devices = range(lax.axis_size(axis))
    route = [((i - distance) % len(devices), i) for i in devices]
    return lax.ppermute(block, axis, route)


def tile_product(tile, weight_flag, operand, transposed):
    if transposed:
        contraction = (((0,), (0,)), ((), ()))
        out_rows = tile.shape[1]
    else:
        contraction = (((1,), (0,)), ((), ()))
        out_rows = tile.shape[0]

    def compute():
        return lax.dot_general(tile, operand, contraction, preferred_element_type=jnp.float32)

    def skipped():
        return jnp.zeros((out_rows, operand.shape[1]), jnp.float32)

    return lax.cond(weight_flag > 0, compute, skipped)


def ring_shards(features, weight, grad_out, tiles, tile_mask):
    domains = lax.axis_size("dom")
    replicas = lax.axis_size("rep")
    sections = domains // replicas
    replica = lax.axis_index("rep")
    bit_count = replicas.bit_length() - 1
    rows_here = features.shape[0]
    hidden = features.shape[1]
    projected = jnp.dot(features, weight, preferred_element_type=jnp.float32).astype(jnp.bfloat16)
    current = projected
    for level in range(bit_count):
        shifted = shifted_2(current, "dom", sections << level)
        current = jnp.where(replica >> level & 1 == 1, shifted, current)
    partial_value = jnp.zeros((rows_here, hidden), jnp.float32)
    for section in range(sections):
        if section > 0:
            current = shifted_2(current, "dom", 1)
        partial_value = partial_value + tile_product(
            tiles[0, section], tile_mask[0, section], current, False
        )
    total = lax.psum(partial_value, "rep")
    gate_value = jax.nn.sigmoid(total)
    activated = (total * gate_value).astype(jnp.bfloat16)
    score_grad = (
        grad_out.astype(jnp.float32) * gate_value * (1.0 + total * (1.0 - gate_value))
    ).astype(jnp.bfloat16)
    carried = tile_product(tiles[0, sections - 1], tile_mask[0, sections - 1], score_grad, True)
    for section in range(sections - 2, -1, -1):
        carried = shifted_2(carried, "dom", -1)
        carried = carried + tile_product(tiles[0, section], tile_mask[0, section], score_grad, True)
    for level in range(bit_count):
        shifted = shifted_2(carried, "dom", -(sections << level))
        carried = jnp.where(replica >> level & 1 == 1, shifted, carried)
    node_grad = lax.psum(carried, "rep").astype(jnp.bfloat16)
    feature_grad = lax.dot_general(
        node_grad, weight, (((1,), (1,)), ((), ())), preferred_element_type=jnp.float32
    ).astype(jnp.bfloat16)
    scaling = (rows_here * domains) ** (-0.5)
    weight_term = lax.dot_general(
        features, node_grad, (((0,), (0,)), ((), ())), preferred_element_type=jnp.float32
    )
    weight_grad = lax.psum(weight_term, "dom") * scaling
    return (activated, feature_grad, weight_grad)


def layer_kernel(
    domains, scaling,
    x_hbm, w_hbm, g_hbm, tiles_hbm, mask_ref,
    act_hbm, fg_hbm, wg_hbm,
    act_ref, wg_ref, w_ref, g_ref, tiles, xs, ps, from_b, from_a, from_z, part, part_in, ax, st, ws, w_in, w_cross, w_cross_in, w_full, fg_half,
    own_sem, tile_sem, out_sem, x_recv, x_recv_p, x_send_z, x_send_a, x_send_b, x_send_p,
    part_send, part_recv,
    p_recv_p, p_send_p, b_send, b_recv, a_send, a_recv, z_send, z_recv,
    w_send, w_recv, last_send, last_recv,
):
    layers = domains // 4
    folds = layers.bit_length() - 1
    sections = domains // 2
    half = x_hbm.shape[0] // 2
    hidden = x_hbm.shape[1]
    d = lax.axis_index("dom")
    c = lax.axis_index("rep")
    other = 1 - c
    step_a, step_b = 1 + c, 2 - c
    z = d // 4
    a = (d // step_a) % 2
    b = (d // step_b) % 2

    def block_at(z_, b_, a_):
        return z_ * 4 + b_ * step_b + a_ * step_a

    dev_a, dev_b = block_at(z, b, 1 - a), block_at(z, 1 - b, a)
    dev_fold = [block_at(z + (1 << f) * (1 - 2 * ((z // (1 << f)) % 2)), b, a) for f in range(folds)]
    far = dev_fold[1:]

    def copy_to(src, dst, send, recv, dom, rep):
        return pltpu.make_async_remote_copy(
            src_ref=src, dst_ref=dst, send_sem=send, recv_sem=recv,
            device_id=(dom, rep), device_id_type=MESH,
        )

    own_copies = [
        pltpu.make_async_copy(x_hbm.at[pl.ds(h * half, half)], xs.at[d, h], own_sem.at[h])
        for h in range(2)
    ]
    tile_copies = [
        pltpu.make_async_copy(w_hbm, w_ref, tile_sem.at[0]),
        pltpu.make_async_copy(g_hbm, g_ref, tile_sem.at[1]),
        pltpu.make_async_copy(tiles_hbm.at[0], tiles, tile_sem.at[2]),
    ]
    for copy in own_copies + tile_copies:
        copy.start()

    barrier = pltpu.get_barrier_semaphore()
    for dom, rep in [(dev_a, c), (dev_b, c), (d, other)] + [(f, c) for f in far]:
        pl.semaphore_signal(barrier, inc=1, device_id=(dom, rep), device_id_type=MESH)

    @pl.when(z > 0)
    def _():
        pl.semaphore_signal(barrier, inc=1, device_id=(d - 4, c), device_id_type=MESH)

    @pl.when(z < layers - 1)
    def _():
        pl.semaphore_signal(barrier, inc=1, device_id=(d + 4, c), device_id_type=MESH)

    ends = jnp.where(z > 0, 1, 0) + jnp.where(z < layers - 1, 1, 0)
    pl.semaphore_wait(barrier, 3 + len(far) + ends)

    def owner(j):
        return ((d - j + domains) % domains) // sections

    def x_copy_z(j, z_, up):
        return copy_to(xs.at[j, c], xs.at[j, c], x_send_z.at[up, z_], x_recv.at[j], d - 4 + 8 * up, c)

    def x_copy_a(j, z_):
        return copy_to(xs.at[j, c], xs.at[j, c], x_send_a.at[z_], x_recv.at[j], dev_a, c)

    def x_copy_b(j, z_, a_):
        return copy_to(xs.at[j, c], xs.at[j, c], x_send_b.at[z_, a_], x_recv.at[j], dev_b, c)

    def x_copy_p(j):
        return copy_to(xs.at[j, c], xs.at[j, c], x_send_p.at[j], x_recv_p.at[j], d, other)

    def x_arrive(j):
        copy_to(xs.at[j, c], xs.at[j, c], x_send_p.at[j], x_recv.at[j], d, other).wait_recv()

        @pl.when(owner(j) != c)
        def _():
            x_copy_p(j).start()

    for copy in own_copies:
        copy.wait()

    @pl.when(z > 0)
    def _():
        x_copy_z(d, z, 0).start()

    @pl.when(z < layers - 1)
    def _():
        x_copy_z(d, z, 1).start()

    x_copy_b(d, z, a).start()
    x_copy_a(d, z).start()

    def layer_of(n):
        return z + ((n + 1) // 2) * (2 * ((n + 1) % 2) - 1)

    def in_range(z_):
        return jnp.logical_and(z_ >= 0, z_ < layers)

    def from_layer(n):
        z_ = layer_of(n)

        @pl.when(in_range(z_))
        def _():
            j = block_at(z_, b, a)
            x_arrive(j)

            @pl.when(jnp.logical_and(z_ < z, z < layers - 1))
            def _():
                x_copy_z(j, z_, 1).start()

            @pl.when(jnp.logical_and(z_ > z, z > 0))
            def _():
                x_copy_z(j, z_, 0).start()

            x_copy_b(j, z_, a).start()
            x_copy_a(j, z_).start()

    def from_a_side(n):
        z_ = layer_of(n)

        @pl.when(in_range(z_))
        def _():
            j = block_at(z_, b, 1 - a)
            x_arrive(j)
            x_copy_b(j, z_, 1 - a).start()

    def from_b_side(n):
        z_ = layer_of(n)

        @pl.when(in_range(z_))
        def _():
            x_arrive(block_at(z_, 1 - b, a))
            x_arrive(block_at(z_, 1 - b, 1 - a))

    def flag(o):
        return jnp.where(mask_ref[0, o] > 0, 1.0, 0.0)

    def product(j):
        o = (d - j + domains) % domains - c * sections
        m = flag(o).astype(BF16)
        x_top, x_low = xs[j, 0] * m, xs[j, 1] * m
        for r in range(2):
            rows = pl.ds(r * half, half)
            part[r] += jnp.dot(
                tiles[o, rows, pl.ds(0, half)], x_top, preferred_element_type=F32
            ) + jnp.dot(tiles[o, rows, pl.ds(half, half)], x_low, preferred_element_type=F32)

    def products(n):
        z_ = layer_of(n)

        def one(q, carry):
            j = z_ * 4 + q

            @pl.when(owner(j) == c)
            def _():
                @pl.when(j != d)
                def _():
                    copy_to(
                        xs.at[j, other], xs.at[j, other], x_send_p.at[j], x_recv_p.at[j], d, other
                    ).wait_recv()

                product(j)

            return carry

        @pl.when(in_range(z_))
        def _():
            lax.fori_loop(0, 4, one, 0)

    visits = 2 * layers - 1
    for copy in tile_copies:
        copy.wait()
    for r in range(2):
        part[r] = jnp.zeros((half, hidden), F32)

    def gather_step(n, carry):
        for lag, step in enumerate((from_layer, from_a_side, from_b_side)):
            at = n - 2 * lag

            @pl.when(jnp.logical_and(at >= (1 if lag == 0 else 0), at < visits))
            def _():
                step(at)

        @pl.when(n >= 5)
        def _():
            products(n - 5)

        return carry

    lax.fori_loop(1, visits + 5, gather_step, 0)

    def part_copy(r):
        return copy_to(part.at[r], part_in.at[r], part_send.at[r], part_recv.at[r], d, other)

    for r in range(2):
        part_copy(r).start()

    for r in range(2):
        part_copy(r).wait_recv()
        rows = pl.ds(r * half, half)
        ax_here = (part[r] + part_in[r]).astype(BF16)
        ax[rows, :] = ax_here
        total = jnp.dot(ax_here, w_ref[...], preferred_element_type=F32)
        gate = jax.nn.sigmoid(total)
        act_ref[rows, :] = (total * gate).astype(BF16)
        score = g_ref[rows, :].astype(F32) * gate * (1.0 + total * (1.0 - gate))
        st[:, rows] = jnp.transpose(score).astype(BF16)
    act_out = pltpu.make_async_copy(act_ref, act_hbm, out_sem.at[0])
    act_out.start()

    quarter = hidden // 2
    sizes, bases = [quarter], [0]
    for f in range(folds):
        sizes.append(sizes[-1] // 2)
        bases.append(bases[-1] + ((z // (1 << f)) % 2) * sizes[-1])

    def fold_copy(f):
        there = bases[f] + (1 - (z // (1 << f)) % 2) * sizes[f + 1]
        rows = pl.ds(pl.multiple_of(there, sizes[f + 1]), sizes[f + 1])
        return copy_to(
            ws.at[rows], w_in.at[f, pl.ds(0, sizes[f + 1])], w_send.at[f], w_recv.at[f], dev_fold[f], c
        )

    def cross_copy(i):
        return copy_to(
            w_cross.at[i], w_cross_in.at[i], w_send.at[folds + i], w_recv.at[folds + i],
            (dev_a, dev_b)[i], c,
        )

    def unfold_copy(f):
        rows = pl.ds(pl.multiple_of(bases[f + 1], sizes[f + 1]), sizes[f + 1])
        return copy_to(
            w_full.at[c, rows], w_full.at[c, rows], w_send.at[folds + 2 + f], w_recv.at[folds + 2 + f],
            dev_fold[f], c,
        )

    def weight_step(s):
        if s < folds:
            fold_copy(s).wait_recv()
            rows = pl.ds(pl.multiple_of(bases[s + 1], sizes[s + 1]), sizes[s + 1])
            ws[rows, :] += w_in[s, pl.ds(0, sizes[s + 1])]
            if s + 1 < folds:
                fold_copy(s + 1).start()
            else:
                w_cross[0] = ws[rows, :]
                cross_copy(0).start()
        elif s < folds + 2:
            i = s - folds
            cross_copy(i).wait_recv()
            if i == 0:
                w_cross[1] = w_cross[0] + w_cross_in[0]
                cross_copy(1).start()
            else:
                rows = pl.ds(pl.multiple_of(bases[folds], sizes[folds]), sizes[folds])
                w_full[c, rows] = w_cross[1] + w_cross_in[1]
                unfold_copy(folds - 1).start()
        else:
            f = 2 * folds + 1 - s
            unfold_copy(f).wait_recv()
            if f > 0:
                unfold_copy(f - 1).start()

    weight_steps = 2 * folds + 2

    ws[...] = jnp.dot(
        st[pl.ds(pl.multiple_of(c * quarter, quarter), quarter), :], ax[...],
        preferred_element_type=F32,
    )
    fold_copy(0).start()

    near = jnp.minimum(z, layers - 1 - z)
    reach = layers - 1 - near
    long_side = jnp.where(z == near, 1, -1)

    def target_layer(t):
        u = t - (reach - near)
        return jnp.where(
            u < 0, z + long_side * (reach - t), z + (1 - 2 * (u % 2)) * (near - u // 2)
        )

    def piece(k):
        z_ = target_layer(k // 4)
        q = k % 4
        b_ = jnp.where(q < 2, 1 - b, b)
        a_ = jnp.where(q % 2 == 0, 1 - a, a)
        return z_, b_, a_, block_at(z_, b_, a_)

    def p_copy(j):
        return copy_to(ps.at[j, other], ps.at[j, other], p_send_p.at[j], p_recv_p.at[j], d, other)

    def b_copy(z_, a_):
        return copy_to(
            ps.at[block_at(z_, 1 - b, a_), c], from_b.at[z_, a_], b_send.at[z_, a_], b_recv.at[z_, a_],
            dev_b, c,
        )

    def a_copy(z_):
        return copy_to(
            ps.at[block_at(z_, b, 1 - a), c], from_a.at[z_], a_send.at[z_], a_recv.at[z_], dev_a, c
        )

    def z_copy(z_, up):
        return copy_to(
            ps.at[block_at(z_, b, a), c], from_z.at[up, z_], z_send.at[z_], z_recv.at[up, z_],
            d - 4 + 8 * up, c,
        )

    def backward(k, carry):
        z_, b_, a_, j = piece(k)

        @pl.when(owner(j) == c)
        def _():
            o = (d - j + domains) % domains - c * sections
            m = flag(o)
            for h in range(2):
                ps[j, h] = (
                    jnp.dot(st[...], tiles[o, :, pl.ds(h * half, half)], preferred_element_type=F32) * m
                ).astype(BF16)
            p_copy(j).start()

            @pl.when(jnp.logical_and(b_ != b, k < 8))
            def _():
                b_copy(z_, a_).start()

        return carry

    lax.fori_loop(0, domains, backward, 0)

    def relay_partner(k, carry):
        z_, b_, a_, j = piece(k)

        @pl.when(owner(j) != c)
        def _():
            copy_to(ps.at[j, c], ps.at[j, c], p_send_p.at[j], p_recv_p.at[j], d, other).wait_recv()

            @pl.when(jnp.logical_and(b_ != b, k < 8))
            def _():
                b_copy(z_, a_).start()

        return carry

    lax.fori_loop(0, domains, relay_partner, 0)

    def stage_a(t):
        z_ = target_layer(t)
        b_copy(z_, 1 - a).wait_recv()
        j = block_at(z_, b, 1 - a)
        ps[j, c] = (ps[j, c].astype(F32) + from_b[z_, 1 - a].astype(F32)).astype(BF16)
        a_copy(z_).start()

    def stage_z(t):
        z_ = target_layer(t)
        b_copy(z_, a).wait_recv()
        a_copy(z_).wait_recv()
        j = block_at(z_, b, a)

        def mine():
            return ps[j, c].astype(F32) + from_b[z_, a].astype(F32) + from_a[z_].astype(F32)

        @pl.when(z_ == z)
        def _():
            part[0] = mine()

        @pl.when(jnp.logical_and(z_ > z, z == 0))
        def _():
            ps[j, c] = mine().astype(BF16)
            z_copy(z_, 1).start()

        @pl.when(jnp.logical_and(z_ < z, z == layers - 1))
        def _():
            ps[j, c] = mine().astype(BF16)
            z_copy(z_, 0).start()

    def stage_relay(t):
        z_ = target_layer(t)
        j = block_at(z_, b, a)

        def pass_on(up):
            z_copy(z_, up).wait_recv()
            ps[j, c] = (
                ps[j, c].astype(F32) + from_b[z_, a].astype(F32) + from_a[z_].astype(F32)
                + from_z[up, z_].astype(F32)
            ).astype(BF16)
            z_copy(z_, up).start()

        @pl.when(jnp.logical_and(z_ > z, z > 0))
        def _():
            pass_on(1)

        @pl.when(jnp.logical_and(z_ < z, z < layers - 1))
        def _():
            pass_on(0)

    for r in range(2):
        part_copy(r).wait_send()

    stages = max(layers + 1, (weight_steps + 1) // 2)
    for t in range(stages):
        if t < layers:
            stage_a(t)
        if 2 * t < weight_steps:
            weight_step(2 * t)
        if t + 2 < layers:
            b_copy(target_layer(t + 2), 1 - a).start()
            b_copy(target_layer(t + 2), a).start()
        if 1 <= t <= layers:
            stage_z(t - 1)
        if t == 2:
            stage_relay(0)
        if 2 <= t <= layers:
            stage_relay(t - 1)
        if 2 * t + 1 < weight_steps:
            weight_step(2 * t + 1)

    w_last = copy_to(w_full.at[c], w_full.at[c], last_send.at[0], last_recv.at[0], d, other)
    w_last.start()

    @pl.when(z > 0)
    def _():
        z_copy(z, 1).wait_recv()
        part[0] += from_z[1, z].astype(F32)

    @pl.when(z < layers - 1)
    def _():
        z_copy(z, 0).wait_recv()
        part[0] += from_z[0, z].astype(F32)

    node = jnp.transpose(part[0]).astype(BF16)
    fg_half[c] = lax.dot_general(
        node, w_ref[...], (((1,), (1,)), ((), ())), preferred_element_type=F32
    ).astype(BF16)
    f_last = copy_to(fg_half.at[c], fg_half.at[c], last_send.at[1], last_recv.at[1], d, other)
    f_last.start()

    def fg_out(h):
        return pltpu.make_async_copy(
            fg_half.at[h], fg_hbm.at[pl.ds(pl.multiple_of(h * half, half), half)], out_sem.at[1 + h]
        )

    fg_out(c).start()

    copy_to(w_full.at[other], w_full.at[other], last_send.at[0], last_recv.at[0], d, other).wait_recv()
    for h in range(2):
        wg_ref[:, pl.ds(h * quarter, quarter)] = jnp.transpose(w_full[h]) * scaling
    wg_out = pltpu.make_async_copy(wg_ref, wg_hbm, out_sem.at[3])
    wg_out.start()

    def drain_p(j, carry):
        @pl.when(jnp.logical_and(owner(j) != c, j != d))
        def _():
            x_copy_p(j).wait_send()

        @pl.when(owner(j) == c)
        def _():
            p_copy(j).wait_send()

        return carry

    lax.fori_loop(0, domains, drain_p, 0)

    def drain(z_, carry):
        @pl.when(jnp.logical_and(z_ <= z, z < layers - 1))
        def _():
            x_copy_z(block_at(z_, b, a), z_, 1).wait_send()

        @pl.when(jnp.logical_and(z_ >= z, z > 0))
        def _():
            x_copy_z(block_at(z_, b, a), z_, 0).wait_send()

        x_copy_a(block_at(z_, b, a), z_).wait_send()
        a_copy(z_).wait_send()
        for a_ in range(2):
            x_copy_b(block_at(z_, b, a_), z_, a_).wait_send()
            b_copy(z_, a_).wait_send()

        @pl.when(z_ > z)
        def _():
            z_copy(z_, 1).wait_send()

        @pl.when(z_ < z)
        def _():
            z_copy(z_, 0).wait_send()

        return carry

    lax.fori_loop(0, layers, drain, 0)
    for f in range(folds):
        fold_copy(f).wait_send()
        unfold_copy(f).wait_send()
    for i in range(2):
        cross_copy(i).wait_send()
    copy_to(fg_half.at[other], fg_half.at[other], last_send.at[1], last_recv.at[1], d, other).wait_recv()
    fg_out(other).start()
    w_last.wait_send()
    f_last.wait_send()
    act_out.wait()
    wg_out.wait()
    for h in range(2):
        fg_out(h).wait()


def finish_kernel(act, fg, wg, act_out, fg_out, wg_out, sem):
    copies = []
    for src, dst in ((act, act_out), (fg, fg_out), (wg, wg_out)):
        rows = src.shape[0] // 2
        for h in range(2):
            part = pl.ds(h * rows, rows)
            copies.append(pltpu.make_async_copy(src.at[part], dst.at[part], sem.at[len(copies)]))
    for copy in copies:
        copy.start()
    for copy in copies:
        copy.wait()


def kernel_shards(features, weight, grad_out, tiles, tile_mask):
    domains = lax.axis_size("dom")
    layers = domains // 4
    folds = layers.bit_length() - 1
    sections = tiles.shape[1]
    rows, hidden = features.shape
    half, quarter = rows // 2, hidden // 2
    dma = pltpu.SemaphoreType.DMA
    out_shape = (
        jax.ShapeDtypeStruct((rows, hidden), BF16),
        jax.ShapeDtypeStruct((rows, hidden), BF16),
        jax.ShapeDtypeStruct((hidden, hidden), F32),
    )
    anywhere = [pl.BlockSpec(memory_space=pl.ANY)] * 3
    results = pl.pallas_call(
        functools.partial(layer_kernel, domains, float((rows * domains) ** (-0.5))),
        out_shape=out_shape,
        in_specs=[pl.BlockSpec(memory_space=pltpu.HBM)] * 4 + [pl.BlockSpec(memory_space=pltpu.SMEM)],
        out_specs=anywhere,
        scratch_shapes=[
            pltpu.VMEM((rows, hidden), BF16),
            pltpu.VMEM((hidden, hidden), F32),
            pltpu.VMEM(weight.shape, BF16),
            pltpu.VMEM((rows, hidden), BF16),
            pltpu.VMEM(tiles.shape[1:], BF16),
            pltpu.VMEM((domains, 2, half, hidden), BF16),
            pltpu.VMEM((domains, 2, hidden, half), BF16),
            pltpu.VMEM((layers, 2, hidden, half), BF16),
            pltpu.VMEM((layers, hidden, half), BF16),
            pltpu.VMEM((2, layers, hidden, half), BF16),
            pltpu.VMEM((2, half, hidden), F32),
            pltpu.VMEM((2, half, hidden), F32),
            pltpu.VMEM((rows, hidden), BF16),
            pltpu.VMEM((hidden, rows), BF16),
            pltpu.VMEM((quarter, hidden), F32),
            pltpu.VMEM((folds, quarter // 2, hidden), F32),
            pltpu.VMEM((2, quarter // layers, hidden), F32),
            pltpu.VMEM((2, quarter // layers, hidden), F32),
            pltpu.VMEM((2, quarter, hidden), F32),
            pltpu.VMEM((2, half, hidden), BF16),
            dma((2,)), dma((3,)), dma((4,)),
            dma((domains,)), dma((domains,)),
            dma((2, layers)), dma((layers,)), dma((layers, 2)), dma((domains,)),
            dma((2,)), dma((2,)),
            dma((domains,)), dma((domains,)),
            dma((layers, 2)), dma((layers, 2)),
            dma((layers,)), dma((layers,)),
            dma((layers,)), dma((2, layers)),
            dma((2 * folds + 2,)), dma((2 * folds + 2,)),
            dma((2,)), dma((2,)),
        ],
        compiler_params=pltpu.CompilerParams(
            collective_id=0, has_side_effects=True, vmem_limit_bytes=63 * 1024 * 1024
        ),
        cost_estimate=pl.CostEstimate(
            flops=4 * sections * rows * rows * hidden,
            bytes_accessed=2 * sections * rows * rows,
            transcendentals=rows * hidden,
        ),
    )(features, weight, grad_out, tiles, tile_mask)
    return pl.pallas_call(
        finish_kernel,
        out_shape=out_shape,
        in_specs=anywhere,
        out_specs=anywhere,
        scratch_shapes=[dma((6,))],
        cost_estimate=pl.CostEstimate(flops=0, bytes_accessed=6 * rows * hidden * 2, transcendentals=0),
    )(*results)


def solution(mesh):
    domains, replicas = mesh.shape["dom"], mesh.shape["rep"]
    paired = replicas == 2 and domains >= 8 and domains & (domains - 1) == 0
    placed = (P("dom", None), P(), P("dom", None), P("dom", "rep", None, None), P("dom", "rep"))
    return jax.shard_map(
        kernel_shards if paired else ring_shards,
        mesh=mesh,
        in_specs=placed,
        out_specs=(P("dom", None), P("dom", None), P()),
        check_vma=False,
    )
```

```python
import functools

import jax
import jax.numpy as jnp
from jax import lax
from jax.experimental import pallas as pl
from jax.experimental.pallas import tpu as pltpu
from jax.sharding import PartitionSpec as P

MESH = pl.DeviceIdType.MESH
F32 = jnp.float32
BF16 = jnp.bfloat16


def shifted_2(block, axis, distance):
    devices = range(lax.axis_size(axis))
    route = [((i - distance) % len(devices), i) for i in devices]
    return lax.ppermute(block, axis, route)


def tile_product(tile, weight_flag, operand, transposed):
    if transposed:
        contraction = (((0,), (0,)), ((), ()))
        out_rows = tile.shape[1]
    else:
        contraction = (((1,), (0,)), ((), ()))
        out_rows = tile.shape[0]

    def compute():
        return lax.dot_general(tile, operand, contraction, preferred_element_type=jnp.float32)

    def skipped():
        return jnp.zeros((out_rows, operand.shape[1]), jnp.float32)

    return lax.cond(weight_flag > 0, compute, skipped)


def ring_shards(features, weight, grad_out, tiles, tile_mask):
    domains = lax.axis_size("dom")
    replicas = lax.axis_size("rep")
    sections = domains // replicas
    replica = lax.axis_index("rep")
    bit_count = replicas.bit_length() - 1
    rows_here = features.shape[0]
    hidden = features.shape[1]
    projected = jnp.dot(features, weight, preferred_element_type=jnp.float32).astype(jnp.bfloat16)
    current = projected
    for level in range(bit_count):
        shifted = shifted_2(current, "dom", sections << level)
        current = jnp.where(replica >> level & 1 == 1, shifted, current)
    partial_value = jnp.zeros((rows_here, hidden), jnp.float32)
    for section in range(sections):
        if section > 0:
            current = shifted_2(current, "dom", 1)
        partial_value = partial_value + tile_product(
            tiles[0, section], tile_mask[0, section], current, False
        )
    total = lax.psum(partial_value, "rep")
    gate_value = jax.nn.sigmoid(total)
    activated = (total * gate_value).astype(jnp.bfloat16)
    score_grad = (
        grad_out.astype(jnp.float32) * gate_value * (1.0 + total * (1.0 - gate_value))
    ).astype(jnp.bfloat16)
    carried = tile_product(tiles[0, sections - 1], tile_mask[0, sections - 1], score_grad, True)
    for section in range(sections - 2, -1, -1):
        carried = shifted_2(carried, "dom", -1)
        carried = carried + tile_product(tiles[0, section], tile_mask[0, section], score_grad, True)
    for level in range(bit_count):
        shifted = shifted_2(carried, "dom", -(sections << level))
        carried = jnp.where(replica >> level & 1 == 1, shifted, carried)
    node_grad = lax.psum(carried, "rep").astype(jnp.bfloat16)
    feature_grad = lax.dot_general(
        node_grad, weight, (((1,), (1,)), ((), ())), preferred_element_type=jnp.float32
    ).astype(jnp.bfloat16)
    scaling = (rows_here * domains) ** (-0.5)
    weight_term = lax.dot_general(
        features, node_grad, (((0,), (0,)), ((), ())), preferred_element_type=jnp.float32
    )
    weight_grad = lax.psum(weight_term, "dom") * scaling
    return (activated, feature_grad, weight_grad)


def layer_kernel(
    domains, scaling,
    x_hbm, w_hbm, g_hbm, tiles_hbm, mask_ref,
    act_hbm, fg_hbm, wg_hbm,
    act_ref, wg_ref, w_ref, g_ref, tiles, xs, ps, from_b, from_a, from_z, part, part_in, ax, st, ws, w_in, w_cross, w_cross_in, w_full, fg_half,
    own_sem, tile_sem, out_sem, x_recv, x_recv_p, x_send_z, x_send_a, x_send_b, x_send_p,
    y_send, y_recv, y_send_z, y_recv_z, y_send_p, y_recv_p,
    part_send, part_recv,
    p_recv_p, p_send_p, b_send, b_recv, a_send, a_recv, z_send, z_recv,
    w_send, w_recv, last_send, last_recv,
):
    layers = domains // 4
    folds = layers.bit_length() - 1
    sections = domains // 2
    half = x_hbm.shape[0] // 2
    hidden = x_hbm.shape[1]
    cut = half * 3 // 4
    main, rest = pl.ds(0, cut), pl.ds(cut, half - cut)
    d = lax.axis_index("dom")
    c = lax.axis_index("rep")
    other = 1 - c
    step_a, step_b = 1 + c, 2 - c
    z = d // 4
    a = (d // step_a) % 2
    b = (d // step_b) % 2

    def block_at(z_, b_, a_):
        return z_ * 4 + b_ * step_b + a_ * step_a

    dev_a, dev_b = block_at(z, b, 1 - a), block_at(z, 1 - b, a)
    dev_fold = [block_at(z + (1 << f) * (1 - 2 * ((z // (1 << f)) % 2)), b, a) for f in range(folds)]
    far = dev_fold[1:]

    def copy_to(src, dst, send, recv, dom, rep):
        return pltpu.make_async_remote_copy(
            src_ref=src, dst_ref=dst, send_sem=send, recv_sem=recv,
            device_id=(dom, rep), device_id_type=MESH,
        )

    own_copies = [
        pltpu.make_async_copy(x_hbm.at[pl.ds(h * half, half)], xs.at[d, h], own_sem.at[h])
        for h in range(2)
    ]
    tile_copies = [
        pltpu.make_async_copy(w_hbm, w_ref, tile_sem.at[0]),
        pltpu.make_async_copy(g_hbm, g_ref, tile_sem.at[1]),
        pltpu.make_async_copy(tiles_hbm.at[0], tiles, tile_sem.at[2]),
    ]
    for copy in own_copies + tile_copies:
        copy.start()

    barrier = pltpu.get_barrier_semaphore()
    for dom, rep in [(dev_a, c), (dev_b, c), (d, other)] + [(f, c) for f in far]:
        pl.semaphore_signal(barrier, inc=1, device_id=(dom, rep), device_id_type=MESH)

    @pl.when(z > 0)
    def _():
        pl.semaphore_signal(barrier, inc=1, device_id=(d - 4, c), device_id_type=MESH)

    @pl.when(z < layers - 1)
    def _():
        pl.semaphore_signal(barrier, inc=1, device_id=(d + 4, c), device_id_type=MESH)

    ends = jnp.where(z > 0, 1, 0) + jnp.where(z < layers - 1, 1, 0)
    pl.semaphore_wait(barrier, 3 + len(far) + ends)

    def owner(j):
        return ((d - j + domains) % domains) // sections

    def x_copy_z(j, z_, up):
        return copy_to(xs.at[j, c, main], xs.at[j, c, main], x_send_z.at[up, z_], x_recv.at[j], d - 4 + 8 * up, c)

    def x_copy_a(j, z_):
        return copy_to(xs.at[j, c, main], xs.at[j, c, main], x_send_a.at[z_], x_recv.at[j], dev_a, c)

    def x_copy_b(j, z_, a_):
        return copy_to(xs.at[j, c, main], xs.at[j, c, main], x_send_b.at[z_, a_], x_recv.at[j], dev_b, c)

    def x_copy_p(j):
        return copy_to(xs.at[j, c, main], xs.at[j, c, main], x_send_p.at[j], x_recv_p.at[j], d, other)

    def y_copy_a():
        return copy_to(
            xs.at[d, c, rest], xs.at[d, c, rest], y_send.at[2], y_recv.at[d % 4], dev_a, c
        )

    def y_copy_b(a_):
        j = block_at(z, b, a_)
        return copy_to(xs.at[j, c, rest], xs.at[j, c, rest], y_send.at[a_], y_recv.at[j % 4], dev_b, c)

    def y_slab(z_, up):
        slab = xs.at[pl.ds(z_ * 4, 4), c, rest]
        return copy_to(slab, slab, y_send_z.at[up, z_], y_recv_z.at[z_], d - 4 + 8 * up, c)

    def y_copy_p(j):
        return copy_to(
            xs.at[j, c, rest], xs.at[j, c, rest], y_send_p.at[j], y_recv_p.at[j], d, other
        )

    def y_wait(b_, a_):
        j = block_at(z, b_, a_)
        copy_to(
            xs.at[j, c, rest], xs.at[j, c, rest], y_send.at[2], y_recv.at[j % 4], dev_a, c
        ).wait_recv()

    def y_to_partner(z_):
        def one(q, carry):
            j = z_ * 4 + q

            @pl.when(jnp.logical_and(owner(j) != c, j != d))
            def _():
                y_copy_p(j).start()

            return carry

        lax.fori_loop(0, 4, one, 0)

    def y_layer_done():
        y_wait(1 - b, a)
        y_wait(1 - b, 1 - a)

        @pl.when(z > 0)
        def _():
            y_slab(z, 0).start()

        @pl.when(z < layers - 1)
        def _():
            y_slab(z, 1).start()

        y_to_partner(z)

    def y_from_layer(n):
        z_ = layer_of(n)

        @pl.when(in_range(z_))
        def _():
            y_slab(z_, 0).wait_recv()

            @pl.when(jnp.logical_and(z_ < z, z < layers - 1))
            def _():
                y_slab(z_, 1).start()

            @pl.when(jnp.logical_and(z_ > z, z > 0))
            def _():
                y_slab(z_, 0).start()

            y_to_partner(z_)

    def x_arrive(j):
        copy_to(xs.at[j, c, main], xs.at[j, c, main], x_send_p.at[j], x_recv.at[j], d, other).wait_recv()

        @pl.when(owner(j) != c)
        def _():
            x_copy_p(j).start()

    for copy in own_copies:
        copy.wait()

    @pl.when(z > 0)
    def _():
        x_copy_z(d, z, 0).start()

    @pl.when(z < layers - 1)
    def _():
        x_copy_z(d, z, 1).start()

    x_copy_b(d, z, a).start()
    x_copy_a(d, z).start()
    y_copy_b(a).start()
    y_copy_a().start()

    def layer_of(n):
        return z + ((n + 1) // 2) * (2 * ((n + 1) % 2) - 1)

    def in_range(z_):
        return jnp.logical_and(z_ >= 0, z_ < layers)

    def from_layer(n):
        z_ = layer_of(n)

        @pl.when(in_range(z_))
        def _():
            j = block_at(z_, b, a)
            x_arrive(j)

            @pl.when(jnp.logical_and(z_ < z, z < layers - 1))
            def _():
                x_copy_z(j, z_, 1).start()

            @pl.when(jnp.logical_and(z_ > z, z > 0))
            def _():
                x_copy_z(j, z_, 0).start()

            x_copy_b(j, z_, a).start()
            x_copy_a(j, z_).start()

    def from_a_side(n):
        z_ = layer_of(n)

        @pl.when(in_range(z_))
        def _():
            j = block_at(z_, b, 1 - a)
            x_arrive(j)
            x_copy_b(j, z_, 1 - a).start()

    def from_b_side(n):
        z_ = layer_of(n)

        @pl.when(in_range(z_))
        def _():
            x_arrive(block_at(z_, 1 - b, a))
            x_arrive(block_at(z_, 1 - b, 1 - a))

    def flag(o):
        return jnp.where(mask_ref[0, o] > 0, 1.0, 0.0)

    def product(j):
        o = (d - j + domains) % domains - c * sections
        m = flag(o).astype(BF16)
        x_top, x_low = xs[j, 0] * m, xs[j, 1] * m
        for r in range(2):
            rows = pl.ds(r * half, half)
            part[r] += jnp.dot(
                tiles[o, rows, pl.ds(0, half)], x_top, preferred_element_type=F32
            ) + jnp.dot(tiles[o, rows, pl.ds(half, half)], x_low, preferred_element_type=F32)

    def products(n):
        z_ = layer_of(n)

        def one(q, carry):
            j = z_ * 4 + q

            @pl.when(owner(j) == c)
            def _():
                @pl.when(j != d)
                def _():
                    for send, recv, rows in ((x_send_p, x_recv_p, main), (y_send_p, y_recv_p, rest)):
                        copy_to(
                            xs.at[j, other, rows], xs.at[j, other, rows], send.at[j], recv.at[j], d, other
                        ).wait_recv()

                product(j)

            return carry

        @pl.when(in_range(z_))
        def _():
            lax.fori_loop(0, 4, one, 0)

    visits = 2 * layers - 1
    for copy in tile_copies:
        copy.wait()
    for r in range(2):
        part[r] = jnp.zeros((half, hidden), F32)

    y_wait(b, 1 - a)
    y_copy_b(1 - a).start()

    def gather_step(n, carry):
        for lag, step in enumerate((from_layer, from_a_side, from_b_side)):
            at = n - 2 * lag

            @pl.when(jnp.logical_and(at >= (1 if lag == 0 else 0), at < visits))
            def _():
                step(at)

        @pl.when(n == 2)
        def _():
            y_layer_done()

        @pl.when(jnp.logical_and(n >= 4, n - 3 < visits))
        def _():
            y_from_layer(n - 3)

        @pl.when(n >= 5)
        def _():
            products(n - 5)

        return carry

    lax.fori_loop(1, visits + 5, gather_step, 0)

    def part_copy(r):
        return copy_to(part.at[r], part_in.at[r], part_send.at[r], part_recv.at[r], d, other)

    for r in range(2):
        part_copy(r).start()

    for r in range(2):
        part_copy(r).wait_recv()
        rows = pl.ds(r * half, half)
        ax_here = (part[r] + part_in[r]).astype(BF16)
        ax[rows, :] = ax_here
        total = jnp.dot(ax_here, w_ref[...], preferred_element_type=F32)
        gate = jax.nn.sigmoid(total)
        act_ref[rows, :] = (total * gate).astype(BF16)
        score = g_ref[rows, :].astype(F32) * gate * (1.0 + total * (1.0 - gate))
        st[:, rows] = jnp.transpose(score).astype(BF16)
    act_out = pltpu.make_async_copy(act_ref, act_hbm, out_sem.at[0])
    act_out.start()

    quarter = hidden // 2
    sizes, bases = [quarter], [0]
    for f in range(folds):
        sizes.append(sizes[-1] // 2)
        bases.append(bases[-1] + ((z // (1 << f)) % 2) * sizes[-1])

    def fold_copy(f):
        there = bases[f] + (1 - (z // (1 << f)) % 2) * sizes[f + 1]
        rows = pl.ds(pl.multiple_of(there, sizes[f + 1]), sizes[f + 1])
        return copy_to(
            ws.at[rows], w_in.at[f, pl.ds(0, sizes[f + 1])], w_send.at[f], w_recv.at[f], dev_fold[f], c
        )

    def cross_copy(i):
        return copy_to(
            w_cross.at[i], w_cross_in.at[i], w_send.at[folds + i], w_recv.at[folds + i],
            (dev_a, dev_b)[i], c,
        )

    def unfold_copy(f):
        rows = pl.ds(pl.multiple_of(bases[f + 1], sizes[f + 1]), sizes[f + 1])
        return copy_to(
            w_full.at[c, rows], w_full.at[c, rows], w_send.at[folds + 2 + f], w_recv.at[folds + 2 + f],
            dev_fold[f], c,
        )

    def weight_step(s):
        if s < folds:
            fold_copy(s).wait_recv()
            rows = pl.ds(pl.multiple_of(bases[s + 1], sizes[s + 1]), sizes[s + 1])
            ws[rows, :] += w_in[s, pl.ds(0, sizes[s + 1])]
            if s + 1 < folds:
                fold_copy(s + 1).start()
            else:
                w_cross[0] = ws[rows, :]
                cross_copy(0).start()
        elif s < folds + 2:
            i = s - folds
            cross_copy(i).wait_recv()
            if i == 0:
                w_cross[1] = w_cross[0] + w_cross_in[0]
                cross_copy(1).start()
            else:
                rows = pl.ds(pl.multiple_of(bases[folds], sizes[folds]), sizes[folds])
                w_full[c, rows] = w_cross[1] + w_cross_in[1]
                unfold_copy(folds - 1).start()
        else:
            f = 2 * folds + 1 - s
            unfold_copy(f).wait_recv()
            if f > 0:
                unfold_copy(f - 1).start()

    weight_steps = 2 * folds + 2

    ws[...] = jnp.dot(
        st[pl.ds(pl.multiple_of(c * quarter, quarter), quarter), :], ax[...],
        preferred_element_type=F32,
    )
    fold_copy(0).start()

    near = jnp.minimum(z, layers - 1 - z)
    reach = layers - 1 - near
    long_side = jnp.where(z == near, 1, -1)

    def target_layer(t):
        u = t - (reach - near)
        return jnp.where(
            u < 0, z + long_side * (reach - t), z + (1 - 2 * (u % 2)) * (near - u // 2)
        )

    def piece(k):
        z_ = target_layer(k // 4)
        q = k % 4
        b_ = jnp.where(q < 2, 1 - b, b)
        a_ = jnp.where(q % 2 == 0, 1 - a, a)
        return z_, b_, a_, block_at(z_, b_, a_)

    def p_copy(j):
        return copy_to(ps.at[j, other], ps.at[j, other], p_send_p.at[j], p_recv_p.at[j], d, other)

    def b_copy(z_, a_):
        return copy_to(
            ps.at[block_at(z_, 1 - b, a_), c], from_b.at[z_, a_], b_send.at[z_, a_], b_recv.at[z_, a_],
            dev_b, c,
        )

    def a_copy(z_):
        return copy_to(
            ps.at[block_at(z_, b, 1 - a), c], from_a.at[z_], a_send.at[z_], a_recv.at[z_], dev_a, c
        )

    def z_copy(z_, up):
        return copy_to(
            ps.at[block_at(z_, b, a), c], from_z.at[up, z_], z_send.at[z_], z_recv.at[up, z_],
            d - 4 + 8 * up, c,
        )

    def backward(k, carry):
        z_, b_, a_, j = piece(k)

        @pl.when(owner(j) == c)
        def _():
            o = (d - j + domains) % domains - c * sections
            m = flag(o)
            for h in range(2):
                ps[j, h] = (
                    jnp.dot(st[...], tiles[o, :, pl.ds(h * half, half)], preferred_element_type=F32) * m
                ).astype(BF16)
            p_copy(j).start()

            @pl.when(jnp.logical_and(b_ != b, k < 8))
            def _():
                b_copy(z_, a_).start()

        return carry

    lax.fori_loop(0, domains, backward, 0)

    def relay_partner(k, carry):
        z_, b_, a_, j = piece(k)

        @pl.when(owner(j) != c)
        def _():
            copy_to(ps.at[j, c], ps.at[j, c], p_send_p.at[j], p_recv_p.at[j], d, other).wait_recv()

            @pl.when(jnp.logical_and(b_ != b, k < 8))
            def _():
                b_copy(z_, a_).start()

        return carry

    lax.fori_loop(0, domains, relay_partner, 0)

    def stage_a(t):
        z_ = target_layer(t)
        b_copy(z_, 1 - a).wait_recv()
        j = block_at(z_, b, 1 - a)
        ps[j, c] = (ps[j, c].astype(F32) + from_b[z_, 1 - a].astype(F32)).astype(BF16)
        a_copy(z_).start()

    def stage_z(t):
        z_ = target_layer(t)
        b_copy(z_, a).wait_recv()
        a_copy(z_).wait_recv()
        j = block_at(z_, b, a)

        def mine():
            return ps[j, c].astype(F32) + from_b[z_, a].astype(F32) + from_a[z_].astype(F32)

        @pl.when(z_ == z)
        def _():
            part[0] = mine()

        @pl.when(jnp.logical_and(z_ > z, z == 0))
        def _():
            ps[j, c] = mine().astype(BF16)
            z_copy(z_, 1).start()

        @pl.when(jnp.logical_and(z_ < z, z == layers - 1))
        def _():
            ps[j, c] = mine().astype(BF16)
            z_copy(z_, 0).start()

    def stage_relay(t):
        z_ = target_layer(t)
        j = block_at(z_, b, a)

        def pass_on(up):
            z_copy(z_, up).wait_recv()
            ps[j, c] = (
                ps[j, c].astype(F32) + from_b[z_, a].astype(F32) + from_a[z_].astype(F32)
                + from_z[up, z_].astype(F32)
            ).astype(BF16)
            z_copy(z_, up).start()

        @pl.when(jnp.logical_and(z_ > z, z > 0))
        def _():
            pass_on(1)

        @pl.when(jnp.logical_and(z_ < z, z < layers - 1))
        def _():
            pass_on(0)

    for r in range(2):
        part_copy(r).wait_send()

    stages = max(layers + 1, (weight_steps + 1) // 2)
    for t in range(stages):
        if t < layers:
            stage_a(t)
        if 2 * t < weight_steps:
            weight_step(2 * t)
        if t + 2 < layers:
            b_copy(target_layer(t + 2), 1 - a).start()
            b_copy(target_layer(t + 2), a).start()
        if 1 <= t <= layers:
            stage_z(t - 1)
        if t == 2:
            stage_relay(0)
        if 2 <= t <= layers:
            stage_relay(t - 1)
        if 2 * t + 1 < weight_steps:
            weight_step(2 * t + 1)

    w_last = copy_to(w_full.at[c], w_full.at[c], last_send.at[0], last_recv.at[0], d, other)
    w_last.start()

    @pl.when(z > 0)
    def _():
        z_copy(z, 1).wait_recv()
        part[0] += from_z[1, z].astype(F32)

    @pl.when(z < layers - 1)
    def _():
        z_copy(z, 0).wait_recv()
        part[0] += from_z[0, z].astype(F32)

    node = jnp.transpose(part[0]).astype(BF16)
    fg_half[c] = lax.dot_general(
        node, w_ref[...], (((1,), (1,)), ((), ())), preferred_element_type=F32
    ).astype(BF16)
    f_last = copy_to(fg_half.at[c], fg_half.at[c], last_send.at[1], last_recv.at[1], d, other)
    f_last.start()

    def fg_out(h):
        return pltpu.make_async_copy(
            fg_half.at[h], fg_hbm.at[pl.ds(pl.multiple_of(h * half, half), half)], out_sem.at[1 + h]
        )

    fg_out(c).start()

    copy_to(w_full.at[other], w_full.at[other], last_send.at[0], last_recv.at[0], d, other).wait_recv()
    for h in range(2):
        wg_ref[:, pl.ds(h * quarter, quarter)] = jnp.transpose(w_full[h]) * scaling
    wg_out = pltpu.make_async_copy(wg_ref, wg_hbm, out_sem.at[3])
    wg_out.start()

    def drain_p(j, carry):
        @pl.when(jnp.logical_and(owner(j) != c, j != d))
        def _():
            x_copy_p(j).wait_send()
            y_copy_p(j).wait_send()

        @pl.when(owner(j) == c)
        def _():
            p_copy(j).wait_send()

        return carry

    lax.fori_loop(0, domains, drain_p, 0)

    def drain(z_, carry):
        @pl.when(jnp.logical_and(z_ <= z, z < layers - 1))
        def _():
            x_copy_z(block_at(z_, b, a), z_, 1).wait_send()
            y_slab(z_, 1).wait_send()

        @pl.when(jnp.logical_and(z_ >= z, z > 0))
        def _():
            x_copy_z(block_at(z_, b, a), z_, 0).wait_send()
            y_slab(z_, 0).wait_send()

        x_copy_a(block_at(z_, b, a), z_).wait_send()
        a_copy(z_).wait_send()
        for a_ in range(2):
            x_copy_b(block_at(z_, b, a_), z_, a_).wait_send()
            b_copy(z_, a_).wait_send()

        @pl.when(z_ > z)
        def _():
            z_copy(z_, 1).wait_send()

        @pl.when(z_ < z)
        def _():
            z_copy(z_, 0).wait_send()

        return carry

    lax.fori_loop(0, layers, drain, 0)
    y_copy_a().wait_send()
    for a_ in range(2):
        y_copy_b(a_).wait_send()
    for f in range(folds):
        fold_copy(f).wait_send()
        unfold_copy(f).wait_send()
    for i in range(2):
        cross_copy(i).wait_send()
    copy_to(fg_half.at[other], fg_half.at[other], last_send.at[1], last_recv.at[1], d, other).wait_recv()
    fg_out(other).start()
    w_last.wait_send()
    f_last.wait_send()
    act_out.wait()
    wg_out.wait()
    for h in range(2):
        fg_out(h).wait()


def finish_kernel(act, fg, wg, act_out, fg_out, wg_out, act_v, fg_v, wg_v, sem):
    pairs = ((act, act_v, act_out), (fg, fg_v, fg_out), (wg, wg_v, wg_out))
    inward = [pltpu.make_async_copy(p[0], p[1], sem.at[0, i]) for i, p in enumerate(pairs)]
    outward = [pltpu.make_async_copy(p[1], p[2], sem.at[1, i]) for i, p in enumerate(pairs)]
    for copy in inward:
        copy.start()
    for first, second in zip(inward, outward):
        first.wait()
        second.start()
    for copy in outward:
        copy.wait()


def kernel_shards(features, weight, grad_out, tiles, tile_mask):
    domains = lax.axis_size("dom")
    layers = domains // 4
    folds = layers.bit_length() - 1
    sections = tiles.shape[1]
    rows, hidden = features.shape
    half, quarter = rows // 2, hidden // 2
    dma = pltpu.SemaphoreType.DMA
    out_shape = (
        jax.ShapeDtypeStruct((rows, hidden), BF16),
        jax.ShapeDtypeStruct((rows, hidden), BF16),
        jax.ShapeDtypeStruct((hidden, hidden), F32),
    )
    anywhere = [pl.BlockSpec(memory_space=pl.ANY)] * 3
    results = pl.pallas_call(
        functools.partial(layer_kernel, domains, float((rows * domains) ** (-0.5))),
        out_shape=out_shape,
        in_specs=[pl.BlockSpec(memory_space=pltpu.HBM)] * 4 + [pl.BlockSpec(memory_space=pltpu.SMEM)],
        out_specs=anywhere,
        scratch_shapes=[
            pltpu.VMEM((rows, hidden), BF16),
            pltpu.VMEM((hidden, hidden), F32),
            pltpu.VMEM(weight.shape, BF16),
            pltpu.VMEM((rows, hidden), BF16),
            pltpu.VMEM(tiles.shape[1:], BF16),
            pltpu.VMEM((domains, 2, half, hidden), BF16),
            pltpu.VMEM((domains, 2, hidden, half), BF16),
            pltpu.VMEM((layers, 2, hidden, half), BF16),
            pltpu.VMEM((layers, hidden, half), BF16),
            pltpu.VMEM((2, layers, hidden, half), BF16),
            pltpu.VMEM((2, half, hidden), F32),
            pltpu.VMEM((2, half, hidden), F32),
            pltpu.VMEM((rows, hidden), BF16),
            pltpu.VMEM((hidden, rows), BF16),
            pltpu.VMEM((quarter, hidden), F32),
            pltpu.VMEM((folds, quarter // 2, hidden), F32),
            pltpu.VMEM((2, quarter // layers, hidden), F32),
            pltpu.VMEM((2, quarter // layers, hidden), F32),
            pltpu.VMEM((2, quarter, hidden), F32),
            pltpu.VMEM((2, half, hidden), BF16),
            dma((2,)), dma((3,)), dma((4,)),
            dma((domains,)), dma((domains,)),
            dma((2, layers)), dma((layers,)), dma((layers, 2)), dma((domains,)),
            dma((3,)), dma((4,)), dma((2, layers)), dma((layers,)), dma((domains,)), dma((domains,)),
            dma((2,)), dma((2,)),
            dma((domains,)), dma((domains,)),
            dma((layers, 2)), dma((layers, 2)),
            dma((layers,)), dma((layers,)),
            dma((layers,)), dma((2, layers)),
            dma((2 * folds + 2,)), dma((2 * folds + 2,)),
            dma((2,)), dma((2,)),
        ],
        compiler_params=pltpu.CompilerParams(
            collective_id=0, has_side_effects=True, vmem_limit_bytes=63 * 1024 * 1024
        ),
        cost_estimate=pl.CostEstimate(
            flops=4 * sections * rows * rows * hidden,
            bytes_accessed=2 * sections * rows * rows,
            transcendentals=rows * hidden,
        ),
    )(features, weight, grad_out, tiles, tile_mask)
    return pl.pallas_call(
        finish_kernel,
        out_shape=out_shape,
        in_specs=anywhere,
        out_specs=anywhere,
        scratch_shapes=[
            pltpu.VMEM((rows, hidden), BF16),
            pltpu.VMEM((rows, hidden), BF16),
            pltpu.VMEM((hidden, hidden), F32),
            dma((2, 3)),
        ],
        compiler_params=pltpu.CompilerParams(vmem_limit_bytes=63 * 1024 * 1024),
        cost_estimate=pl.CostEstimate(flops=0, bytes_accessed=6 * rows * hidden * 2, transcendentals=0),
    )(*results)


def solution(mesh):
    domains, replicas = mesh.shape["dom"], mesh.shape["rep"]
    paired = replicas == 2 and domains >= 8 and domains & (domains - 1) == 0
    placed = (P("dom", None), P(), P("dom", None), P("dom", "rep", None, None), P("dom", "rep"))
    return jax.shard_map(
        kernel_shards if paired else ring_shards,
        mesh=mesh,
        in_specs=placed,
        out_specs=(P("dom", None), P("dom", None), P()),
        check_vma=False,
    )
```

```python
import functools

import jax
import jax.numpy as jnp
from jax import lax
from jax.experimental import pallas as pl
from jax.experimental.pallas import tpu as pltpu
from jax.sharding import PartitionSpec as P

MESH = pl.DeviceIdType.MESH
F32 = jnp.float32
BF16 = jnp.bfloat16


def shifted_2(block, axis, distance):
    devices = range(lax.axis_size(axis))
    route = [((i - distance) % len(devices), i) for i in devices]
    return lax.ppermute(block, axis, route)


def tile_product(tile, weight_flag, operand, transposed):
    if transposed:
        contraction = (((0,), (0,)), ((), ()))
        out_rows = tile.shape[1]
    else:
        contraction = (((1,), (0,)), ((), ()))
        out_rows = tile.shape[0]

    def compute():
        return lax.dot_general(tile, operand, contraction, preferred_element_type=jnp.float32)

    def skipped():
        return jnp.zeros((out_rows, operand.shape[1]), jnp.float32)

    return lax.cond(weight_flag > 0, compute, skipped)


def ring_shards(features, weight, grad_out, tiles, tile_mask):
    domains = lax.axis_size("dom")
    replicas = lax.axis_size("rep")
    sections = domains // replicas
    replica = lax.axis_index("rep")
    bit_count = replicas.bit_length() - 1
    rows_here = features.shape[0]
    hidden = features.shape[1]
    projected = jnp.dot(features, weight, preferred_element_type=jnp.float32).astype(jnp.bfloat16)
    current = projected
    for level in range(bit_count):
        shifted = shifted_2(current, "dom", sections << level)
        current = jnp.where(replica >> level & 1 == 1, shifted, current)
    partial_value = jnp.zeros((rows_here, hidden), jnp.float32)
    for section in range(sections):
        if section > 0:
            current = shifted_2(current, "dom", 1)
        partial_value = partial_value + tile_product(
            tiles[0, section], tile_mask[0, section], current, False
        )
    total = lax.psum(partial_value, "rep")
    gate_value = jax.nn.sigmoid(total)
    activated = (total * gate_value).astype(jnp.bfloat16)
    score_grad = (
        grad_out.astype(jnp.float32) * gate_value * (1.0 + total * (1.0 - gate_value))
    ).astype(jnp.bfloat16)
    carried = tile_product(tiles[0, sections - 1], tile_mask[0, sections - 1], score_grad, True)
    for section in range(sections - 2, -1, -1):
        carried = shifted_2(carried, "dom", -1)
        carried = carried + tile_product(tiles[0, section], tile_mask[0, section], score_grad, True)
    for level in range(bit_count):
        shifted = shifted_2(carried, "dom", -(sections << level))
        carried = jnp.where(replica >> level & 1 == 1, shifted, carried)
    node_grad = lax.psum(carried, "rep").astype(jnp.bfloat16)
    feature_grad = lax.dot_general(
        node_grad, weight, (((1,), (1,)), ((), ())), preferred_element_type=jnp.float32
    ).astype(jnp.bfloat16)
    scaling = (rows_here * domains) ** (-0.5)
    weight_term = lax.dot_general(
        features, node_grad, (((0,), (0,)), ((), ())), preferred_element_type=jnp.float32
    )
    weight_grad = lax.psum(weight_term, "dom") * scaling
    return (activated, feature_grad, weight_grad)


def layer_kernel(
    domains, scaling,
    x_hbm, w_hbm, g_hbm, tiles_hbm, mask_ref,
    act_hbm, fg_hbm, wg_hbm,
    act_ref, wg_ref, w_ref, g_ref, tiles, xs, ps, rest_z, rest_in, from_b, from_a, from_z, part, part_in, ax, st, ws, w_in, w_cross, w_cross_in, w_full, fg_half,
    own_sem, tile_sem, out_sem, x_recv, x_recv_p, x_send_z, x_send_a, x_send_b, x_send_p,
    y_send, y_recv, y_send_z, y_recv_z, y_send_p, y_recv_p,
    part_send, part_recv,
    r_send, r_recv, r_send_in, r_recv_in,
    p_recv_p, p_send_p, b_send, b_recv, a_send, a_recv, z_send, z_recv,
    w_send, w_recv, last_send, last_recv,
):
    layers = domains // 4
    folds = layers.bit_length() - 1
    sections = domains // 2
    half = x_hbm.shape[0] // 2
    hidden = x_hbm.shape[1]
    cut = half * 7 // 8
    main, rest = pl.ds(0, cut), pl.ds(cut, half - cut)
    d = lax.axis_index("dom")
    c = lax.axis_index("rep")
    other = 1 - c
    step_a, step_b = 1 + c, 2 - c
    z = d // 4
    a = (d // step_a) % 2
    b = (d // step_b) % 2

    def block_at(z_, b_, a_):
        return z_ * 4 + b_ * step_b + a_ * step_a

    dev_a, dev_b = block_at(z, b, 1 - a), block_at(z, 1 - b, a)
    dev_fold = [block_at(z + (1 << f) * (1 - 2 * ((z // (1 << f)) % 2)), b, a) for f in range(folds)]
    far = dev_fold[1:]

    def copy_to(src, dst, send, recv, dom, rep):
        return pltpu.make_async_remote_copy(
            src_ref=src, dst_ref=dst, send_sem=send, recv_sem=recv,
            device_id=(dom, rep), device_id_type=MESH,
        )

    own_copies = [
        pltpu.make_async_copy(x_hbm.at[pl.ds(h * half, half)], xs.at[d, h], own_sem.at[h])
        for h in range(2)
    ]
    tile_copies = [
        pltpu.make_async_copy(w_hbm, w_ref, tile_sem.at[0]),
        pltpu.make_async_copy(g_hbm, g_ref, tile_sem.at[1]),
        pltpu.make_async_copy(tiles_hbm.at[0], tiles, tile_sem.at[2]),
    ]
    for copy in own_copies + tile_copies:
        copy.start()

    barrier = pltpu.get_barrier_semaphore()
    for dom, rep in [(dev_a, c), (dev_b, c), (d, other)] + [(f, c) for f in far]:
        pl.semaphore_signal(barrier, inc=1, device_id=(dom, rep), device_id_type=MESH)

    @pl.when(z > 0)
    def _():
        pl.semaphore_signal(barrier, inc=1, device_id=(d - 4, c), device_id_type=MESH)

    @pl.when(z < layers - 1)
    def _():
        pl.semaphore_signal(barrier, inc=1, device_id=(d + 4, c), device_id_type=MESH)

    ends = jnp.where(z > 0, 1, 0) + jnp.where(z < layers - 1, 1, 0)
    pl.semaphore_wait(barrier, 3 + len(far) + ends)

    def owner(j):
        return ((d - j + domains) % domains) // sections

    def x_copy_z(j, z_, up):
        return copy_to(xs.at[j, c, main], xs.at[j, c, main], x_send_z.at[up, z_], x_recv.at[j], d - 4 + 8 * up, c)

    def x_copy_a(j, z_):
        return copy_to(xs.at[j, c, main], xs.at[j, c, main], x_send_a.at[z_], x_recv.at[j], dev_a, c)

    def x_copy_b(j, z_, a_):
        return copy_to(xs.at[j, c, main], xs.at[j, c, main], x_send_b.at[z_, a_], x_recv.at[j], dev_b, c)

    def x_copy_p(j):
        return copy_to(xs.at[j, c, main], xs.at[j, c, main], x_send_p.at[j], x_recv_p.at[j], d, other)

    def y_copy_a():
        return copy_to(
            xs.at[d, c, rest], xs.at[d, c, rest], y_send.at[2], y_recv.at[d % 4], dev_a, c
        )

    def y_copy_b(a_):
        j = block_at(z, b, a_)
        return copy_to(xs.at[j, c, rest], xs.at[j, c, rest], y_send.at[a_], y_recv.at[j % 4], dev_b, c)

    def y_slab(z_, up):
        slab = xs.at[pl.ds(z_ * 4, 4), c, rest]
        return copy_to(slab, slab, y_send_z.at[up, z_], y_recv_z.at[z_], d - 4 + 8 * up, c)

    def y_copy_p(j):
        return copy_to(
            xs.at[j, c, rest], xs.at[j, c, rest], y_send_p.at[j], y_recv_p.at[j], d, other
        )

    def y_wait(b_, a_):
        j = block_at(z, b_, a_)
        copy_to(
            xs.at[j, c, rest], xs.at[j, c, rest], y_send.at[2], y_recv.at[j % 4], dev_a, c
        ).wait_recv()

    def y_to_partner(z_):
        def one(q, carry):
            j = z_ * 4 + q

            @pl.when(jnp.logical_and(owner(j) != c, j != d))
            def _():
                y_copy_p(j).start()

            return carry

        lax.fori_loop(0, 4, one, 0)

    def y_layer_done():
        y_wait(1 - b, a)
        y_wait(1 - b, 1 - a)

        @pl.when(z > 0)
        def _():
            y_slab(z, 0).start()

        @pl.when(z < layers - 1)
        def _():
            y_slab(z, 1).start()

        y_to_partner(z)

    def y_from_layer(n):
        z_ = layer_of(n)

        @pl.when(in_range(z_))
        def _():
            y_slab(z_, 0).wait_recv()

            @pl.when(jnp.logical_and(z_ < z, z < layers - 1))
            def _():
                y_slab(z_, 1).start()

            @pl.when(jnp.logical_and(z_ > z, z > 0))
            def _():
                y_slab(z_, 0).start()

            y_to_partner(z_)

    def x_arrive(j):
        copy_to(xs.at[j, c, main], xs.at[j, c, main], x_send_p.at[j], x_recv.at[j], d, other).wait_recv()

        @pl.when(owner(j) != c)
        def _():
            x_copy_p(j).start()

    for copy in own_copies:
        copy.wait()

    @pl.when(z > 0)
    def _():
        x_copy_z(d, z, 0).start()

    @pl.when(z < layers - 1)
    def _():
        x_copy_z(d, z, 1).start()

    x_copy_b(d, z, a).start()
    x_copy_a(d, z).start()
    y_copy_b(a).start()
    y_copy_a().start()

    def layer_of(n):
        return z + ((n + 1) // 2) * (2 * ((n + 1) % 2) - 1)

    def in_range(z_):
        return jnp.logical_and(z_ >= 0, z_ < layers)

    def from_layer(n):
        z_ = layer_of(n)

        @pl.when(in_range(z_))
        def _():
            j = block_at(z_, b, a)
            x_arrive(j)

            @pl.when(jnp.logical_and(z_ < z, z < layers - 1))
            def _():
                x_copy_z(j, z_, 1).start()

            @pl.when(jnp.logical_and(z_ > z, z > 0))
            def _():
                x_copy_z(j, z_, 0).start()

            x_copy_b(j, z_, a).start()
            x_copy_a(j, z_).start()

    def from_a_side(n):
        z_ = layer_of(n)

        @pl.when(in_range(z_))
        def _():
            j = block_at(z_, b, 1 - a)
            x_arrive(j)
            x_copy_b(j, z_, 1 - a).start()

    def from_b_side(n):
        z_ = layer_of(n)

        @pl.when(in_range(z_))
        def _():
            x_arrive(block_at(z_, 1 - b, a))
            x_arrive(block_at(z_, 1 - b, 1 - a))

    def flag(o):
        return jnp.where(mask_ref[0, o] > 0, 1.0, 0.0)

    def product(j):
        o = (d - j + domains) % domains - c * sections
        m = flag(o).astype(BF16)
        x_top, x_low = xs[j, 0] * m, xs[j, 1] * m
        for r in range(2):
            rows = pl.ds(r * half, half)
            part[r] += jnp.dot(
                tiles[o, rows, pl.ds(0, half)], x_top, preferred_element_type=F32
            ) + jnp.dot(tiles[o, rows, pl.ds(half, half)], x_low, preferred_element_type=F32)

    def products(n):
        z_ = layer_of(n)

        def one(q, carry):
            j = z_ * 4 + q

            @pl.when(owner(j) == c)
            def _():
                @pl.when(j != d)
                def _():
                    for send, recv, rows in ((x_send_p, x_recv_p, main), (y_send_p, y_recv_p, rest)):
                        copy_to(
                            xs.at[j, other, rows], xs.at[j, other, rows], send.at[j], recv.at[j], d, other
                        ).wait_recv()

                product(j)

            return carry

        @pl.when(in_range(z_))
        def _():
            lax.fori_loop(0, 4, one, 0)

    visits = 2 * layers - 1
    for copy in tile_copies:
        copy.wait()
    for r in range(2):
        part[r] = jnp.zeros((half, hidden), F32)

    y_wait(b, 1 - a)
    y_copy_b(1 - a).start()

    def gather_step(n, carry):
        for lag, step in ((1, from_a_side), (0, from_layer), (2, from_b_side)):
            at = n - 2 * lag

            @pl.when(jnp.logical_and(at >= (1 if lag == 0 else 0), at < visits))
            def _():
                step(at)

        @pl.when(n == 2)
        def _():
            y_layer_done()

        @pl.when(jnp.logical_and(n >= 4, n - 3 < visits))
        def _():
            y_from_layer(n - 3)

        @pl.when(n >= 5)
        def _():
            products(n - 5)

        return carry

    lax.fori_loop(1, visits + 5, gather_step, 0)

    def part_copy(r):
        return copy_to(part.at[r], part_in.at[r], part_send.at[r], part_recv.at[r], d, other)

    for r in range(2):
        part_copy(r).start()

    for r in range(2):
        part_copy(r).wait_recv()
        rows = pl.ds(r * half, half)
        ax_here = (part[r] + part_in[r]).astype(BF16)
        ax[rows, :] = ax_here
        total = jnp.dot(ax_here, w_ref[...], preferred_element_type=F32)
        gate = jax.nn.sigmoid(total)
        act_ref[rows, :] = (total * gate).astype(BF16)
        score = g_ref[rows, :].astype(F32) * gate * (1.0 + total * (1.0 - gate))
        st[:, rows] = jnp.transpose(score).astype(BF16)
    act_out = pltpu.make_async_copy(act_ref, act_hbm, out_sem.at[0])
    act_out.start()

    quarter = hidden // 2
    sizes, bases = [quarter], [0]
    for f in range(folds):
        sizes.append(sizes[-1] // 2)
        bases.append(bases[-1] + ((z // (1 << f)) % 2) * sizes[-1])

    def fold_copy(f):
        there = bases[f] + (1 - (z // (1 << f)) % 2) * sizes[f + 1]
        rows = pl.ds(pl.multiple_of(there, sizes[f + 1]), sizes[f + 1])
        return copy_to(
            ws.at[rows], w_in.at[f, pl.ds(0, sizes[f + 1])], w_send.at[f], w_recv.at[f], dev_fold[f], c
        )

    def cross_copy(i):
        return copy_to(
            w_cross.at[i], w_cross_in.at[i], w_send.at[folds + i], w_recv.at[folds + i],
            (dev_a, dev_b)[i], c,
        )

    def unfold_copy(f):
        rows = pl.ds(pl.multiple_of(bases[f + 1], sizes[f + 1]), sizes[f + 1])
        return copy_to(
            w_full.at[c, rows], w_full.at[c, rows], w_send.at[folds + 2 + f], w_recv.at[folds + 2 + f],
            dev_fold[f], c,
        )

    def weight_step(s):
        if s < folds:
            fold_copy(s).wait_recv()
            rows = pl.ds(pl.multiple_of(bases[s + 1], sizes[s + 1]), sizes[s + 1])
            ws[rows, :] += w_in[s, pl.ds(0, sizes[s + 1])]
            if s + 1 < folds:
                fold_copy(s + 1).start()
            else:
                w_cross[0] = ws[rows, :]
                cross_copy(0).start()
        elif s < folds + 2:
            i = s - folds
            cross_copy(i).wait_recv()
            if i == 0:
                w_cross[1] = w_cross[0] + w_cross_in[0]
                cross_copy(1).start()
            else:
                rows = pl.ds(pl.multiple_of(bases[folds], sizes[folds]), sizes[folds])
                w_full[c, rows] = w_cross[1] + w_cross_in[1]
                unfold_copy(folds - 1).start()
        else:
            f = 2 * folds + 1 - s
            unfold_copy(f).wait_recv()
            if f > 0:
                unfold_copy(f - 1).start()

    weight_steps = 2 * folds + 2

    ws[...] = jnp.dot(
        st[pl.ds(pl.multiple_of(c * quarter, quarter), quarter), :], ax[...],
        preferred_element_type=F32,
    )
    fold_copy(0).start()

    near = jnp.minimum(z, layers - 1 - z)
    reach = layers - 1 - near
    long_side = jnp.where(z == near, 1, -1)

    def target_layer(t):
        u = t - (reach - near)
        return jnp.where(
            u < 0, z + long_side * (reach - t), z + (1 - 2 * (u % 2)) * (near - u // 2)
        )

    def piece(k):
        z_ = target_layer(k // 4)
        q = k % 4
        b_ = jnp.where(q < 2, 1 - b, b)
        a_ = jnp.where(q % 2 == 0, 1 - a, a)
        return z_, b_, a_, block_at(z_, b_, a_)

    def p_copy(j):
        return copy_to(ps.at[j, other], ps.at[j, other], p_send_p.at[j], p_recv_p.at[j], d, other)

    def b_copy(z_, a_):
        return copy_to(
            ps.at[block_at(z_, 1 - b, a_), c, main], from_b.at[z_, a_, main],
            b_send.at[z_, a_], b_recv.at[z_, a_], dev_b, c,
        )

    def a_copy(z_):
        return copy_to(
            ps.at[block_at(z_, b, 1 - a), c, main], from_a.at[z_, main],
            a_send.at[z_], a_recv.at[z_], dev_a, c,
        )

    def z_copy(z_, up):
        return copy_to(
            ps.at[block_at(z_, b, a), c, main], from_z.at[up, z_, main],
            z_send.at[z_], z_recv.at[up, z_], d - 4 + 8 * up, c,
        )

    def r_slab(z_, up):
        return copy_to(
            ps.at[pl.ds(z_ * 4, 4), c, rest], rest_z.at[up, z_],
            r_send.at[z_], r_recv.at[up, z_], d - 4 + 8 * up, c,
        )

    def r_copy_b(a_):
        return copy_to(
            ps.at[block_at(z, 1 - b, a_), c, rest], rest_in.at[a_],
            r_send_in.at[a_], r_recv_in.at[a_], dev_b, c,
        )

    def r_copy_a():
        return copy_to(
            ps.at[block_at(z, b, 1 - a), c, rest], rest_in.at[2],
            r_send_in.at[2], r_recv_in.at[2], dev_a, c,
        )

    def rest_add(z_, up):
        r_slab(z_, up).wait_recv()
        slab = pl.ds(z_ * 4, 4)
        ps[slab, c, rest] = (ps[slab, c, rest].astype(F32) + rest_z[up, z_].astype(F32)).astype(BF16)

    def rest_first(t):
        z_ = target_layer(t)

        @pl.when(jnp.logical_and(z_ > z, z == 0))
        def _():
            r_slab(z_, 1).start()

        @pl.when(jnp.logical_and(z_ < z, z == layers - 1))
        def _():
            r_slab(z_, 0).start()

    def rest_relay(t):
        z_ = target_layer(t)

        @pl.when(jnp.logical_and(z_ > z, z > 0))
        def _():
            rest_add(z_, 1)
            r_slab(z_, 1).start()

        @pl.when(jnp.logical_and(z_ < z, z < layers - 1))
        def _():
            rest_add(z_, 0)
            r_slab(z_, 0).start()

    def rest_own():
        @pl.when(z > 0)
        def _():
            rest_add(z, 1)

        @pl.when(z < layers - 1)
        def _():
            rest_add(z, 0)

        r_copy_b(1 - a).start()
        r_copy_b(a).start()

    def rest_round():
        r_copy_b(1 - a).wait_recv()
        j = block_at(z, b, 1 - a)
        ps[j, c, rest] = (ps[j, c, rest].astype(F32) + rest_in[1 - a].astype(F32)).astype(BF16)
        r_copy_a().start()

    def backward(k, carry):
        z_, b_, a_, j = piece(k)

        @pl.when(owner(j) == c)
        def _():
            o = (d - j + domains) % domains - c * sections
            m = flag(o)
            for h in range(2):
                ps[j, h] = (
                    jnp.dot(st[...], tiles[o, :, pl.ds(h * half, half)], preferred_element_type=F32) * m
                ).astype(BF16)
            p_copy(j).start()

            @pl.when(jnp.logical_and(b_ != b, k < 8))
            def _():
                b_copy(z_, a_).start()

        return carry

    lax.fori_loop(0, domains, backward, 0)

    def relay_partner(k, carry):
        z_, b_, a_, j = piece(k)

        @pl.when(owner(j) != c)
        def _():
            copy_to(ps.at[j, c], ps.at[j, c], p_send_p.at[j], p_recv_p.at[j], d, other).wait_recv()

            @pl.when(jnp.logical_and(b_ != b, k < 8))
            def _():
                b_copy(z_, a_).start()

        return carry

    lax.fori_loop(0, domains, relay_partner, 0)

    def stage_a(t):
        z_ = target_layer(t)
        b_copy(z_, 1 - a).wait_recv()
        j = block_at(z_, b, 1 - a)
        ps[j, c, main] = (
            ps[j, c, main].astype(F32) + from_b[z_, 1 - a, main].astype(F32)
        ).astype(BF16)
        a_copy(z_).start()

    def stage_z(t):
        z_ = target_layer(t)
        b_copy(z_, a).wait_recv()
        a_copy(z_).wait_recv()
        j = block_at(z_, b, a)

        def mine():
            return (
                ps[j, c, main].astype(F32) + from_b[z_, a, main].astype(F32)
                + from_a[z_, main].astype(F32)
            )

        @pl.when(z_ == z)
        def _():
            part[0, main] = mine()

        @pl.when(jnp.logical_and(z_ > z, z == 0))
        def _():
            ps[j, c, main] = mine().astype(BF16)
            z_copy(z_, 1).start()

        @pl.when(jnp.logical_and(z_ < z, z == layers - 1))
        def _():
            ps[j, c, main] = mine().astype(BF16)
            z_copy(z_, 0).start()

    def stage_relay(t):
        z_ = target_layer(t)
        j = block_at(z_, b, a)

        def pass_on(up):
            z_copy(z_, up).wait_recv()
            ps[j, c, main] = (
                ps[j, c, main].astype(F32) + from_b[z_, a, main].astype(F32)
                + from_a[z_, main].astype(F32) + from_z[up, z_, main].astype(F32)
            ).astype(BF16)
            z_copy(z_, up).start()

        @pl.when(jnp.logical_and(z_ > z, z > 0))
        def _():
            pass_on(1)

        @pl.when(jnp.logical_and(z_ < z, z < layers - 1))
        def _():
            pass_on(0)

    for r in range(2):
        part_copy(r).wait_send()

    for t in range(layers - 1):
        rest_first(t)

    stages = max(layers + 1, (weight_steps + 1) // 2)
    for t in range(stages):
        if t < layers:
            stage_a(t)
        if 2 * t < weight_steps:
            weight_step(2 * t)
        if t + 2 < layers:
            b_copy(target_layer(t + 2), 1 - a).start()
            b_copy(target_layer(t + 2), a).start()
        if 1 <= t <= layers:
            stage_z(t - 1)
        if t == 2:
            stage_relay(0)
        if 2 <= t <= layers:
            stage_relay(t - 1)
        if 1 <= t < layers:
            rest_relay(t - 1)
        if t == layers - 1:
            rest_own()
        if t == layers:
            rest_round()
        if 2 * t + 1 < weight_steps:
            weight_step(2 * t + 1)

    w_last = copy_to(w_full.at[c], w_full.at[c], last_send.at[0], last_recv.at[0], d, other)
    w_last.start()

    @pl.when(z > 0)
    def _():
        z_copy(z, 1).wait_recv()
        part[0, main] += from_z[1, z, main].astype(F32)

    @pl.when(z < layers - 1)
    def _():
        z_copy(z, 0).wait_recv()
        part[0, main] += from_z[0, z, main].astype(F32)

    r_copy_b(a).wait_recv()
    r_copy_a().wait_recv()
    part[0, rest] = (
        ps[d, c, rest].astype(F32) + rest_in[a].astype(F32) + rest_in[2].astype(F32)
    )
    node = jnp.transpose(part[0]).astype(BF16)
    fg_half[c] = lax.dot_general(
        node, w_ref[...], (((1,), (1,)), ((), ())), preferred_element_type=F32
    ).astype(BF16)
    f_last = copy_to(fg_half.at[c], fg_half.at[c], last_send.at[1], last_recv.at[1], d, other)
    f_last.start()

    def fg_out(h):
        return pltpu.make_async_copy(
            fg_half.at[h], fg_hbm.at[pl.ds(pl.multiple_of(h * half, half), half)], out_sem.at[1 + h]
        )

    fg_out(c).start()

    copy_to(w_full.at[other], w_full.at[other], last_send.at[0], last_recv.at[0], d, other).wait_recv()
    for h in range(2):
        wg_ref[:, pl.ds(h * quarter, quarter)] = jnp.transpose(w_full[h]) * scaling
    wg_out = pltpu.make_async_copy(wg_ref, wg_hbm, out_sem.at[3])
    wg_out.start()

    def drain_p(j, carry):
        @pl.when(jnp.logical_and(owner(j) != c, j != d))
        def _():
            x_copy_p(j).wait_send()
            y_copy_p(j).wait_send()

        @pl.when(owner(j) == c)
        def _():
            p_copy(j).wait_send()

        return carry

    lax.fori_loop(0, domains, drain_p, 0)

    def drain(z_, carry):
        @pl.when(jnp.logical_and(z_ <= z, z < layers - 1))
        def _():
            x_copy_z(block_at(z_, b, a), z_, 1).wait_send()
            y_slab(z_, 1).wait_send()

        @pl.when(jnp.logical_and(z_ >= z, z > 0))
        def _():
            x_copy_z(block_at(z_, b, a), z_, 0).wait_send()
            y_slab(z_, 0).wait_send()

        x_copy_a(block_at(z_, b, a), z_).wait_send()
        a_copy(z_).wait_send()
        for a_ in range(2):
            x_copy_b(block_at(z_, b, a_), z_, a_).wait_send()
            b_copy(z_, a_).wait_send()

        @pl.when(z_ > z)
        def _():
            z_copy(z_, 1).wait_send()
            r_slab(z_, 1).wait_send()

        @pl.when(z_ < z)
        def _():
            z_copy(z_, 0).wait_send()
            r_slab(z_, 0).wait_send()

        return carry

    lax.fori_loop(0, layers, drain, 0)
    y_copy_a().wait_send()
    for a_ in range(2):
        y_copy_b(a_).wait_send()
        r_copy_b(a_).wait_send()
    r_copy_a().wait_send()
    for f in range(folds):
        fold_copy(f).wait_send()
        unfold_copy(f).wait_send()
    for i in range(2):
        cross_copy(i).wait_send()
    copy_to(fg_half.at[other], fg_half.at[other], last_send.at[1], last_recv.at[1], d, other).wait_recv()
    fg_out(other).start()
    w_last.wait_send()
    f_last.wait_send()
    act_out.wait()
    wg_out.wait()
    for h in range(2):
        fg_out(h).wait()


def finish_kernel(act, fg, wg, act_out, fg_out, wg_out, act_v, fg_v, wg_v, sem):
    pairs = ((act, act_v, act_out), (fg, fg_v, fg_out), (wg, wg_v, wg_out))
    inward = [pltpu.make_async_copy(p[0], p[1], sem.at[0, i]) for i, p in enumerate(pairs)]
    outward = [pltpu.make_async_copy(p[1], p[2], sem.at[1, i]) for i, p in enumerate(pairs)]
    for copy in inward:
        copy.start()
    for first, second in zip(inward, outward):
        first.wait()
        second.start()
    for copy in outward:
        copy.wait()


def kernel_shards(features, weight, grad_out, tiles, tile_mask):
    domains = lax.axis_size("dom")
    layers = domains // 4
    folds = layers.bit_length() - 1
    sections = tiles.shape[1]
    rows, hidden = features.shape
    half, quarter = rows // 2, hidden // 2
    dma = pltpu.SemaphoreType.DMA
    out_shape = (
        jax.ShapeDtypeStruct((rows, hidden), BF16),
        jax.ShapeDtypeStruct((rows, hidden), BF16),
        jax.ShapeDtypeStruct((hidden, hidden), F32),
    )
    anywhere = [pl.BlockSpec(memory_space=pl.ANY)] * 3
    results = pl.pallas_call(
        functools.partial(layer_kernel, domains, float((rows * domains) ** (-0.5))),
        out_shape=out_shape,
        in_specs=[pl.BlockSpec(memory_space=pltpu.HBM)] * 4 + [pl.BlockSpec(memory_space=pltpu.SMEM)],
        out_specs=anywhere,
        scratch_shapes=[
            pltpu.VMEM((rows, hidden), BF16),
            pltpu.VMEM((hidden, hidden), F32),
            pltpu.VMEM(weight.shape, BF16),
            pltpu.VMEM((rows, hidden), BF16),
            pltpu.VMEM(tiles.shape[1:], BF16),
            pltpu.VMEM((domains, 2, half, hidden), BF16),
            pltpu.VMEM((domains, 2, hidden, half), BF16),
            pltpu.VMEM((2, layers, 4, half // 8, half), BF16),
            pltpu.VMEM((3, half // 8, half), BF16),
            pltpu.VMEM((layers, 2, hidden, half), BF16),
            pltpu.VMEM((layers, hidden, half), BF16),
            pltpu.VMEM((2, layers, hidden, half), BF16),
            pltpu.VMEM((2, half, hidden), F32),
            pltpu.VMEM((2, half, hidden), F32),
            pltpu.VMEM((rows, hidden), BF16),
            pltpu.VMEM((hidden, rows), BF16),
            pltpu.VMEM((quarter, hidden), F32),
            pltpu.VMEM((folds, quarter // 2, hidden), F32),
            pltpu.VMEM((2, quarter // layers, hidden), F32),
            pltpu.VMEM((2, quarter // layers, hidden), F32),
            pltpu.VMEM((2, quarter, hidden), F32),
            pltpu.VMEM((2, half, hidden), BF16),
            dma((2,)), dma((3,)), dma((4,)),
            dma((domains,)), dma((domains,)),
            dma((2, layers)), dma((layers,)), dma((layers, 2)), dma((domains,)),
            dma((3,)), dma((4,)), dma((2, layers)), dma((layers,)), dma((domains,)), dma((domains,)),
            dma((2,)), dma((2,)),
            dma((layers,)), dma((2, layers)), dma((3,)), dma((3,)),
            dma((domains,)), dma((domains,)),
            dma((layers, 2)), dma((layers, 2)),
            dma((layers,)), dma((layers,)),
            dma((layers,)), dma((2, layers)),
            dma((2 * folds + 2,)), dma((2 * folds + 2,)),
            dma((2,)), dma((2,)),
        ],
        compiler_params=pltpu.CompilerParams(
            collective_id=0, has_side_effects=True, vmem_limit_bytes=63 * 1024 * 1024
        ),
        cost_estimate=pl.CostEstimate(
            flops=4 * sections * rows * rows * hidden,
            bytes_accessed=2 * sections * rows * rows,
            transcendentals=rows * hidden,
        ),
    )(features, weight, grad_out, tiles, tile_mask)
    return pl.pallas_call(
        finish_kernel,
        out_shape=out_shape,
        in_specs=anywhere,
        out_specs=anywhere,
        scratch_shapes=[
            pltpu.VMEM((rows, hidden), BF16),
            pltpu.VMEM((rows, hidden), BF16),
            pltpu.VMEM((hidden, hidden), F32),
            dma((2, 3)),
        ],
        compiler_params=pltpu.CompilerParams(vmem_limit_bytes=63 * 1024 * 1024),
        cost_estimate=pl.CostEstimate(flops=0, bytes_accessed=6 * rows * hidden * 2, transcendentals=0),
    )(*results)


def solution(mesh):
    domains, replicas = mesh.shape["dom"], mesh.shape["rep"]
    paired = replicas == 2 and domains >= 8 and domains & (domains - 1) == 0
    placed = (P("dom", None), P(), P("dom", None), P("dom", "rep", None, None), P("dom", "rep"))
    return jax.shard_map(
        kernel_shards if paired else ring_shards,
        mesh=mesh,
        in_specs=placed,
        out_specs=(P("dom", None), P("dom", None), P()),
        check_vma=False,
    )
```

```python
import functools

import jax
import jax.numpy as jnp
from jax import lax
from jax.experimental import pallas as pl
from jax.experimental.pallas import tpu as pltpu
from jax.sharding import PartitionSpec as P

MESH = pl.DeviceIdType.MESH
F32 = jnp.float32
BF16 = jnp.bfloat16


def shifted_2(block, axis, distance):
    devices = range(lax.axis_size(axis))
    route = [((i - distance) % len(devices), i) for i in devices]
    return lax.ppermute(block, axis, route)


def tile_product(tile, weight_flag, operand, transposed):
    if transposed:
        contraction = (((0,), (0,)), ((), ()))
        out_rows = tile.shape[1]
    else:
        contraction = (((1,), (0,)), ((), ()))
        out_rows = tile.shape[0]

    def compute():
        return lax.dot_general(tile, operand, contraction, preferred_element_type=jnp.float32)

    def skipped():
        return jnp.zeros((out_rows, operand.shape[1]), jnp.float32)

    return lax.cond(weight_flag > 0, compute, skipped)


def ring_shards(features, weight, grad_out, tiles, tile_mask):
    domains = lax.axis_size("dom")
    replicas = lax.axis_size("rep")
    sections = domains // replicas
    replica = lax.axis_index("rep")
    bit_count = replicas.bit_length() - 1
    rows_here = features.shape[0]
    hidden = features.shape[1]
    projected = jnp.dot(features, weight, preferred_element_type=jnp.float32).astype(jnp.bfloat16)
    current = projected
    for level in range(bit_count):
        shifted = shifted_2(current, "dom", sections << level)
        current = jnp.where(replica >> level & 1 == 1, shifted, current)
    partial_value = jnp.zeros((rows_here, hidden), jnp.float32)
    for section in range(sections):
        if section > 0:
            current = shifted_2(current, "dom", 1)
        partial_value = partial_value + tile_product(
            tiles[0, section], tile_mask[0, section], current, False
        )
    total = lax.psum(partial_value, "rep")
    gate_value = jax.nn.sigmoid(total)
    activated = (total * gate_value).astype(jnp.bfloat16)
    score_grad = (
        grad_out.astype(jnp.float32) * gate_value * (1.0 + total * (1.0 - gate_value))
    ).astype(jnp.bfloat16)
    carried = tile_product(tiles[0, sections - 1], tile_mask[0, sections - 1], score_grad, True)
    for section in range(sections - 2, -1, -1):
        carried = shifted_2(carried, "dom", -1)
        carried = carried + tile_product(tiles[0, section], tile_mask[0, section], score_grad, True)
    for level in range(bit_count):
        shifted = shifted_2(carried, "dom", -(sections << level))
        carried = jnp.where(replica >> level & 1 == 1, shifted, carried)
    node_grad = lax.psum(carried, "rep").astype(jnp.bfloat16)
    feature_grad = lax.dot_general(
        node_grad, weight, (((1,), (1,)), ((), ())), preferred_element_type=jnp.float32
    ).astype(jnp.bfloat16)
    scaling = (rows_here * domains) ** (-0.5)
    weight_term = lax.dot_general(
        features, node_grad, (((0,), (0,)), ((), ())), preferred_element_type=jnp.float32
    )
    weight_grad = lax.psum(weight_term, "dom") * scaling
    return (activated, feature_grad, weight_grad)


def layer_kernel(
    domains, scaling,
    x_hbm, w_hbm, g_hbm, tiles_hbm, mask_ref,
    act_hbm, fg_hbm, wg_hbm,
    act_ref, wg_ref, w_ref, g_ref, tiles, xs, ps, from_b, from_a, from_z, part, part_in, ax, st, ws, w_in, w_cross, w_cross_in, w_full, fg_half,
    own_sem, tile_sem, out_sem, x_recv, x_recv_p, x_send_z, x_send_a, x_send_b, x_send_p,
    y_send, y_recv, y_send_z, y_recv_z, y_send_p, y_recv_p,
    part_send, part_recv,
    p_recv_p, p_send_p, b_send, b_recv, a_send, a_recv, z_send, z_recv,
    w_send, w_recv, last_send, last_recv,
):
    layers = domains // 4
    folds = layers.bit_length() - 1
    sections = domains // 2
    half = x_hbm.shape[0] // 2
    hidden = x_hbm.shape[1]
    cut = half * 7 // 8
    main, rest = pl.ds(0, cut), pl.ds(cut, half - cut)
    d = lax.axis_index("dom")
    c = lax.axis_index("rep")
    other = 1 - c
    step_a, step_b = 1 + c, 2 - c
    z = d // 4
    a = (d // step_a) % 2
    b = (d // step_b) % 2

    def block_at(z_, b_, a_):
        return z_ * 4 + b_ * step_b + a_ * step_a

    dev_a, dev_b = block_at(z, b, 1 - a), block_at(z, 1 - b, a)
    dev_fold = [block_at(z + (1 << f) * (1 - 2 * ((z // (1 << f)) % 2)), b, a) for f in range(folds)]
    far = dev_fold[1:]

    def copy_to(src, dst, send, recv, dom, rep):
        return pltpu.make_async_remote_copy(
            src_ref=src, dst_ref=dst, send_sem=send, recv_sem=recv,
            device_id=(dom, rep), device_id_type=MESH,
        )

    own_copies = [
        pltpu.make_async_copy(x_hbm.at[pl.ds(h * half, half)], xs.at[d, h], own_sem.at[h])
        for h in range(2)
    ]
    tile_copies = [
        pltpu.make_async_copy(w_hbm, w_ref, tile_sem.at[0]),
        pltpu.make_async_copy(g_hbm, g_ref, tile_sem.at[1]),
        pltpu.make_async_copy(tiles_hbm.at[0], tiles, tile_sem.at[2]),
    ]
    for copy in own_copies + tile_copies:
        copy.start()

    barrier = pltpu.get_barrier_semaphore()
    for dom, rep in [(dev_a, c), (dev_b, c), (d, other)] + [(f, c) for f in far]:
        pl.semaphore_signal(barrier, inc=1, device_id=(dom, rep), device_id_type=MESH)

    @pl.when(z > 0)
    def _():
        pl.semaphore_signal(barrier, inc=1, device_id=(d - 4, c), device_id_type=MESH)

    @pl.when(z < layers - 1)
    def _():
        pl.semaphore_signal(barrier, inc=1, device_id=(d + 4, c), device_id_type=MESH)

    ends = jnp.where(z > 0, 1, 0) + jnp.where(z < layers - 1, 1, 0)
    pl.semaphore_wait(barrier, 3 + len(far) + ends)

    def owner(j):
        return ((d - j + domains) % domains) // sections

    def x_copy_z(j, z_, up):
        return copy_to(xs.at[j, c, main], xs.at[j, c, main], x_send_z.at[up, z_], x_recv.at[j], d - 4 + 8 * up, c)

    def x_copy_a(j, z_):
        return copy_to(xs.at[j, c, main], xs.at[j, c, main], x_send_a.at[z_], x_recv.at[j], dev_a, c)

    def x_copy_b(j, z_, a_):
        return copy_to(xs.at[j, c, main], xs.at[j, c, main], x_send_b.at[z_, a_], x_recv.at[j], dev_b, c)

    def x_copy_p(j):
        return copy_to(xs.at[j, c, main], xs.at[j, c, main], x_send_p.at[j], x_recv_p.at[j], d, other)

    def y_copy_a():
        return copy_to(
            xs.at[d, c, rest], xs.at[d, c, rest], y_send.at[2], y_recv.at[d % 4], dev_a, c
        )

    def y_copy_b(a_):
        j = block_at(z, b, a_)
        return copy_to(xs.at[j, c, rest], xs.at[j, c, rest], y_send.at[a_], y_recv.at[j % 4], dev_b, c)

    def y_slab(z_, up):
        slab = xs.at[pl.ds(z_ * 4, 4), c, rest]
        return copy_to(slab, slab, y_send_z.at[up, z_], y_recv_z.at[z_], d - 4 + 8 * up, c)

    def y_copy_p(j):
        return copy_to(
            xs.at[j, c, rest], xs.at[j, c, rest], y_send_p.at[j], y_recv_p.at[j], d, other
        )

    def y_wait(b_, a_):
        j = block_at(z, b_, a_)
        copy_to(
            xs.at[j, c, rest], xs.at[j, c, rest], y_send.at[2], y_recv.at[j % 4], dev_a, c
        ).wait_recv()

    def y_to_partner(z_):
        def one(q, carry):
            j = z_ * 4 + q

            @pl.when(jnp.logical_and(owner(j) != c, j != d))
            def _():
                y_copy_p(j).start()

            return carry

        lax.fori_loop(0, 4, one, 0)

    def y_layer_done():
        y_wait(1 - b, a)
        y_wait(1 - b, 1 - a)

        @pl.when(z > 0)
        def _():
            y_slab(z, 0).start()

        @pl.when(z < layers - 1)
        def _():
            y_slab(z, 1).start()

        y_to_partner(z)

    def y_from_layer(n):
        z_ = layer_of(n)

        @pl.when(in_range(z_))
        def _():
            y_slab(z_, 0).wait_recv()

            @pl.when(jnp.logical_and(z_ < z, z < layers - 1))
            def _():
                y_slab(z_, 1).start()

            @pl.when(jnp.logical_and(z_ > z, z > 0))
            def _():
                y_slab(z_, 0).start()

            y_to_partner(z_)

    def x_arrive(j):
        copy_to(xs.at[j, c, main], xs.at[j, c, main], x_send_p.at[j], x_recv.at[j], d, other).wait_recv()

        @pl.when(owner(j) != c)
        def _():
            x_copy_p(j).start()

    for copy in own_copies:
        copy.wait()

    @pl.when(z > 0)
    def _():
        x_copy_z(d, z, 0).start()

    @pl.when(z < layers - 1)
    def _():
        x_copy_z(d, z, 1).start()

    x_copy_b(d, z, a).start()
    x_copy_a(d, z).start()
    y_copy_b(a).start()
    y_copy_a().start()

    def layer_of(n):
        return z + ((n + 1) // 2) * (2 * ((n + 1) % 2) - 1)

    def in_range(z_):
        return jnp.logical_and(z_ >= 0, z_ < layers)

    def from_layer(n):
        z_ = layer_of(n)

        @pl.when(in_range(z_))
        def _():
            j = block_at(z_, b, a)
            x_arrive(j)

            @pl.when(jnp.logical_and(z_ < z, z < layers - 1))
            def _():
                x_copy_z(j, z_, 1).start()

            @pl.when(jnp.logical_and(z_ > z, z > 0))
            def _():
                x_copy_z(j, z_, 0).start()

            x_copy_b(j, z_, a).start()
            x_copy_a(j, z_).start()

    def from_a_side(n):
        z_ = layer_of(n)

        @pl.when(in_range(z_))
        def _():
            j = block_at(z_, b, 1 - a)
            x_arrive(j)
            x_copy_b(j, z_, 1 - a).start()

    def from_b_side(n):
        z_ = layer_of(n)

        @pl.when(in_range(z_))
        def _():
            x_arrive(block_at(z_, 1 - b, a))
            x_arrive(block_at(z_, 1 - b, 1 - a))

    def flag(o):
        return jnp.where(mask_ref[0, o] > 0, 1.0, 0.0)

    def product(j):
        o = (d - j + domains) % domains - c * sections
        m = flag(o).astype(BF16)
        x_top, x_low = xs[j, 0] * m, xs[j, 1] * m
        for r in range(2):
            rows = pl.ds(r * half, half)
            part[r] += jnp.dot(
                tiles[o, rows, pl.ds(0, half)], x_top, preferred_element_type=F32
            ) + jnp.dot(tiles[o, rows, pl.ds(half, half)], x_low, preferred_element_type=F32)

    def products(n):
        z_ = layer_of(n)

        def one(q, carry):
            j = z_ * 4 + q

            @pl.when(owner(j) == c)
            def _():
                @pl.when(j != d)
                def _():
                    for send, recv, rows in ((x_send_p, x_recv_p, main), (y_send_p, y_recv_p, rest)):
                        copy_to(
                            xs.at[j, other, rows], xs.at[j, other, rows], send.at[j], recv.at[j], d, other
                        ).wait_recv()

                product(j)

            return carry

        @pl.when(in_range(z_))
        def _():
            lax.fori_loop(0, 4, one, 0)

    visits = 2 * layers - 1
    for copy in tile_copies:
        copy.wait()
    for r in range(2):
        part[r] = jnp.zeros((half, hidden), F32)

    y_wait(b, 1 - a)
    y_copy_b(1 - a).start()

    def gather_step(n, carry):
        for lag, step in ((1, from_a_side), (0, from_layer), (2, from_b_side)):
            at = n - 2 * lag

            @pl.when(jnp.logical_and(at >= (1 if lag == 0 else 0), at < visits))
            def _():
                step(at)

        @pl.when(n == 2)
        def _():
            y_layer_done()

        @pl.when(jnp.logical_and(n >= 4, n - 3 < visits))
        def _():
            y_from_layer(n - 3)

        @pl.when(n >= 5)
        def _():
            products(n - 5)

        return carry

    lax.fori_loop(1, visits + 5, gather_step, 0)

    def part_copy(r):
        return copy_to(part.at[r], part_in.at[r], part_send.at[r], part_recv.at[r], d, other)

    for r in range(2):
        part_copy(r).start()

    for r in range(2):
        part_copy(r).wait_recv()
        rows = pl.ds(r * half, half)
        ax_here = (part[r] + part_in[r]).astype(BF16)
        ax[rows, :] = ax_here
        total = jnp.dot(ax_here, w_ref[...], preferred_element_type=F32)
        gate = jax.nn.sigmoid(total)
        act_ref[rows, :] = (total * gate).astype(BF16)
        score = g_ref[rows, :].astype(F32) * gate * (1.0 + total * (1.0 - gate))
        st[:, rows] = jnp.transpose(score).astype(BF16)
    act_out = pltpu.make_async_copy(act_ref, act_hbm, out_sem.at[0])
    act_out.start()

    quarter = hidden // 2
    sizes, bases = [quarter], [0]
    for f in range(folds):
        sizes.append(sizes[-1] // 2)
        bases.append(bases[-1] + ((z // (1 << f)) % 2) * sizes[-1])

    def fold_copy(f):
        there = bases[f] + (1 - (z // (1 << f)) % 2) * sizes[f + 1]
        rows = pl.ds(pl.multiple_of(there, sizes[f + 1]), sizes[f + 1])
        return copy_to(
            ws.at[rows], w_in.at[f, pl.ds(0, sizes[f + 1])], w_send.at[f], w_recv.at[f], dev_fold[f], c
        )

    def cross_copy(i):
        return copy_to(
            w_cross.at[i], w_cross_in.at[i], w_send.at[folds + i], w_recv.at[folds + i],
            (dev_a, dev_b)[i], c,
        )

    def unfold_copy(f):
        rows = pl.ds(pl.multiple_of(bases[f + 1], sizes[f + 1]), sizes[f + 1])
        return copy_to(
            w_full.at[c, rows], w_full.at[c, rows], w_send.at[folds + 2 + f], w_recv.at[folds + 2 + f],
            dev_fold[f], c,
        )

    def weight_step(s):
        if s < folds:
            fold_copy(s).wait_recv()
            rows = pl.ds(pl.multiple_of(bases[s + 1], sizes[s + 1]), sizes[s + 1])
            ws[rows, :] += w_in[s, pl.ds(0, sizes[s + 1])]
            if s + 1 < folds:
                fold_copy(s + 1).start()
            else:
                w_cross[0] = ws[rows, :]
                cross_copy(0).start()
        elif s < folds + 2:
            i = s - folds
            cross_copy(i).wait_recv()
            if i == 0:
                w_cross[1] = w_cross[0] + w_cross_in[0]
                cross_copy(1).start()
            else:
                rows = pl.ds(pl.multiple_of(bases[folds], sizes[folds]), sizes[folds])
                w_full[c, rows] = w_cross[1] + w_cross_in[1]
                unfold_copy(folds - 1).start()
        else:
            f = 2 * folds + 1 - s
            unfold_copy(f).wait_recv()
            if f > 0:
                unfold_copy(f - 1).start()

    weight_steps = 2 * folds + 2

    ws[...] = jnp.dot(
        st[pl.ds(pl.multiple_of(c * quarter, quarter), quarter), :], ax[...],
        preferred_element_type=F32,
    )
    fold_copy(0).start()

    near = jnp.minimum(z, layers - 1 - z)
    reach = layers - 1 - near
    long_side = jnp.where(z == near, 1, -1)

    def target_layer(t):
        u = t - (reach - near)
        return jnp.where(
            u < 0, z + long_side * (reach - t), z + (1 - 2 * (u % 2)) * (near - u // 2)
        )

    def piece(k):
        z_ = target_layer(k // 4)
        q = k % 4
        b_ = jnp.where(q < 2, 1 - b, b)
        a_ = jnp.where(q % 2 == 0, 1 - a, a)
        return z_, b_, a_, block_at(z_, b_, a_)

    def p_copy(j):
        return copy_to(ps.at[j, other], ps.at[j, other], p_send_p.at[j], p_recv_p.at[j], d, other)

    def b_copy(z_, a_):
        return copy_to(
            ps.at[block_at(z_, 1 - b, a_), c], from_b.at[z_, a_], b_send.at[z_, a_], b_recv.at[z_, a_],
            dev_b, c,
        )

    def a_copy(z_):
        return copy_to(
            ps.at[block_at(z_, b, 1 - a), c], from_a.at[z_], a_send.at[z_], a_recv.at[z_], dev_a, c
        )

    def z_copy(z_, up):
        return copy_to(
            ps.at[block_at(z_, b, a), c], from_z.at[up, z_], z_send.at[z_], z_recv.at[up, z_],
            d - 4 + 8 * up, c,
        )

    def backward(k):
        z_, b_, a_, j = piece(k)

        @pl.when(owner(j) == c)
        def _():
            o = (d - j + domains) % domains - c * sections
            m = flag(o)
            for h in range(2):
                ps[j, h] = (
                    jnp.dot(st[...], tiles[o, :, pl.ds(h * half, half)], preferred_element_type=F32) * m
                ).astype(BF16)
            p_copy(j).start()

            @pl.when(jnp.logical_and(b_ != b, k < 8))
            def _():
                b_copy(z_, a_).start()

    def relay_partner(k):
        z_, b_, a_, j = piece(k)

        @pl.when(owner(j) != c)
        def _():
            copy_to(ps.at[j, c], ps.at[j, c], p_send_p.at[j], p_recv_p.at[j], d, other).wait_recv()

            @pl.when(jnp.logical_and(b_ != b, k < 8))
            def _():
                b_copy(z_, a_).start()

    def backward_step(k, carry):
        @pl.when(k < domains)
        def _():
            backward(k)

        @pl.when(k >= 4)
        def _():
            relay_partner(k - 4)

        return carry

    lax.fori_loop(0, domains + 4, backward_step, 0)

    def stage_a(t):
        z_ = target_layer(t)
        b_copy(z_, 1 - a).wait_recv()
        j = block_at(z_, b, 1 - a)
        ps[j, c] = (ps[j, c].astype(F32) + from_b[z_, 1 - a].astype(F32)).astype(BF16)
        a_copy(z_).start()

    def stage_z(t):
        z_ = target_layer(t)
        b_copy(z_, a).wait_recv()
        a_copy(z_).wait_recv()
        j = block_at(z_, b, a)

        def mine():
            return ps[j, c].astype(F32) + from_b[z_, a].astype(F32) + from_a[z_].astype(F32)

        @pl.when(z_ == z)
        def _():
            part[0] = mine()

        @pl.when(jnp.logical_and(z_ > z, z == 0))
        def _():
            ps[j, c] = mine().astype(BF16)
            z_copy(z_, 1).start()

        @pl.when(jnp.logical_and(z_ < z, z == layers - 1))
        def _():
            ps[j, c] = mine().astype(BF16)
            z_copy(z_, 0).start()

    def stage_relay(t):
        z_ = target_layer(t)
        j = block_at(z_, b, a)

        def pass_on(up):
            z_copy(z_, up).wait_recv()
            ps[j, c] = (
                ps[j, c].astype(F32) + from_b[z_, a].astype(F32) + from_a[z_].astype(F32)
                + from_z[up, z_].astype(F32)
            ).astype(BF16)
            z_copy(z_, up).start()

        @pl.when(jnp.logical_and(z_ > z, z > 0))
        def _():
            pass_on(1)

        @pl.when(jnp.logical_and(z_ < z, z < layers - 1))
        def _():
            pass_on(0)

    for r in range(2):
        part_copy(r).wait_send()

    stages = max(layers + 1, (weight_steps + 1) // 2)
    for t in range(stages):
        if t < layers:
            stage_a(t)
        if 2 * t < weight_steps:
            weight_step(2 * t)
        if t + 2 < layers:
            b_copy(target_layer(t + 2), 1 - a).start()
            b_copy(target_layer(t + 2), a).start()
        if 1 <= t <= layers:
            stage_z(t - 1)
        if t == 2:
            stage_relay(0)
        if 2 <= t <= layers:
            stage_relay(t - 1)
        if 2 * t + 1 < weight_steps:
            weight_step(2 * t + 1)

    w_last = copy_to(w_full.at[c], w_full.at[c], last_send.at[0], last_recv.at[0], d, other)
    w_last.start()

    @pl.when(z > 0)
    def _():
        z_copy(z, 1).wait_recv()
        part[0] += from_z[1, z].astype(F32)

    @pl.when(z < layers - 1)
    def _():
        z_copy(z, 0).wait_recv()
        part[0] += from_z[0, z].astype(F32)

    node = jnp.transpose(part[0]).astype(BF16)
    fg_half[c] = lax.dot_general(
        node, w_ref[...], (((1,), (1,)), ((), ())), preferred_element_type=F32
    ).astype(BF16)
    f_last = copy_to(fg_half.at[c], fg_half.at[c], last_send.at[1], last_recv.at[1], d, other)
    f_last.start()

    def fg_out(h):
        return pltpu.make_async_copy(
            fg_half.at[h], fg_hbm.at[pl.ds(pl.multiple_of(h * half, half), half)], out_sem.at[1 + h]
        )

    fg_out(c).start()

    copy_to(w_full.at[other], w_full.at[other], last_send.at[0], last_recv.at[0], d, other).wait_recv()
    for h in range(2):
        wg_ref[:, pl.ds(h * quarter, quarter)] = jnp.transpose(w_full[h]) * scaling
    wg_out = pltpu.make_async_copy(wg_ref, wg_hbm, out_sem.at[3])
    wg_out.start()

    def drain_p(j, carry):
        @pl.when(jnp.logical_and(owner(j) != c, j != d))
        def _():
            x_copy_p(j).wait_send()
            y_copy_p(j).wait_send()

        @pl.when(owner(j) == c)
        def _():
            p_copy(j).wait_send()

        return carry

    lax.fori_loop(0, domains, drain_p, 0)

    def drain(z_, carry):
        @pl.when(jnp.logical_and(z_ <= z, z < layers - 1))
        def _():
            x_copy_z(block_at(z_, b, a), z_, 1).wait_send()
            y_slab(z_, 1).wait_send()

        @pl.when(jnp.logical_and(z_ >= z, z > 0))
        def _():
            x_copy_z(block_at(z_, b, a), z_, 0).wait_send()
            y_slab(z_, 0).wait_send()

        x_copy_a(block_at(z_, b, a), z_).wait_send()
        a_copy(z_).wait_send()
        for a_ in range(2):
            x_copy_b(block_at(z_, b, a_), z_, a_).wait_send()
            b_copy(z_, a_).wait_send()

        @pl.when(z_ > z)
        def _():
            z_copy(z_, 1).wait_send()

        @pl.when(z_ < z)
        def _():
            z_copy(z_, 0).wait_send()

        return carry

    lax.fori_loop(0, layers, drain, 0)
    y_copy_a().wait_send()
    for a_ in range(2):
        y_copy_b(a_).wait_send()
    for f in range(folds):
        fold_copy(f).wait_send()
        unfold_copy(f).wait_send()
    for i in range(2):
        cross_copy(i).wait_send()
    copy_to(fg_half.at[other], fg_half.at[other], last_send.at[1], last_recv.at[1], d, other).wait_recv()
    fg_out(other).start()
    w_last.wait_send()
    f_last.wait_send()
    act_out.wait()
    wg_out.wait()
    for h in range(2):
        fg_out(h).wait()


def finish_kernel(act, fg, wg, act_out, fg_out, wg_out, act_v, fg_v, wg_v, sem):
    pairs = ((act, act_v, act_out), (fg, fg_v, fg_out), (wg, wg_v, wg_out))
    inward = [pltpu.make_async_copy(p[0], p[1], sem.at[0, i]) for i, p in enumerate(pairs)]
    outward = [pltpu.make_async_copy(p[1], p[2], sem.at[1, i]) for i, p in enumerate(pairs)]
    for copy in inward:
        copy.start()
    for first, second in zip(inward, outward):
        first.wait()
        second.start()
    for copy in outward:
        copy.wait()


def kernel_shards(features, weight, grad_out, tiles, tile_mask):
    domains = lax.axis_size("dom")
    layers = domains // 4
    folds = layers.bit_length() - 1
    sections = tiles.shape[1]
    rows, hidden = features.shape
    half, quarter = rows // 2, hidden // 2
    dma = pltpu.SemaphoreType.DMA
    out_shape = (
        jax.ShapeDtypeStruct((rows, hidden), BF16),
        jax.ShapeDtypeStruct((rows, hidden), BF16),
        jax.ShapeDtypeStruct((hidden, hidden), F32),
    )
    anywhere = [pl.BlockSpec(memory_space=pl.ANY)] * 3
    results = pl.pallas_call(
        functools.partial(layer_kernel, domains, float((rows * domains) ** (-0.5))),
        out_shape=out_shape,
        in_specs=[pl.BlockSpec(memory_space=pltpu.HBM)] * 4 + [pl.BlockSpec(memory_space=pltpu.SMEM)],
        out_specs=anywhere,
        scratch_shapes=[
            pltpu.VMEM((rows, hidden), BF16),
            pltpu.VMEM((hidden, hidden), F32),
            pltpu.VMEM(weight.shape, BF16),
            pltpu.VMEM((rows, hidden), BF16),
            pltpu.VMEM(tiles.shape[1:], BF16),
            pltpu.VMEM((domains, 2, half, hidden), BF16),
            pltpu.VMEM((domains, 2, hidden, half), BF16),
            pltpu.VMEM((layers, 2, hidden, half), BF16),
            pltpu.VMEM((layers, hidden, half), BF16),
            pltpu.VMEM((2, layers, hidden, half), BF16),
            pltpu.VMEM((2, half, hidden), F32),
            pltpu.VMEM((2, half, hidden), F32),
            pltpu.VMEM((rows, hidden), BF16),
            pltpu.VMEM((hidden, rows), BF16),
            pltpu.VMEM((quarter, hidden), F32),
            pltpu.VMEM((folds, quarter // 2, hidden), F32),
            pltpu.VMEM((2, quarter // layers, hidden), F32),
            pltpu.VMEM((2, quarter // layers, hidden), F32),
            pltpu.VMEM((2, quarter, hidden), F32),
            pltpu.VMEM((2, half, hidden), BF16),
            dma((2,)), dma((3,)), dma((4,)),
            dma((domains,)), dma((domains,)),
            dma((2, layers)), dma((layers,)), dma((layers, 2)), dma((domains,)),
            dma((3,)), dma((4,)), dma((2, layers)), dma((layers,)), dma((domains,)), dma((domains,)),
            dma((2,)), dma((2,)),
            dma((domains,)), dma((domains,)),
            dma((layers, 2)), dma((layers, 2)),
            dma((layers,)), dma((layers,)),
            dma((layers,)), dma((2, layers)),
            dma((2 * folds + 2,)), dma((2 * folds + 2,)),
            dma((2,)), dma((2,)),
        ],
        compiler_params=pltpu.CompilerParams(
            collective_id=0, has_side_effects=True, vmem_limit_bytes=63 * 1024 * 1024
        ),
        cost_estimate=pl.CostEstimate(
            flops=4 * sections * rows * rows * hidden,
            bytes_accessed=2 * sections * rows * rows,
            transcendentals=rows * hidden,
        ),
    )(features, weight, grad_out, tiles, tile_mask)
    return pl.pallas_call(
        finish_kernel,
        out_shape=out_shape,
        in_specs=anywhere,
        out_specs=anywhere,
        scratch_shapes=[
            pltpu.VMEM((rows, hidden), BF16),
            pltpu.VMEM((rows, hidden), BF16),
            pltpu.VMEM((hidden, hidden), F32),
            dma((2, 3)),
        ],
        compiler_params=pltpu.CompilerParams(vmem_limit_bytes=63 * 1024 * 1024),
        cost_estimate=pl.CostEstimate(flops=0, bytes_accessed=6 * rows * hidden * 2, transcendentals=0),
    )(*results)


def solution(mesh):
    domains, replicas = mesh.shape["dom"], mesh.shape["rep"]
    paired = replicas == 2 and domains >= 8 and domains & (domains - 1) == 0
    placed = (P("dom", None), P(), P("dom", None), P("dom", "rep", None, None), P("dom", "rep"))
    return jax.shard_map(
        kernel_shards if paired else ring_shards,
        mesh=mesh,
        in_specs=placed,
        out_specs=(P("dom", None), P("dom", None), P()),
        check_vma=False,
    )
```

```python
import functools

import jax
import jax.numpy as jnp
from jax import lax
from jax.experimental import pallas as pl
from jax.experimental.pallas import tpu as pltpu
from jax.sharding import PartitionSpec as P

MESH = pl.DeviceIdType.MESH
F32 = jnp.float32
BF16 = jnp.bfloat16


def shifted_2(block, axis, distance):
    devices = range(lax.axis_size(axis))
    route = [((i - distance) % len(devices), i) for i in devices]
    return lax.ppermute(block, axis, route)


def tile_product(tile, weight_flag, operand, transposed):
    if transposed:
        contraction = (((0,), (0,)), ((), ()))
        out_rows = tile.shape[1]
    else:
        contraction = (((1,), (0,)), ((), ()))
        out_rows = tile.shape[0]

    def compute():
        return lax.dot_general(tile, operand, contraction, preferred_element_type=jnp.float32)

    def skipped():
        return jnp.zeros((out_rows, operand.shape[1]), jnp.float32)

    return lax.cond(weight_flag > 0, compute, skipped)


def ring_shards(features, weight, grad_out, tiles, tile_mask):
    domains = lax.axis_size("dom")
    replicas = lax.axis_size("rep")
    sections = domains // replicas
    replica = lax.axis_index("rep")
    bit_count = replicas.bit_length() - 1
    rows_here = features.shape[0]
    hidden = features.shape[1]
    projected = jnp.dot(features, weight, preferred_element_type=jnp.float32).astype(jnp.bfloat16)
    current = projected
    for level in range(bit_count):
        shifted = shifted_2(current, "dom", sections << level)
        current = jnp.where(replica >> level & 1 == 1, shifted, current)
    partial_value = jnp.zeros((rows_here, hidden), jnp.float32)
    for section in range(sections):
        if section > 0:
            current = shifted_2(current, "dom", 1)
        partial_value = partial_value + tile_product(
            tiles[0, section], tile_mask[0, section], current, False
        )
    total = lax.psum(partial_value, "rep")
    gate_value = jax.nn.sigmoid(total)
    activated = (total * gate_value).astype(jnp.bfloat16)
    score_grad = (
        grad_out.astype(jnp.float32) * gate_value * (1.0 + total * (1.0 - gate_value))
    ).astype(jnp.bfloat16)
    carried = tile_product(tiles[0, sections - 1], tile_mask[0, sections - 1], score_grad, True)
    for section in range(sections - 2, -1, -1):
        carried = shifted_2(carried, "dom", -1)
        carried = carried + tile_product(tiles[0, section], tile_mask[0, section], score_grad, True)
    for level in range(bit_count):
        shifted = shifted_2(carried, "dom", -(sections << level))
        carried = jnp.where(replica >> level & 1 == 1, shifted, carried)
    node_grad = lax.psum(carried, "rep").astype(jnp.bfloat16)
    feature_grad = lax.dot_general(
        node_grad, weight, (((1,), (1,)), ((), ())), preferred_element_type=jnp.float32
    ).astype(jnp.bfloat16)
    scaling = (rows_here * domains) ** (-0.5)
    weight_term = lax.dot_general(
        features, node_grad, (((0,), (0,)), ((), ())), preferred_element_type=jnp.float32
    )
    weight_grad = lax.psum(weight_term, "dom") * scaling
    return (activated, feature_grad, weight_grad)


def layer_kernel(
    domains, scaling,
    x_hbm, w_hbm, g_hbm, tiles_hbm, mask_ref,
    act_hbm, fg_hbm, wg_hbm,
    act_ref, wg_ref, w_ref, g_ref, tiles, xs, ps, from_b, from_a, from_z, part, part_in, ax, st, ws, w_in, w_cross, w_cross_in, w_full, fg_half,
    own_sem, tile_sem, out_sem, x_recv, x_recv_p, x_send_z, x_send_a, x_send_b, x_send_p,
    y_send, y_recv, y_send_z, y_recv_z, y_send_p, y_recv_p,
    part_send, part_recv,
    p_recv_p, p_send_p, b_send, b_recv, a_send, a_recv, z_send, z_recv,
    w_send, w_recv, last_send, last_recv,
):
    layers = domains // 4
    folds = layers.bit_length() - 1
    sections = domains // 2
    half = x_hbm.shape[0] // 2
    hidden = x_hbm.shape[1]
    cut = half * 7 // 8
    main, rest = pl.ds(0, cut), pl.ds(cut, half - cut)
    d = lax.axis_index("dom")
    c = lax.axis_index("rep")
    other = 1 - c
    step_a, step_b = 1 + c, 2 - c
    z = d // 4
    a = (d // step_a) % 2
    b = (d // step_b) % 2

    def block_at(z_, b_, a_):
        return z_ * 4 + b_ * step_b + a_ * step_a

    dev_a, dev_b = block_at(z, b, 1 - a), block_at(z, 1 - b, a)
    dev_fold = [block_at(z + (1 << f) * (1 - 2 * ((z // (1 << f)) % 2)), b, a) for f in range(folds)]
    far = dev_fold[1:]

    def copy_to(src, dst, send, recv, dom, rep):
        return pltpu.make_async_remote_copy(
            src_ref=src, dst_ref=dst, send_sem=send, recv_sem=recv,
            device_id=(dom, rep), device_id_type=MESH,
        )

    own_copies = [
        pltpu.make_async_copy(x_hbm.at[pl.ds(h * half, half)], xs.at[d, h], own_sem.at[h])
        for h in range(2)
    ]
    tile_copies = [
        pltpu.make_async_copy(w_hbm, w_ref, tile_sem.at[0]),
        pltpu.make_async_copy(g_hbm, g_ref, tile_sem.at[1]),
        pltpu.make_async_copy(tiles_hbm.at[0], tiles, tile_sem.at[2]),
    ]
    for copy in own_copies + tile_copies:
        copy.start()

    barrier = pltpu.get_barrier_semaphore()
    for dom, rep in [(dev_a, c), (dev_b, c), (d, other)] + [(f, c) for f in far]:
        pl.semaphore_signal(barrier, inc=1, device_id=(dom, rep), device_id_type=MESH)

    @pl.when(z > 0)
    def _():
        pl.semaphore_signal(barrier, inc=1, device_id=(d - 4, c), device_id_type=MESH)

    @pl.when(z < layers - 1)
    def _():
        pl.semaphore_signal(barrier, inc=1, device_id=(d + 4, c), device_id_type=MESH)

    ends = jnp.where(z > 0, 1, 0) + jnp.where(z < layers - 1, 1, 0)
    pl.semaphore_wait(barrier, 3 + len(far) + ends)

    def owner(j):
        return ((d - j + domains) % domains) // sections

    def x_copy_z(j, z_, up):
        return copy_to(xs.at[j, c, main], xs.at[j, c, main], x_send_z.at[up, z_], x_recv.at[j], d - 4 + 8 * up, c)

    def x_copy_a(j, z_):
        return copy_to(xs.at[j, c, main], xs.at[j, c, main], x_send_a.at[z_], x_recv.at[j], dev_a, c)

    def x_copy_b(j, z_, a_):
        return copy_to(xs.at[j, c, main], xs.at[j, c, main], x_send_b.at[z_, a_], x_recv.at[j], dev_b, c)

    def x_copy_p(j):
        return copy_to(xs.at[j, c, main], xs.at[j, c, main], x_send_p.at[j], x_recv_p.at[j], d, other)

    def y_copy_a():
        return copy_to(
            xs.at[d, c, rest], xs.at[d, c, rest], y_send.at[2], y_recv.at[d % 4], dev_a, c
        )

    def y_copy_b(a_):
        j = block_at(z, b, a_)
        return copy_to(xs.at[j, c, rest], xs.at[j, c, rest], y_send.at[a_], y_recv.at[j % 4], dev_b, c)

    def y_slab(z_, up):
        slab = xs.at[pl.ds(z_ * 4, 4), c, rest]
        return copy_to(slab, slab, y_send_z.at[up, z_], y_recv_z.at[z_], d - 4 + 8 * up, c)

    def y_copy_p(j):
        return copy_to(
            xs.at[j, c, rest], xs.at[j, c, rest], y_send_p.at[j], y_recv_p.at[j], d, other
        )

    def y_wait(b_, a_):
        j = block_at(z, b_, a_)
        copy_to(
            xs.at[j, c, rest], xs.at[j, c, rest], y_send.at[2], y_recv.at[j % 4], dev_a, c
        ).wait_recv()

    def y_to_partner(z_):
        def one(q, carry):
            j = z_ * 4 + q

            @pl.when(jnp.logical_and(owner(j) != c, j != d))
            def _():
                y_copy_p(j).start()

            return carry

        lax.fori_loop(0, 4, one, 0)

    def y_layer_done():
        y_wait(1 - b, a)
        y_wait(1 - b, 1 - a)

        @pl.when(z > 0)
        def _():
            y_slab(z, 0).start()

        @pl.when(z < layers - 1)
        def _():
            y_slab(z, 1).start()

        y_to_partner(z)

    def y_from_layer(n):
        z_ = layer_of(n)

        @pl.when(in_range(z_))
        def _():
            y_slab(z_, 0).wait_recv()

            @pl.when(jnp.logical_and(z_ < z, z < layers - 1))
            def _():
                y_slab(z_, 1).start()

            @pl.when(jnp.logical_and(z_ > z, z > 0))
            def _():
                y_slab(z_, 0).start()

            y_to_partner(z_)

    def x_arrive(j):
        copy_to(xs.at[j, c, main], xs.at[j, c, main], x_send_p.at[j], x_recv.at[j], d, other).wait_recv()

        @pl.when(owner(j) != c)
        def _():
            x_copy_p(j).start()

    for copy in own_copies:
        copy.wait()

    @pl.when(z > 0)
    def _():
        x_copy_z(d, z, 0).start()

    @pl.when(z < layers - 1)
    def _():
        x_copy_z(d, z, 1).start()

    x_copy_b(d, z, a).start()
    x_copy_a(d, z).start()
    y_copy_b(a).start()
    y_copy_a().start()

    def layer_of(n):
        return z + ((n + 1) // 2) * (2 * ((n + 1) % 2) - 1)

    def in_range(z_):
        return jnp.logical_and(z_ >= 0, z_ < layers)

    def from_layer(n):
        z_ = layer_of(n)

        @pl.when(in_range(z_))
        def _():
            j = block_at(z_, b, a)
            x_arrive(j)

            @pl.when(jnp.logical_and(z_ < z, z < layers - 1))
            def _():
                x_copy_z(j, z_, 1).start()

            @pl.when(jnp.logical_and(z_ > z, z > 0))
            def _():
                x_copy_z(j, z_, 0).start()

            x_copy_b(j, z_, a).start()
            x_copy_a(j, z_).start()

    def from_a_side(n):
        z_ = layer_of(n)

        @pl.when(in_range(z_))
        def _():
            j = block_at(z_, b, 1 - a)
            x_arrive(j)
            x_copy_b(j, z_, 1 - a).start()

    def from_b_side(n):
        z_ = layer_of(n)

        @pl.when(in_range(z_))
        def _():
            x_arrive(block_at(z_, 1 - b, a))
            x_arrive(block_at(z_, 1 - b, 1 - a))

    def flag(o):
        return jnp.where(mask_ref[0, o] > 0, 1.0, 0.0)

    def product(j):
        o = (d - j + domains) % domains - c * sections
        m = flag(o).astype(BF16)
        x_top, x_low = xs[j, 0] * m, xs[j, 1] * m
        for r in range(2):
            rows = pl.ds(r * half, half)
            part[r] += jnp.dot(
                tiles[o, rows, pl.ds(0, half)], x_top, preferred_element_type=F32
            ) + jnp.dot(tiles[o, rows, pl.ds(half, half)], x_low, preferred_element_type=F32)

    def products(n):
        z_ = layer_of(n)

        def one(q, carry):
            j = z_ * 4 + q

            @pl.when(owner(j) == c)
            def _():
                @pl.when(j != d)
                def _():
                    for send, recv, rows in ((x_send_p, x_recv_p, main), (y_send_p, y_recv_p, rest)):
                        copy_to(
                            xs.at[j, other, rows], xs.at[j, other, rows], send.at[j], recv.at[j], d, other
                        ).wait_recv()

                product(j)

            return carry

        @pl.when(in_range(z_))
        def _():
            lax.fori_loop(0, 4, one, 0)

    visits = 2 * layers - 1
    for copy in tile_copies:
        copy.wait()
    for r in range(2):
        part[r] = jnp.zeros((half, hidden), F32)

    y_wait(b, 1 - a)
    y_copy_b(1 - a).start()

    def gather_step(n, carry):
        for lag, step in ((1, from_a_side), (0, from_layer), (2, from_b_side)):
            at = n - 2 * lag

            @pl.when(jnp.logical_and(at >= (1 if lag == 0 else 0), at < visits))
            def _():
                step(at)

        @pl.when(n == 2)
        def _():
            y_layer_done()

        @pl.when(jnp.logical_and(n >= 4, n - 3 < visits))
        def _():
            y_from_layer(n - 3)

        @pl.when(n >= 5)
        def _():
            products(n - 5)

        return carry

    lax.fori_loop(1, visits + 5, gather_step, 0)

    def part_copy(r):
        return copy_to(part.at[r], part_in.at[r], part_send.at[r], part_recv.at[r], d, other)

    for r in range(2):
        part_copy(r).start()

    for r in range(2):
        part_copy(r).wait_recv()
        rows = pl.ds(r * half, half)
        ax_here = (part[r] + part_in[r]).astype(BF16)
        ax[rows, :] = ax_here
        total = jnp.dot(ax_here, w_ref[...], preferred_element_type=F32)
        gate = jax.nn.sigmoid(total)
        act_ref[rows, :] = (total * gate).astype(BF16)
        score = g_ref[rows, :].astype(F32) * gate * (1.0 + total * (1.0 - gate))
        st[:, rows] = jnp.transpose(score).astype(BF16)
    act_out = pltpu.make_async_copy(act_ref, act_hbm, out_sem.at[0])
    act_out.start()

    quarter = hidden // 2
    sizes, bases = [quarter], [0]
    for f in range(folds):
        sizes.append(sizes[-1] // 2)
        bases.append(bases[-1] + ((z // (1 << f)) % 2) * sizes[-1])

    def fold_copy(f):
        there = bases[f] + (1 - (z // (1 << f)) % 2) * sizes[f + 1]
        rows = pl.ds(pl.multiple_of(there, sizes[f + 1]), sizes[f + 1])
        return copy_to(
            ws.at[rows], w_in.at[f, pl.ds(0, sizes[f + 1])], w_send.at[f], w_recv.at[f], dev_fold[f], c
        )

    def cross_copy(i):
        return copy_to(
            w_cross.at[i], w_cross_in.at[i], w_send.at[folds + i], w_recv.at[folds + i],
            (dev_a, dev_b)[i], c,
        )

    def unfold_copy(f):
        rows = pl.ds(pl.multiple_of(bases[f + 1], sizes[f + 1]), sizes[f + 1])
        return copy_to(
            w_full.at[c, rows], w_full.at[c, rows], w_send.at[folds + 2 + f], w_recv.at[folds + 2 + f],
            dev_fold[f], c,
        )

    def weight_step(s):
        if s < folds:
            fold_copy(s).wait_recv()
            rows = pl.ds(pl.multiple_of(bases[s + 1], sizes[s + 1]), sizes[s + 1])
            ws[rows, :] += w_in[s, pl.ds(0, sizes[s + 1])]
            if s + 1 < folds:
                fold_copy(s + 1).start()
            else:
                w_cross[0] = ws[rows, :]
                cross_copy(0).start()
        elif s < folds + 2:
            i = s - folds
            cross_copy(i).wait_recv()
            if i == 0:
                w_cross[1] = w_cross[0] + w_cross_in[0]
                cross_copy(1).start()
            else:
                rows = pl.ds(pl.multiple_of(bases[folds], sizes[folds]), sizes[folds])
                w_full[c, rows] = w_cross[1] + w_cross_in[1]
                unfold_copy(folds - 1).start()
        else:
            f = 2 * folds + 1 - s
            unfold_copy(f).wait_recv()
            if f > 0:
                unfold_copy(f - 1).start()

    ws[...] = jnp.dot(
        st[pl.ds(pl.multiple_of(c * quarter, quarter), quarter), :], ax[...],
        preferred_element_type=F32,
    )
    fold_copy(0).start()

    near = jnp.minimum(z, layers - 1 - z)
    reach = layers - 1 - near
    long_side = jnp.where(z == near, 1, -1)

    def target_layer(t):
        u = t - (reach - near)
        return jnp.where(
            u < 0, z + long_side * (reach - t), z + (1 - 2 * (u % 2)) * (near - u // 2)
        )

    def piece(k):
        z_ = target_layer(k // 4)
        q = k % 4
        b_ = jnp.where(q < 2, 1 - b, b)
        a_ = jnp.where(q % 2 == 0, 1 - a, a)
        return z_, b_, a_, block_at(z_, b_, a_)

    def p_copy(j):
        return copy_to(ps.at[j, other], ps.at[j, other], p_send_p.at[j], p_recv_p.at[j], d, other)

    def b_copy(z_, a_):
        return copy_to(
            ps.at[block_at(z_, 1 - b, a_), c], from_b.at[z_, a_], b_send.at[z_, a_], b_recv.at[z_, a_],
            dev_b, c,
        )

    def a_copy(z_):
        return copy_to(
            ps.at[block_at(z_, b, 1 - a), c], from_a.at[z_], a_send.at[z_], a_recv.at[z_], dev_a, c
        )

    def z_copy(z_, up):
        return copy_to(
            ps.at[block_at(z_, b, a), c], from_z.at[up, z_], z_send.at[z_], z_recv.at[up, z_],
            d - 4 + 8 * up, c,
        )

    def backward(k):
        z_, b_, a_, j = piece(k)

        @pl.when(owner(j) == c)
        def _():
            o = (d - j + domains) % domains - c * sections
            m = flag(o)
            for h in range(2):
                ps[j, h] = (
                    jnp.dot(st[...], tiles[o, :, pl.ds(h * half, half)], preferred_element_type=F32) * m
                ).astype(BF16)
            p_copy(j).start()

            @pl.when(jnp.logical_and(b_ != b, k < 8))
            def _():
                b_copy(z_, a_).start()

    def relay_partner(k):
        z_, b_, a_, j = piece(k)

        @pl.when(owner(j) != c)
        def _():
            copy_to(ps.at[j, c], ps.at[j, c], p_send_p.at[j], p_recv_p.at[j], d, other).wait_recv()

            @pl.when(jnp.logical_and(b_ != b, k < 8))
            def _():
                b_copy(z_, a_).start()

    def backward_step(k, carry):
        @pl.when(k < domains)
        def _():
            backward(k)

        @pl.when(k >= 4)
        def _():
            relay_partner(k - 4)

        for f in range(folds):
            @pl.when(k == 8 * f + 6)
            def _():
                weight_step(f)

        return carry

    lax.fori_loop(0, domains + 4, backward_step, 0)

    def stage_a(t):
        z_ = target_layer(t)
        b_copy(z_, 1 - a).wait_recv()
        j = block_at(z_, b, 1 - a)
        ps[j, c] = (ps[j, c].astype(F32) + from_b[z_, 1 - a].astype(F32)).astype(BF16)
        a_copy(z_).start()

    def stage_z(t):
        z_ = target_layer(t)
        b_copy(z_, a).wait_recv()
        a_copy(z_).wait_recv()
        j = block_at(z_, b, a)

        def mine():
            return ps[j, c].astype(F32) + from_b[z_, a].astype(F32) + from_a[z_].astype(F32)

        @pl.when(z_ == z)
        def _():
            part[0] = mine()

        @pl.when(jnp.logical_and(z_ > z, z == 0))
        def _():
            ps[j, c] = mine().astype(BF16)
            z_copy(z_, 1).start()

        @pl.when(jnp.logical_and(z_ < z, z == layers - 1))
        def _():
            ps[j, c] = mine().astype(BF16)
            z_copy(z_, 0).start()

    def stage_relay(t):
        z_ = target_layer(t)
        j = block_at(z_, b, a)

        def pass_on(up):
            z_copy(z_, up).wait_recv()
            ps[j, c] = (
                ps[j, c].astype(F32) + from_b[z_, a].astype(F32) + from_a[z_].astype(F32)
                + from_z[up, z_].astype(F32)
            ).astype(BF16)
            z_copy(z_, up).start()

        @pl.when(jnp.logical_and(z_ > z, z > 0))
        def _():
            pass_on(1)

        @pl.when(jnp.logical_and(z_ < z, z < layers - 1))
        def _():
            pass_on(0)

    for r in range(2):
        part_copy(r).wait_send()

    stages = max(layers + 1, folds + 3)
    for t in range(stages):
        if t < layers:
            stage_a(t)
        if 1 <= t <= folds + 2:
            weight_step(folds + t - 1)
        if t + 2 < layers:
            b_copy(target_layer(t + 2), 1 - a).start()
            b_copy(target_layer(t + 2), a).start()
        if 1 <= t <= layers:
            stage_z(t - 1)
        if t == 2:
            stage_relay(0)
        if 2 <= t <= layers:
            stage_relay(t - 1)
    w_last = copy_to(w_full.at[c], w_full.at[c], last_send.at[0], last_recv.at[0], d, other)
    w_last.start()

    @pl.when(z > 0)
    def _():
        z_copy(z, 1).wait_recv()
        part[0] += from_z[1, z].astype(F32)

    @pl.when(z < layers - 1)
    def _():
        z_copy(z, 0).wait_recv()
        part[0] += from_z[0, z].astype(F32)

    node = jnp.transpose(part[0]).astype(BF16)
    fg_half[c] = lax.dot_general(
        node, w_ref[...], (((1,), (1,)), ((), ())), preferred_element_type=F32
    ).astype(BF16)
    f_last = copy_to(fg_half.at[c], fg_half.at[c], last_send.at[1], last_recv.at[1], d, other)
    f_last.start()

    def fg_out(h):
        return pltpu.make_async_copy(
            fg_half.at[h], fg_hbm.at[pl.ds(pl.multiple_of(h * half, half), half)], out_sem.at[1 + h]
        )

    fg_out(c).start()

    copy_to(w_full.at[other], w_full.at[other], last_send.at[0], last_recv.at[0], d, other).wait_recv()
    for h in range(2):
        wg_ref[:, pl.ds(h * quarter, quarter)] = jnp.transpose(w_full[h]) * scaling
    wg_out = pltpu.make_async_copy(wg_ref, wg_hbm, out_sem.at[3])
    wg_out.start()

    def drain_p(j, carry):
        @pl.when(jnp.logical_and(owner(j) != c, j != d))
        def _():
            x_copy_p(j).wait_send()
            y_copy_p(j).wait_send()

        @pl.when(owner(j) == c)
        def _():
            p_copy(j).wait_send()

        return carry

    lax.fori_loop(0, domains, drain_p, 0)

    def drain(z_, carry):
        @pl.when(jnp.logical_and(z_ <= z, z < layers - 1))
        def _():
            x_copy_z(block_at(z_, b, a), z_, 1).wait_send()
            y_slab(z_, 1).wait_send()

        @pl.when(jnp.logical_and(z_ >= z, z > 0))
        def _():
            x_copy_z(block_at(z_, b, a), z_, 0).wait_send()
            y_slab(z_, 0).wait_send()

        x_copy_a(block_at(z_, b, a), z_).wait_send()
        a_copy(z_).wait_send()
        for a_ in range(2):
            x_copy_b(block_at(z_, b, a_), z_, a_).wait_send()
            b_copy(z_, a_).wait_send()

        @pl.when(z_ > z)
        def _():
            z_copy(z_, 1).wait_send()

        @pl.when(z_ < z)
        def _():
            z_copy(z_, 0).wait_send()

        return carry

    lax.fori_loop(0, layers, drain, 0)
    y_copy_a().wait_send()
    for a_ in range(2):
        y_copy_b(a_).wait_send()
    for f in range(folds):
        fold_copy(f).wait_send()
        unfold_copy(f).wait_send()
    for i in range(2):
        cross_copy(i).wait_send()
    copy_to(fg_half.at[other], fg_half.at[other], last_send.at[1], last_recv.at[1], d, other).wait_recv()
    fg_out(other).start()
    w_last.wait_send()
    f_last.wait_send()
    act_out.wait()
    wg_out.wait()
    for h in range(2):
        fg_out(h).wait()


def finish_kernel(act, fg, wg, act_out, fg_out, wg_out, act_v, fg_v, wg_v, sem):
    pairs = ((act, act_v, act_out), (fg, fg_v, fg_out), (wg, wg_v, wg_out))
    inward = [pltpu.make_async_copy(p[0], p[1], sem.at[0, i]) for i, p in enumerate(pairs)]
    outward = [pltpu.make_async_copy(p[1], p[2], sem.at[1, i]) for i, p in enumerate(pairs)]
    for copy in inward:
        copy.start()
    for first, second in zip(inward, outward):
        first.wait()
        second.start()
    for copy in outward:
        copy.wait()


def kernel_shards(features, weight, grad_out, tiles, tile_mask):
    domains = lax.axis_size("dom")
    layers = domains // 4
    folds = layers.bit_length() - 1
    sections = tiles.shape[1]
    rows, hidden = features.shape
    half, quarter = rows // 2, hidden // 2
    dma = pltpu.SemaphoreType.DMA
    out_shape = (
        jax.ShapeDtypeStruct((rows, hidden), BF16),
        jax.ShapeDtypeStruct((rows, hidden), BF16),
        jax.ShapeDtypeStruct((hidden, hidden), F32),
    )
    anywhere = [pl.BlockSpec(memory_space=pl.ANY)] * 3
    results = pl.pallas_call(
        functools.partial(layer_kernel, domains, float((rows * domains) ** (-0.5))),
        out_shape=out_shape,
        in_specs=[pl.BlockSpec(memory_space=pltpu.HBM)] * 4 + [pl.BlockSpec(memory_space=pltpu.SMEM)],
        out_specs=anywhere,
        scratch_shapes=[
            pltpu.VMEM((rows, hidden), BF16),
            pltpu.VMEM((hidden, hidden), F32),
            pltpu.VMEM(weight.shape, BF16),
            pltpu.VMEM((rows, hidden), BF16),
            pltpu.VMEM(tiles.shape[1:], BF16),
            pltpu.VMEM((domains, 2, half, hidden), BF16),
            pltpu.VMEM((domains, 2, hidden, half), BF16),
            pltpu.VMEM((layers, 2, hidden, half), BF16),
            pltpu.VMEM((layers, hidden, half), BF16),
            pltpu.VMEM((2, layers, hidden, half), BF16),
            pltpu.VMEM((2, half, hidden), F32),
            pltpu.VMEM((2, half, hidden), F32),
            pltpu.VMEM((rows, hidden), BF16),
            pltpu.VMEM((hidden, rows), BF16),
            pltpu.VMEM((quarter, hidden), F32),
            pltpu.VMEM((folds, quarter // 2, hidden), F32),
            pltpu.VMEM((2, quarter // layers, hidden), F32),
            pltpu.VMEM((2, quarter // layers, hidden), F32),
            pltpu.VMEM((2, quarter, hidden), F32),
            pltpu.VMEM((2, half, hidden), BF16),
            dma((2,)), dma((3,)), dma((4,)),
            dma((domains,)), dma((domains,)),
            dma((2, layers)), dma((layers,)), dma((layers, 2)), dma((domains,)),
            dma((3,)), dma((4,)), dma((2, layers)), dma((layers,)), dma((domains,)), dma((domains,)),
            dma((2,)), dma((2,)),
            dma((domains,)), dma((domains,)),
            dma((layers, 2)), dma((layers, 2)),
            dma((layers,)), dma((layers,)),
            dma((layers,)), dma((2, layers)),
            dma((2 * folds + 2,)), dma((2 * folds + 2,)),
            dma((2,)), dma((2,)),
        ],
        compiler_params=pltpu.CompilerParams(
            collective_id=0, has_side_effects=True, vmem_limit_bytes=63 * 1024 * 1024
        ),
        cost_estimate=pl.CostEstimate(
            flops=4 * sections * rows * rows * hidden,
            bytes_accessed=2 * sections * rows * rows,
            transcendentals=rows * hidden,
        ),
    )(features, weight, grad_out, tiles, tile_mask)
    return pl.pallas_call(
        finish_kernel,
        out_shape=out_shape,
        in_specs=anywhere,
        out_specs=anywhere,
        scratch_shapes=[
            pltpu.VMEM((rows, hidden), BF16),
            pltpu.VMEM((rows, hidden), BF16),
            pltpu.VMEM((hidden, hidden), F32),
            dma((2, 3)),
        ],
        compiler_params=pltpu.CompilerParams(vmem_limit_bytes=63 * 1024 * 1024),
        cost_estimate=pl.CostEstimate(flops=0, bytes_accessed=6 * rows * hidden * 2, transcendentals=0),
    )(*results)


def solution(mesh):
    domains, replicas = mesh.shape["dom"], mesh.shape["rep"]
    paired = replicas == 2 and domains >= 8 and domains & (domains - 1) == 0
    placed = (P("dom", None), P(), P("dom", None), P("dom", "rep", None, None), P("dom", "rep"))
    return jax.shard_map(
        kernel_shards if paired else ring_shards,
        mesh=mesh,
        in_specs=placed,
        out_specs=(P("dom", None), P("dom", None), P()),
        check_vma=False,
    )
```

```python
import functools

import jax
import jax.numpy as jnp
from jax import lax
from jax.experimental import pallas as pl
from jax.experimental.pallas import tpu as pltpu
from jax.sharding import PartitionSpec as P

MESH = pl.DeviceIdType.MESH
F32 = jnp.float32
BF16 = jnp.bfloat16


def shifted_2(block, axis, distance):
    devices = range(lax.axis_size(axis))
    route = [((i - distance) % len(devices), i) for i in devices]
    return lax.ppermute(block, axis, route)


def tile_product(tile, weight_flag, operand, transposed):
    if transposed:
        contraction = (((0,), (0,)), ((), ()))
        out_rows = tile.shape[1]
    else:
        contraction = (((1,), (0,)), ((), ()))
        out_rows = tile.shape[0]

    def compute():
        return lax.dot_general(tile, operand, contraction, preferred_element_type=jnp.float32)

    def skipped():
        return jnp.zeros((out_rows, operand.shape[1]), jnp.float32)

    return lax.cond(weight_flag > 0, compute, skipped)


def ring_shards(features, weight, grad_out, tiles, tile_mask):
    domains = lax.axis_size("dom")
    replicas = lax.axis_size("rep")
    sections = domains // replicas
    replica = lax.axis_index("rep")
    bit_count = replicas.bit_length() - 1
    rows_here = features.shape[0]
    hidden = features.shape[1]
    projected = jnp.dot(features, weight, preferred_element_type=jnp.float32).astype(jnp.bfloat16)
    current = projected
    for level in range(bit_count):
        shifted = shifted_2(current, "dom", sections << level)
        current = jnp.where(replica >> level & 1 == 1, shifted, current)
    partial_value = jnp.zeros((rows_here, hidden), jnp.float32)
    for section in range(sections):
        if section > 0:
            current = shifted_2(current, "dom", 1)
        partial_value = partial_value + tile_product(
            tiles[0, section], tile_mask[0, section], current, False
        )
    total = lax.psum(partial_value, "rep")
    gate_value = jax.nn.sigmoid(total)
    activated = (total * gate_value).astype(jnp.bfloat16)
    score_grad = (
        grad_out.astype(jnp.float32) * gate_value * (1.0 + total * (1.0 - gate_value))
    ).astype(jnp.bfloat16)
    carried = tile_product(tiles[0, sections - 1], tile_mask[0, sections - 1], score_grad, True)
    for section in range(sections - 2, -1, -1):
        carried = shifted_2(carried, "dom", -1)
        carried = carried + tile_product(tiles[0, section], tile_mask[0, section], score_grad, True)
    for level in range(bit_count):
        shifted = shifted_2(carried, "dom", -(sections << level))
        carried = jnp.where(replica >> level & 1 == 1, shifted, carried)
    node_grad = lax.psum(carried, "rep").astype(jnp.bfloat16)
    feature_grad = lax.dot_general(
        node_grad, weight, (((1,), (1,)), ((), ())), preferred_element_type=jnp.float32
    ).astype(jnp.bfloat16)
    scaling = (rows_here * domains) ** (-0.5)
    weight_term = lax.dot_general(
        features, node_grad, (((0,), (0,)), ((), ())), preferred_element_type=jnp.float32
    )
    weight_grad = lax.psum(weight_term, "dom") * scaling
    return (activated, feature_grad, weight_grad)


def layer_kernel(
    domains, scaling,
    x_hbm, w_hbm, g_hbm, tiles_hbm, mask_ref,
    act_hbm, fg_hbm, wg_hbm,
    act_ref, wg_ref, w_ref, g_ref, tiles, xs, ps, from_b, from_a, from_z, part, part_out, part_in, ax, st, ws, w_in, w_cross, w_cross_in, w_full, fg_half,
    own_sem, tile_sem, out_sem, x_recv, x_recv_p, x_send_z, x_send_a, x_send_b, x_send_p,
    y_send, y_recv, y_send_z, y_recv_z, y_send_p, y_recv_p,
    part_send, part_recv,
    p_recv_p, p_send_p, b_send, b_recv, a_send, a_recv, z_send, z_recv,
    w_send, w_recv, last_send, last_recv,
):
    layers = domains // 4
    folds = layers.bit_length() - 1
    sections = domains // 2
    half = x_hbm.shape[0] // 2
    hidden = x_hbm.shape[1]
    cut = half * 7 // 8
    main, rest = pl.ds(0, cut), pl.ds(cut, half - cut)
    d = lax.axis_index("dom")
    c = lax.axis_index("rep")
    other = 1 - c
    step_a, step_b = 1 + c, 2 - c
    z = d // 4
    a = (d // step_a) % 2
    b = (d // step_b) % 2

    def block_at(z_, b_, a_):
        return z_ * 4 + b_ * step_b + a_ * step_a

    dev_a, dev_b = block_at(z, b, 1 - a), block_at(z, 1 - b, a)
    dev_fold = [block_at(z + (1 << f) * (1 - 2 * ((z // (1 << f)) % 2)), b, a) for f in range(folds)]
    far = dev_fold[1:]

    def copy_to(src, dst, send, recv, dom, rep):
        return pltpu.make_async_remote_copy(
            src_ref=src, dst_ref=dst, send_sem=send, recv_sem=recv,
            device_id=(dom, rep), device_id_type=MESH,
        )

    own_copies = [
        pltpu.make_async_copy(x_hbm.at[pl.ds(h * half, half)], xs.at[d, h], own_sem.at[h])
        for h in range(2)
    ]
    tile_copies = [
        pltpu.make_async_copy(w_hbm, w_ref, tile_sem.at[0]),
        pltpu.make_async_copy(g_hbm, g_ref, tile_sem.at[1]),
        pltpu.make_async_copy(tiles_hbm.at[0], tiles, tile_sem.at[2]),
    ]
    for copy in own_copies + tile_copies:
        copy.start()

    barrier = pltpu.get_barrier_semaphore()
    for dom, rep in [(dev_a, c), (dev_b, c), (d, other)] + [(f, c) for f in far]:
        pl.semaphore_signal(barrier, inc=1, device_id=(dom, rep), device_id_type=MESH)

    @pl.when(z > 0)
    def _():
        pl.semaphore_signal(barrier, inc=1, device_id=(d - 4, c), device_id_type=MESH)

    @pl.when(z < layers - 1)
    def _():
        pl.semaphore_signal(barrier, inc=1, device_id=(d + 4, c), device_id_type=MESH)

    ends = jnp.where(z > 0, 1, 0) + jnp.where(z < layers - 1, 1, 0)
    pl.semaphore_wait(barrier, 3 + len(far) + ends)

    def owner(j):
        return ((d - j + domains) % domains) // sections

    def x_copy_z(j, z_, up):
        return copy_to(xs.at[j, c, main], xs.at[j, c, main], x_send_z.at[up, z_], x_recv.at[j], d - 4 + 8 * up, c)

    def x_copy_a(j, z_):
        return copy_to(xs.at[j, c, main], xs.at[j, c, main], x_send_a.at[z_], x_recv.at[j], dev_a, c)

    def x_copy_b(j, z_, a_):
        return copy_to(xs.at[j, c, main], xs.at[j, c, main], x_send_b.at[z_, a_], x_recv.at[j], dev_b, c)

    def x_copy_p(j):
        return copy_to(xs.at[j, c, main], xs.at[j, c, main], x_send_p.at[j], x_recv_p.at[j], d, other)

    def y_copy_a():
        return copy_to(
            xs.at[d, c, rest], xs.at[d, c, rest], y_send.at[2], y_recv.at[d % 4], dev_a, c
        )

    def y_copy_b(a_):
        j = block_at(z, b, a_)
        return copy_to(xs.at[j, c, rest], xs.at[j, c, rest], y_send.at[a_], y_recv.at[j % 4], dev_b, c)

    def y_slab(z_, up):
        slab = xs.at[pl.ds(z_ * 4, 4), c, rest]
        return copy_to(slab, slab, y_send_z.at[up, z_], y_recv_z.at[z_], d - 4 + 8 * up, c)

    def y_copy_p(j):
        return copy_to(
            xs.at[j, c, rest], xs.at[j, c, rest], y_send_p.at[j], y_recv_p.at[j], d, other
        )

    def y_wait(b_, a_):
        j = block_at(z, b_, a_)
        copy_to(
            xs.at[j, c, rest], xs.at[j, c, rest], y_send.at[2], y_recv.at[j % 4], dev_a, c
        ).wait_recv()

    def y_to_partner(z_):
        def one(q, carry):
            j = z_ * 4 + q

            @pl.when(jnp.logical_and(owner(j) != c, j != d))
            def _():
                y_copy_p(j).start()

            return carry

        lax.fori_loop(0, 4, one, 0)

    def y_layer_done():
        y_wait(1 - b, a)
        y_wait(1 - b, 1 - a)

        @pl.when(z > 0)
        def _():
            y_slab(z, 0).start()

        @pl.when(z < layers - 1)
        def _():
            y_slab(z, 1).start()

        y_to_partner(z)

    def y_from_layer(n):
        z_ = layer_of(n)

        @pl.when(in_range(z_))
        def _():
            y_slab(z_, 0).wait_recv()

            @pl.when(jnp.logical_and(z_ < z, z < layers - 1))
            def _():
                y_slab(z_, 1).start()

            @pl.when(jnp.logical_and(z_ > z, z > 0))
            def _():
                y_slab(z_, 0).start()

            y_to_partner(z_)

    def x_arrive(j):
        copy_to(xs.at[j, c, main], xs.at[j, c, main], x_send_p.at[j], x_recv.at[j], d, other).wait_recv()

        @pl.when(owner(j) != c)
        def _():
            x_copy_p(j).start()

    for copy in own_copies:
        copy.wait()

    @pl.when(z > 0)
    def _():
        x_copy_z(d, z, 0).start()

    @pl.when(z < layers - 1)
    def _():
        x_copy_z(d, z, 1).start()

    x_copy_b(d, z, a).start()
    x_copy_a(d, z).start()
    y_copy_b(a).start()
    y_copy_a().start()

    def layer_of(n):
        return z + ((n + 1) // 2) * (2 * ((n + 1) % 2) - 1)

    def in_range(z_):
        return jnp.logical_and(z_ >= 0, z_ < layers)

    def from_layer(n):
        z_ = layer_of(n)

        @pl.when(in_range(z_))
        def _():
            j = block_at(z_, b, a)
            x_arrive(j)

            @pl.when(jnp.logical_and(z_ < z, z < layers - 1))
            def _():
                x_copy_z(j, z_, 1).start()

            @pl.when(jnp.logical_and(z_ > z, z > 0))
            def _():
                x_copy_z(j, z_, 0).start()

            x_copy_b(j, z_, a).start()
            x_copy_a(j, z_).start()

    def from_a_side(n):
        z_ = layer_of(n)

        @pl.when(in_range(z_))
        def _():
            j = block_at(z_, b, 1 - a)
            x_arrive(j)
            x_copy_b(j, z_, 1 - a).start()

    def from_b_side(n):
        z_ = layer_of(n)

        @pl.when(in_range(z_))
        def _():
            x_arrive(block_at(z_, 1 - b, a))
            x_arrive(block_at(z_, 1 - b, 1 - a))

    def flag(o):
        return jnp.where(mask_ref[0, o] > 0, 1.0, 0.0)

    def product(j):
        o = (d - j + domains) % domains - c * sections
        m = flag(o).astype(BF16)
        x_top, x_low = xs[j, 0] * m, xs[j, 1] * m
        for r in range(2):
            rows = pl.ds(r * half, half)
            part[r] += jnp.dot(
                tiles[o, rows, pl.ds(0, half)], x_top, preferred_element_type=F32
            ) + jnp.dot(tiles[o, rows, pl.ds(half, half)], x_low, preferred_element_type=F32)

    def products(n):
        z_ = layer_of(n)

        def one(q, carry):
            j = z_ * 4 + q

            @pl.when(owner(j) == c)
            def _():
                @pl.when(j != d)
                def _():
                    for send, recv, rows in ((x_send_p, x_recv_p, main), (y_send_p, y_recv_p, rest)):
                        copy_to(
                            xs.at[j, other, rows], xs.at[j, other, rows], send.at[j], recv.at[j], d, other
                        ).wait_recv()

                product(j)

            return carry

        @pl.when(in_range(z_))
        def _():
            lax.fori_loop(0, 4, one, 0)

    visits = 2 * layers - 1
    for copy in tile_copies:
        copy.wait()
    for r in range(2):
        part[r] = jnp.zeros((half, hidden), F32)

    y_wait(b, 1 - a)
    y_copy_b(1 - a).start()

    def gather_step(n, carry):
        for lag, step in ((1, from_a_side), (0, from_layer), (2, from_b_side)):
            at = n - 2 * lag

            @pl.when(jnp.logical_and(at >= (1 if lag == 0 else 0), at < visits))
            def _():
                step(at)

        @pl.when(n == 2)
        def _():
            y_layer_done()

        @pl.when(jnp.logical_and(n >= 4, n - 3 < visits))
        def _():
            y_from_layer(n - 3)

        @pl.when(n >= 5)
        def _():
            products(n - 5)

        return carry

    lax.fori_loop(1, visits + 5, gather_step, 0)

    def part_copy(r):
        return copy_to(part_out.at[r], part_in.at[r], part_send.at[r], part_recv.at[r], d, other)

    for r in range(2):
        part_out[r] = part[r].astype(BF16)
        part_copy(r).start()

    for r in range(2):
        part_copy(r).wait_recv()
        rows = pl.ds(r * half, half)
        ax_here = (part_out[r].astype(F32) + part_in[r].astype(F32)).astype(BF16)
        ax[rows, :] = ax_here
        total = jnp.dot(ax_here, w_ref[...], preferred_element_type=F32)
        gate = jax.nn.sigmoid(total)
        act_ref[rows, :] = (total * gate).astype(BF16)
        score = g_ref[rows, :].astype(F32) * gate * (1.0 + total * (1.0 - gate))
        st[:, rows] = jnp.transpose(score).astype(BF16)
    act_out = pltpu.make_async_copy(act_ref, act_hbm, out_sem.at[0])
    act_out.start()

    quarter = hidden // 2
    sizes, bases = [quarter], [0]
    for f in range(folds):
        sizes.append(sizes[-1] // 2)
        bases.append(bases[-1] + ((z // (1 << f)) % 2) * sizes[-1])

    def fold_copy(f):
        there = bases[f] + (1 - (z // (1 << f)) % 2) * sizes[f + 1]
        rows = pl.ds(pl.multiple_of(there, sizes[f + 1]), sizes[f + 1])
        return copy_to(
            ws.at[rows], w_in.at[f, pl.ds(0, sizes[f + 1])], w_send.at[f], w_recv.at[f], dev_fold[f], c
        )

    def cross_copy(i):
        return copy_to(
            w_cross.at[i], w_cross_in.at[i], w_send.at[folds + i], w_recv.at[folds + i],
            (dev_a, dev_b)[i], c,
        )

    def unfold_copy(f):
        rows = pl.ds(pl.multiple_of(bases[f + 1], sizes[f + 1]), sizes[f + 1])
        return copy_to(
            w_full.at[c, rows], w_full.at[c, rows], w_send.at[folds + 2 + f], w_recv.at[folds + 2 + f],
            dev_fold[f], c,
        )

    def weight_step(s):
        if s < folds:
            fold_copy(s).wait_recv()
            rows = pl.ds(pl.multiple_of(bases[s + 1], sizes[s + 1]), sizes[s + 1])
            ws[rows, :] += w_in[s, pl.ds(0, sizes[s + 1])]
            if s + 1 < folds:
                fold_copy(s + 1).start()
            else:
                w_cross[0] = ws[rows, :]
                cross_copy(0).start()
        elif s < folds + 2:
            i = s - folds
            cross_copy(i).wait_recv()
            if i == 0:
                w_cross[1] = w_cross[0] + w_cross_in[0]
                cross_copy(1).start()
            else:
                rows = pl.ds(pl.multiple_of(bases[folds], sizes[folds]), sizes[folds])
                w_full[c, rows] = w_cross[1] + w_cross_in[1]
                unfold_copy(folds - 1).start()
        else:
            f = 2 * folds + 1 - s
            unfold_copy(f).wait_recv()
            if f > 0:
                unfold_copy(f - 1).start()

    ws[...] = jnp.dot(
        st[pl.ds(pl.multiple_of(c * quarter, quarter), quarter), :], ax[...],
        preferred_element_type=F32,
    )
    fold_copy(0).start()

    near = jnp.minimum(z, layers - 1 - z)
    reach = layers - 1 - near
    long_side = jnp.where(z == near, 1, -1)

    def target_layer(t):
        u = t - (reach - near)
        return jnp.where(
            u < 0, z + long_side * (reach - t), z + (1 - 2 * (u % 2)) * (near - u // 2)
        )

    def piece(k):
        z_ = target_layer(k // 4)
        q = k % 4
        b_ = jnp.where(q < 2, 1 - b, b)
        a_ = jnp.where(q % 2 == 0, 1 - a, a)
        return z_, b_, a_, block_at(z_, b_, a_)

    def p_copy(j):
        return copy_to(ps.at[j, other], ps.at[j, other], p_send_p.at[j], p_recv_p.at[j], d, other)

    def b_copy(z_, a_):
        return copy_to(
            ps.at[block_at(z_, 1 - b, a_), c], from_b.at[z_, a_], b_send.at[z_, a_], b_recv.at[z_, a_],
            dev_b, c,
        )

    def a_copy(z_):
        return copy_to(
            ps.at[block_at(z_, b, 1 - a), c], from_a.at[z_], a_send.at[z_], a_recv.at[z_], dev_a, c
        )

    def z_copy(z_, up):
        return copy_to(
            ps.at[block_at(z_, b, a), c], from_z.at[up, z_], z_send.at[z_], z_recv.at[up, z_],
            d - 4 + 8 * up, c,
        )

    def backward(k):
        z_, b_, a_, j = piece(k)

        @pl.when(owner(j) == c)
        def _():
            o = (d - j + domains) % domains - c * sections
            m = flag(o)
            for h in range(2):
                ps[j, h] = (
                    jnp.dot(st[...], tiles[o, :, pl.ds(h * half, half)], preferred_element_type=F32) * m
                ).astype(BF16)
            p_copy(j).start()

            @pl.when(jnp.logical_and(b_ != b, k < 8))
            def _():
                b_copy(z_, a_).start()

    def relay_partner(k):
        z_, b_, a_, j = piece(k)

        @pl.when(owner(j) != c)
        def _():
            copy_to(ps.at[j, c], ps.at[j, c], p_send_p.at[j], p_recv_p.at[j], d, other).wait_recv()

            @pl.when(jnp.logical_and(b_ != b, k < 8))
            def _():
                b_copy(z_, a_).start()

    def backward_step(k, carry):
        @pl.when(k < domains)
        def _():
            backward(k)

        @pl.when(k >= 4)
        def _():
            relay_partner(k - 4)

        for f in range(folds):
            @pl.when(k == 8 * f + 6)
            def _():
                weight_step(f)

        return carry

    lax.fori_loop(0, domains + 4, backward_step, 0)

    def stage_a(t):
        z_ = target_layer(t)
        b_copy(z_, 1 - a).wait_recv()
        j = block_at(z_, b, 1 - a)
        ps[j, c] = (ps[j, c].astype(F32) + from_b[z_, 1 - a].astype(F32)).astype(BF16)
        a_copy(z_).start()

    def stage_z(t):
        z_ = target_layer(t)
        b_copy(z_, a).wait_recv()
        a_copy(z_).wait_recv()
        j = block_at(z_, b, a)

        def mine():
            return ps[j, c].astype(F32) + from_b[z_, a].astype(F32) + from_a[z_].astype(F32)

        @pl.when(z_ == z)
        def _():
            part[0] = mine()

        @pl.when(jnp.logical_and(z_ > z, z == 0))
        def _():
            ps[j, c] = mine().astype(BF16)
            z_copy(z_, 1).start()

        @pl.when(jnp.logical_and(z_ < z, z == layers - 1))
        def _():
            ps[j, c] = mine().astype(BF16)
            z_copy(z_, 0).start()

    def stage_relay(t):
        z_ = target_layer(t)
        j = block_at(z_, b, a)

        def pass_on(up):
            z_copy(z_, up).wait_recv()
            ps[j, c] = (
                ps[j, c].astype(F32) + from_b[z_, a].astype(F32) + from_a[z_].astype(F32)
                + from_z[up, z_].astype(F32)
            ).astype(BF16)
            z_copy(z_, up).start()

        @pl.when(jnp.logical_and(z_ > z, z > 0))
        def _():
            pass_on(1)

        @pl.when(jnp.logical_and(z_ < z, z < layers - 1))
        def _():
            pass_on(0)

    for r in range(2):
        part_copy(r).wait_send()

    stages = max(layers + 1, folds + 3)
    for t in range(stages):
        if t < layers:
            stage_a(t)
        if 1 <= t <= folds + 2:
            weight_step(folds + t - 1)
        if t + 2 < layers:
            b_copy(target_layer(t + 2), 1 - a).start()
            b_copy(target_layer(t + 2), a).start()
        if 1 <= t <= layers:
            stage_z(t - 1)
        if t == 2:
            stage_relay(0)
        if 2 <= t <= layers:
            stage_relay(t - 1)
    w_last = copy_to(w_full.at[c], w_full.at[c], last_send.at[0], last_recv.at[0], d, other)
    w_last.start()

    @pl.when(z > 0)
    def _():
        z_copy(z, 1).wait_recv()
        part[0] += from_z[1, z].astype(F32)

    @pl.when(z < layers - 1)
    def _():
        z_copy(z, 0).wait_recv()
        part[0] += from_z[0, z].astype(F32)

    node = jnp.transpose(part[0]).astype(BF16)
    fg_half[c] = lax.dot_general(
        node, w_ref[...], (((1,), (1,)), ((), ())), preferred_element_type=F32
    ).astype(BF16)
    f_last = copy_to(fg_half.at[c], fg_half.at[c], last_send.at[1], last_recv.at[1], d, other)
    f_last.start()

    def fg_out(h):
        return pltpu.make_async_copy(
            fg_half.at[h], fg_hbm.at[pl.ds(pl.multiple_of(h * half, half), half)], out_sem.at[1 + h]
        )

    fg_out(c).start()

    copy_to(w_full.at[other], w_full.at[other], last_send.at[0], last_recv.at[0], d, other).wait_recv()
    for h in range(2):
        wg_ref[:, pl.ds(h * quarter, quarter)] = jnp.transpose(w_full[h]) * scaling
    wg_out = pltpu.make_async_copy(wg_ref, wg_hbm, out_sem.at[3])
    wg_out.start()

    def drain_p(j, carry):
        @pl.when(jnp.logical_and(owner(j) != c, j != d))
        def _():
            x_copy_p(j).wait_send()
            y_copy_p(j).wait_send()

        @pl.when(owner(j) == c)
        def _():
            p_copy(j).wait_send()

        return carry

    lax.fori_loop(0, domains, drain_p, 0)

    def drain(z_, carry):
        @pl.when(jnp.logical_and(z_ <= z, z < layers - 1))
        def _():
            x_copy_z(block_at(z_, b, a), z_, 1).wait_send()
            y_slab(z_, 1).wait_send()

        @pl.when(jnp.logical_and(z_ >= z, z > 0))
        def _():
            x_copy_z(block_at(z_, b, a), z_, 0).wait_send()
            y_slab(z_, 0).wait_send()

        x_copy_a(block_at(z_, b, a), z_).wait_send()
        a_copy(z_).wait_send()
        for a_ in range(2):
            x_copy_b(block_at(z_, b, a_), z_, a_).wait_send()
            b_copy(z_, a_).wait_send()

        @pl.when(z_ > z)
        def _():
            z_copy(z_, 1).wait_send()

        @pl.when(z_ < z)
        def _():
            z_copy(z_, 0).wait_send()

        return carry

    lax.fori_loop(0, layers, drain, 0)
    y_copy_a().wait_send()
    for a_ in range(2):
        y_copy_b(a_).wait_send()
    for f in range(folds):
        fold_copy(f).wait_send()
        unfold_copy(f).wait_send()
    for i in range(2):
        cross_copy(i).wait_send()
    copy_to(fg_half.at[other], fg_half.at[other], last_send.at[1], last_recv.at[1], d, other).wait_recv()
    fg_out(other).start()
    w_last.wait_send()
    f_last.wait_send()
    act_out.wait()
    wg_out.wait()
    for h in range(2):
        fg_out(h).wait()


def finish_kernel(act, fg, wg, act_out, fg_out, wg_out, act_v, fg_v, wg_v, sem):
    pairs = ((act, act_v, act_out), (fg, fg_v, fg_out), (wg, wg_v, wg_out))
    inward = [pltpu.make_async_copy(p[0], p[1], sem.at[0, i]) for i, p in enumerate(pairs)]
    outward = [pltpu.make_async_copy(p[1], p[2], sem.at[1, i]) for i, p in enumerate(pairs)]
    for copy in inward:
        copy.start()
    for first, second in zip(inward, outward):
        first.wait()
        second.start()
    for copy in outward:
        copy.wait()


def kernel_shards(features, weight, grad_out, tiles, tile_mask):
    domains = lax.axis_size("dom")
    layers = domains // 4
    folds = layers.bit_length() - 1
    sections = tiles.shape[1]
    rows, hidden = features.shape
    half, quarter = rows // 2, hidden // 2
    dma = pltpu.SemaphoreType.DMA
    out_shape = (
        jax.ShapeDtypeStruct((rows, hidden), BF16),
        jax.ShapeDtypeStruct((rows, hidden), BF16),
        jax.ShapeDtypeStruct((hidden, hidden), F32),
    )
    anywhere = [pl.BlockSpec(memory_space=pl.ANY)] * 3
    results = pl.pallas_call(
        functools.partial(layer_kernel, domains, float((rows * domains) ** (-0.5))),
        out_shape=out_shape,
        in_specs=[pl.BlockSpec(memory_space=pltpu.HBM)] * 4 + [pl.BlockSpec(memory_space=pltpu.SMEM)],
        out_specs=anywhere,
        scratch_shapes=[
            pltpu.VMEM((rows, hidden), BF16),
            pltpu.VMEM((hidden, hidden), F32),
            pltpu.VMEM(weight.shape, BF16),
            pltpu.VMEM((rows, hidden), BF16),
            pltpu.VMEM(tiles.shape[1:], BF16),
            pltpu.VMEM((domains, 2, half, hidden), BF16),
            pltpu.VMEM((domains, 2, hidden, half), BF16),
            pltpu.VMEM((layers, 2, hidden, half), BF16),
            pltpu.VMEM((layers, hidden, half), BF16),
            pltpu.VMEM((2, layers, hidden, half), BF16),
            pltpu.VMEM((2, half, hidden), F32),
            pltpu.VMEM((2, half, hidden), BF16),
            pltpu.VMEM((2, half, hidden), BF16),
            pltpu.VMEM((rows, hidden), BF16),
            pltpu.VMEM((hidden, rows), BF16),
            pltpu.VMEM((quarter, hidden), F32),
            pltpu.VMEM((folds, quarter // 2, hidden), F32),
            pltpu.VMEM((2, quarter // layers, hidden), F32),
            pltpu.VMEM((2, quarter // layers, hidden), F32),
            pltpu.VMEM((2, quarter, hidden), F32),
            pltpu.VMEM((2, half, hidden), BF16),
            dma((2,)), dma((3,)), dma((4,)),
            dma((domains,)), dma((domains,)),
            dma((2, layers)), dma((layers,)), dma((layers, 2)), dma((domains,)),
            dma((3,)), dma((4,)), dma((2, layers)), dma((layers,)), dma((domains,)), dma((domains,)),
            dma((2,)), dma((2,)),
            dma((domains,)), dma((domains,)),
            dma((layers, 2)), dma((layers, 2)),
            dma((layers,)), dma((layers,)),
            dma((layers,)), dma((2, layers)),
            dma((2 * folds + 2,)), dma((2 * folds + 2,)),
            dma((2,)), dma((2,)),
        ],
        compiler_params=pltpu.CompilerParams(
            collective_id=0, has_side_effects=True, vmem_limit_bytes=63 * 1024 * 1024
        ),
        cost_estimate=pl.CostEstimate(
            flops=4 * sections * rows * rows * hidden,
            bytes_accessed=2 * sections * rows * rows,
            transcendentals=rows * hidden,
        ),
    )(features, weight, grad_out, tiles, tile_mask)
    return pl.pallas_call(
        finish_kernel,
        out_shape=out_shape,
        in_specs=anywhere,
        out_specs=anywhere,
        scratch_shapes=[
            pltpu.VMEM((rows, hidden), BF16),
            pltpu.VMEM((rows, hidden), BF16),
            pltpu.VMEM((hidden, hidden), F32),
            dma((2, 3)),
        ],
        compiler_params=pltpu.CompilerParams(vmem_limit_bytes=63 * 1024 * 1024),
        cost_estimate=pl.CostEstimate(flops=0, bytes_accessed=6 * rows * hidden * 2, transcendentals=0),
    )(*results)


def solution(mesh):
    domains, replicas = mesh.shape["dom"], mesh.shape["rep"]
    paired = replicas == 2 and domains >= 8 and domains & (domains - 1) == 0
    placed = (P("dom", None), P(), P("dom", None), P("dom", "rep", None, None), P("dom", "rep"))
    return jax.shard_map(
        kernel_shards if paired else ring_shards,
        mesh=mesh,
        in_specs=placed,
        out_specs=(P("dom", None), P("dom", None), P()),
        check_vma=False,
    )
```

```python
import functools

import jax
import jax.numpy as jnp
from jax import lax
from jax.experimental import pallas as pl
from jax.experimental.pallas import tpu as pltpu
from jax.sharding import PartitionSpec as P

MESH = pl.DeviceIdType.MESH
F32 = jnp.float32
BF16 = jnp.bfloat16


def shifted_2(block, axis, distance):
    devices = range(lax.axis_size(axis))
    route = [((i - distance) % len(devices), i) for i in devices]
    return lax.ppermute(block, axis, route)


def tile_product(tile, weight_flag, operand, transposed):
    if transposed:
        contraction = (((0,), (0,)), ((), ()))
        out_rows = tile.shape[1]
    else:
        contraction = (((1,), (0,)), ((), ()))
        out_rows = tile.shape[0]

    def compute():
        return lax.dot_general(tile, operand, contraction, preferred_element_type=jnp.float32)

    def skipped():
        return jnp.zeros((out_rows, operand.shape[1]), jnp.float32)

    return lax.cond(weight_flag > 0, compute, skipped)


def ring_shards(features, weight, grad_out, tiles, tile_mask):
    domains = lax.axis_size("dom")
    replicas = lax.axis_size("rep")
    sections = domains // replicas
    replica = lax.axis_index("rep")
    bit_count = replicas.bit_length() - 1
    rows_here = features.shape[0]
    hidden = features.shape[1]
    projected = jnp.dot(features, weight, preferred_element_type=jnp.float32).astype(jnp.bfloat16)
    current = projected
    for level in range(bit_count):
        shifted = shifted_2(current, "dom", sections << level)
        current = jnp.where(replica >> level & 1 == 1, shifted, current)
    partial_value = jnp.zeros((rows_here, hidden), jnp.float32)
    for section in range(sections):
        if section > 0:
            current = shifted_2(current, "dom", 1)
        partial_value = partial_value + tile_product(
            tiles[0, section], tile_mask[0, section], current, False
        )
    total = lax.psum(partial_value, "rep")
    gate_value = jax.nn.sigmoid(total)
    activated = (total * gate_value).astype(jnp.bfloat16)
    score_grad = (
        grad_out.astype(jnp.float32) * gate_value * (1.0 + total * (1.0 - gate_value))
    ).astype(jnp.bfloat16)
    carried = tile_product(tiles[0, sections - 1], tile_mask[0, sections - 1], score_grad, True)
    for section in range(sections - 2, -1, -1):
        carried = shifted_2(carried, "dom", -1)
        carried = carried + tile_product(tiles[0, section], tile_mask[0, section], score_grad, True)
    for level in range(bit_count):
        shifted = shifted_2(carried, "dom", -(sections << level))
        carried = jnp.where(replica >> level & 1 == 1, shifted, carried)
    node_grad = lax.psum(carried, "rep").astype(jnp.bfloat16)
    feature_grad = lax.dot_general(
        node_grad, weight, (((1,), (1,)), ((), ())), preferred_element_type=jnp.float32
    ).astype(jnp.bfloat16)
    scaling = (rows_here * domains) ** (-0.5)
    weight_term = lax.dot_general(
        features, node_grad, (((0,), (0,)), ((), ())), preferred_element_type=jnp.float32
    )
    weight_grad = lax.psum(weight_term, "dom") * scaling
    return (activated, feature_grad, weight_grad)


def layer_kernel(
    domains, scaling,
    x_hbm, w_hbm, g_hbm, tiles_hbm, mask_ref,
    act_hbm, fg_hbm, wg_hbm,
    act_ref, wg_ref, w_ref, g_ref, tiles, xs, ps, from_b, from_a, from_z, part, part_out, part_in, ax, st, ws, w_in, w_cross, w_cross_in, w_full, fg_half,
    own_sem, tile_sem, out_sem, x_recv, x_recv_p, x_send_z, x_send_a, x_send_b, x_send_p,
    y_send, y_recv, y_send_z, y_recv_z, y_send_p, y_recv_p,
    part_send, part_recv,
    p_recv_p, p_send_p, b_send, b_recv, a_send, a_recv, z_send, z_recv,
    w_send, w_recv, last_send, last_recv,
):
    layers = domains // 4
    folds = layers.bit_length() - 1
    sections = domains // 2
    half = x_hbm.shape[0] // 2
    hidden = x_hbm.shape[1]
    cut = half * 7 // 8
    main, rest = pl.ds(0, cut), pl.ds(cut, half - cut)
    d = lax.axis_index("dom")
    c = lax.axis_index("rep")
    other = 1 - c
    step_a, step_b = 1 + c, 2 - c
    z = d // 4
    a = (d // step_a) % 2
    b = (d // step_b) % 2

    def block_at(z_, b_, a_):
        return z_ * 4 + b_ * step_b + a_ * step_a

    dev_a, dev_b = block_at(z, b, 1 - a), block_at(z, 1 - b, a)
    dev_fold = [block_at(z + (1 << f) * (1 - 2 * ((z // (1 << f)) % 2)), b, a) for f in range(folds)]
    far = dev_fold[1:]

    def copy_to(src, dst, send, recv, dom, rep):
        return pltpu.make_async_remote_copy(
            src_ref=src, dst_ref=dst, send_sem=send, recv_sem=recv,
            device_id=(dom, rep), device_id_type=MESH,
        )

    own_copies = [
        pltpu.make_async_copy(x_hbm.at[pl.ds(h * half, half)], xs.at[d, h], own_sem.at[h])
        for h in range(2)
    ]
    tile_copies = [
        pltpu.make_async_copy(w_hbm, w_ref, tile_sem.at[0]),
        pltpu.make_async_copy(g_hbm, g_ref, tile_sem.at[1]),
        pltpu.make_async_copy(tiles_hbm.at[0], tiles, tile_sem.at[2]),
    ]
    for copy in own_copies + tile_copies:
        copy.start()

    barrier = pltpu.get_barrier_semaphore()
    for dom, rep in [(dev_a, c), (dev_b, c), (d, other)] + [(f, c) for f in far]:
        pl.semaphore_signal(barrier, inc=1, device_id=(dom, rep), device_id_type=MESH)

    @pl.when(z > 0)
    def _():
        pl.semaphore_signal(barrier, inc=1, device_id=(d - 4, c), device_id_type=MESH)

    @pl.when(z < layers - 1)
    def _():
        pl.semaphore_signal(barrier, inc=1, device_id=(d + 4, c), device_id_type=MESH)

    ends = jnp.where(z > 0, 1, 0) + jnp.where(z < layers - 1, 1, 0)
    pl.semaphore_wait(barrier, 3 + len(far) + ends)

    def owner(j):
        return ((d - j + domains) % domains) // sections

    def x_copy_z(j, z_, up):
        return copy_to(xs.at[j, c, main], xs.at[j, c, main], x_send_z.at[up, z_], x_recv.at[j], d - 4 + 8 * up, c)

    def x_copy_a(j, z_):
        return copy_to(xs.at[j, c, main], xs.at[j, c, main], x_send_a.at[z_], x_recv.at[j], dev_a, c)

    def x_copy_b(j, z_, a_):
        return copy_to(xs.at[j, c, main], xs.at[j, c, main], x_send_b.at[z_, a_], x_recv.at[j], dev_b, c)

    def x_copy_p(j):
        return copy_to(xs.at[j, c, main], xs.at[j, c, main], x_send_p.at[j], x_recv_p.at[j], d, other)

    def y_copy_a():
        return copy_to(
            xs.at[d, c, rest], xs.at[d, c, rest], y_send.at[2], y_recv.at[d % 4], dev_a, c
        )

    def y_copy_b(a_):
        j = block_at(z, b, a_)
        return copy_to(xs.at[j, c, rest], xs.at[j, c, rest], y_send.at[a_], y_recv.at[j % 4], dev_b, c)

    def y_slab(z_, up):
        slab = xs.at[pl.ds(z_ * 4, 4), c, rest]
        return copy_to(slab, slab, y_send_z.at[up, z_], y_recv_z.at[z_], d - 4 + 8 * up, c)

    def y_copy_p(j):
        return copy_to(
            xs.at[j, c, rest], xs.at[j, c, rest], y_send_p.at[j], y_recv_p.at[j], d, other
        )

    def y_wait(b_, a_):
        j = block_at(z, b_, a_)
        copy_to(
            xs.at[j, c, rest], xs.at[j, c, rest], y_send.at[2], y_recv.at[j % 4], dev_a, c
        ).wait_recv()

    def y_to_partner(z_):
        def one(q, carry):
            j = z_ * 4 + q

            @pl.when(jnp.logical_and(owner(j) != c, j != d))
            def _():
                y_copy_p(j).start()

            return carry

        lax.fori_loop(0, 4, one, 0)

    def y_layer_done():
        y_wait(1 - b, a)
        y_wait(1 - b, 1 - a)

        @pl.when(z > 0)
        def _():
            y_slab(z, 0).start()

        @pl.when(z < layers - 1)
        def _():
            y_slab(z, 1).start()

        y_to_partner(z)

    def y_from_layer(n):
        z_ = layer_of(n)

        @pl.when(in_range(z_))
        def _():
            y_slab(z_, 0).wait_recv()

            @pl.when(jnp.logical_and(z_ < z, z < layers - 1))
            def _():
                y_slab(z_, 1).start()

            @pl.when(jnp.logical_and(z_ > z, z > 0))
            def _():
                y_slab(z_, 0).start()

            y_to_partner(z_)

    def x_arrive(j):
        copy_to(xs.at[j, c, main], xs.at[j, c, main], x_send_p.at[j], x_recv.at[j], d, other).wait_recv()

        @pl.when(owner(j) != c)
        def _():
            x_copy_p(j).start()

    for copy in own_copies:
        copy.wait()

    @pl.when(z > 0)
    def _():
        x_copy_z(d, z, 0).start()

    @pl.when(z < layers - 1)
    def _():
        x_copy_z(d, z, 1).start()

    x_copy_b(d, z, a).start()
    x_copy_a(d, z).start()
    y_copy_b(a).start()
    y_copy_a().start()

    def layer_of(n):
        return z + ((n + 1) // 2) * (2 * ((n + 1) % 2) - 1)

    def in_range(z_):
        return jnp.logical_and(z_ >= 0, z_ < layers)

    def from_layer(n):
        z_ = layer_of(n)

        @pl.when(in_range(z_))
        def _():
            j = block_at(z_, b, a)
            x_arrive(j)

            @pl.when(jnp.logical_and(z_ < z, z < layers - 1))
            def _():
                x_copy_z(j, z_, 1).start()

            @pl.when(jnp.logical_and(z_ > z, z > 0))
            def _():
                x_copy_z(j, z_, 0).start()

            x_copy_b(j, z_, a).start()
            x_copy_a(j, z_).start()

    def from_a_side(n):
        z_ = layer_of(n)

        @pl.when(in_range(z_))
        def _():
            j = block_at(z_, b, 1 - a)
            x_arrive(j)
            x_copy_b(j, z_, 1 - a).start()

    def from_b_side(n):
        z_ = layer_of(n)

        @pl.when(in_range(z_))
        def _():
            x_arrive(block_at(z_, 1 - b, a))
            x_arrive(block_at(z_, 1 - b, 1 - a))

    def flag(o):
        return jnp.where(mask_ref[0, o] > 0, 1.0, 0.0)

    def product(j):
        o = (d - j + domains) % domains - c * sections
        m = flag(o).astype(BF16)
        x_top, x_low = xs[j, 0] * m, xs[j, 1] * m
        for r in range(2):
            rows = pl.ds(r * half, half)
            part[r] += jnp.dot(
                tiles[o, rows, pl.ds(0, half)], x_top, preferred_element_type=F32
            ) + jnp.dot(tiles[o, rows, pl.ds(half, half)], x_low, preferred_element_type=F32)

    def products(n):
        z_ = layer_of(n)

        def one(q, carry):
            j = z_ * 4 + q

            @pl.when(owner(j) == c)
            def _():
                @pl.when(j != d)
                def _():
                    for send, recv, rows in ((x_send_p, x_recv_p, main), (y_send_p, y_recv_p, rest)):
                        copy_to(
                            xs.at[j, other, rows], xs.at[j, other, rows], send.at[j], recv.at[j], d, other
                        ).wait_recv()

                product(j)

            return carry

        @pl.when(in_range(z_))
        def _():
            lax.fori_loop(0, 4, one, 0)

    visits = 2 * layers - 1
    for copy in tile_copies:
        copy.wait()
    for r in range(2):
        part[r] = jnp.zeros((half, hidden), F32)

    y_wait(b, 1 - a)
    y_copy_b(1 - a).start()

    def gather_step(n, carry):
        for lag, step in ((1, from_a_side), (0, from_layer), (2, from_b_side)):
            at = n - 2 * lag

            @pl.when(jnp.logical_and(at >= (1 if lag == 0 else 0), at < visits))
            def _():
                step(at)

        @pl.when(n == 2)
        def _():
            y_layer_done()

        @pl.when(jnp.logical_and(n >= 4, n - 3 < visits))
        def _():
            y_from_layer(n - 3)

        @pl.when(n >= 5)
        def _():
            products(n - 5)

        return carry

    lax.fori_loop(1, visits + 5, gather_step, 0)

    def part_copy(r):
        return copy_to(part_out.at[r], part_in.at[r], part_send.at[r], part_recv.at[r], d, other)

    for r in range(2):
        part_out[r] = part[r].astype(BF16)
        part_copy(r).start()

    for r in range(2):
        part_copy(r).wait_recv()
        rows = pl.ds(r * half, half)
        ax_here = (part_out[r].astype(F32) + part_in[r].astype(F32)).astype(BF16)
        ax[rows, :] = ax_here
        total = jnp.dot(ax_here, w_ref[...], preferred_element_type=F32)
        gate = jax.nn.sigmoid(total)
        act_ref[rows, :] = (total * gate).astype(BF16)
        score = g_ref[rows, :].astype(F32) * gate * (1.0 + total * (1.0 - gate))
        st[:, rows] = jnp.transpose(score).astype(BF16)
    act_out = pltpu.make_async_copy(act_ref, act_hbm, out_sem.at[0])
    act_out.start()

    quarter = hidden // 2
    sizes, bases = [quarter], [0]
    for f in range(folds):
        sizes.append(sizes[-1] // 2)
        bases.append(bases[-1] + ((z // (1 << f)) % 2) * sizes[-1])

    def fold_copy(f):
        there = bases[f] + (1 - (z // (1 << f)) % 2) * sizes[f + 1]
        rows = pl.ds(pl.multiple_of(there, sizes[f + 1]), sizes[f + 1])
        return copy_to(
            ws.at[rows], w_in.at[f, pl.ds(0, sizes[f + 1])], w_send.at[f], w_recv.at[f], dev_fold[f], c
        )

    def cross_copy(i):
        return copy_to(
            w_cross.at[i], w_cross_in.at[i], w_send.at[folds + i], w_recv.at[folds + i],
            (dev_a, dev_b)[i], c,
        )

    def unfold_copy(f):
        rows = pl.ds(pl.multiple_of(bases[f + 1], sizes[f + 1]), sizes[f + 1])
        return copy_to(
            w_full.at[c, rows], w_full.at[c, rows], w_send.at[folds + 2 + f], w_recv.at[folds + 2 + f],
            dev_fold[f], c,
        )

    def weight_step(s):
        if s < folds:
            fold_copy(s).wait_recv()
            rows = pl.ds(pl.multiple_of(bases[s + 1], sizes[s + 1]), sizes[s + 1])
            ws[rows, :] += w_in[s, pl.ds(0, sizes[s + 1])]
            if s + 1 < folds:
                fold_copy(s + 1).start()
            else:
                w_cross[0] = ws[rows, :]
                cross_copy(0).start()
        elif s < folds + 2:
            i = s - folds
            cross_copy(i).wait_recv()
            if i == 0:
                w_cross[1] = w_cross[0] + w_cross_in[0]
                cross_copy(1).start()
            else:
                rows = pl.ds(pl.multiple_of(bases[folds], sizes[folds]), sizes[folds])
                w_full[c, rows] = w_cross[1] + w_cross_in[1]
                unfold_copy(folds - 1).start()
        else:
            f = 2 * folds + 1 - s
            unfold_copy(f).wait_recv()
            if f > 0:
                unfold_copy(f - 1).start()

    ws[...] = jnp.dot(
        st[pl.ds(pl.multiple_of(c * quarter, quarter), quarter), :], ax[...],
        preferred_element_type=F32,
    )
    fold_copy(0).start()

    near = jnp.minimum(z, layers - 1 - z)
    reach = layers - 1 - near
    long_side = jnp.where(z == near, 1, -1)

    def target_layer(t):
        u = t - (reach - near)
        return jnp.where(
            u < 0, z + long_side * (reach - t), z + (1 - 2 * (u % 2)) * (near - u // 2)
        )

    def piece(k):
        z_ = target_layer(k // 4)
        q = k % 4
        b_ = jnp.where(q < 2, 1 - b, b)
        a_ = jnp.where(q % 2 == 0, 1 - a, a)
        return z_, b_, a_, block_at(z_, b_, a_)

    def p_copy(j):
        return copy_to(ps.at[j, other], ps.at[j, other], p_send_p.at[j], p_recv_p.at[j], d, other)

    def b_copy(z_, a_):
        return copy_to(
            ps.at[block_at(z_, 1 - b, a_), c], from_b.at[z_, a_], b_send.at[z_, a_], b_recv.at[z_, a_],
            dev_b, c,
        )

    def a_copy(z_):
        return copy_to(
            ps.at[block_at(z_, b, 1 - a), c], from_a.at[z_], a_send.at[z_], a_recv.at[z_], dev_a, c
        )

    def z_copy(z_, up):
        return copy_to(
            ps.at[block_at(z_, b, a), c], from_z.at[up, z_], z_send.at[z_], z_recv.at[up, z_],
            d - 4 + 8 * up, c,
        )

    def backward(k):
        z_, b_, a_, j = piece(k)

        @pl.when(owner(j) == c)
        def _():
            o = (d - j + domains) % domains - c * sections
            m = flag(o)
            for h in range(2):
                ps[j, h] = (
                    jnp.dot(st[...], tiles[o, :, pl.ds(h * half, half)], preferred_element_type=F32) * m
                ).astype(BF16)
            p_copy(j).start()

            @pl.when(jnp.logical_and(b_ != b, k < 12))
            def _():
                b_copy(z_, a_).start()

    def relay_partner(k):
        z_, b_, a_, j = piece(k)

        @pl.when(owner(j) != c)
        def _():
            copy_to(ps.at[j, c], ps.at[j, c], p_send_p.at[j], p_recv_p.at[j], d, other).wait_recv()

            @pl.when(jnp.logical_and(b_ != b, k < 12))
            def _():
                b_copy(z_, a_).start()

    def backward_step(k, carry):
        @pl.when(k < domains)
        def _():
            backward(k)

        @pl.when(k >= 4)
        def _():
            relay_partner(k - 4)

        for f in range(folds):
            @pl.when(k == 8 * f + 6)
            def _():
                weight_step(f)

        return carry

    lax.fori_loop(0, domains + 4, backward_step, 0)

    def stage_a(t):
        z_ = target_layer(t)
        b_copy(z_, 1 - a).wait_recv()
        j = block_at(z_, b, 1 - a)
        ps[j, c] = (ps[j, c].astype(F32) + from_b[z_, 1 - a].astype(F32)).astype(BF16)
        a_copy(z_).start()

    def stage_z(t):
        z_ = target_layer(t)
        b_copy(z_, a).wait_recv()
        a_copy(z_).wait_recv()
        j = block_at(z_, b, a)

        def mine():
            return ps[j, c].astype(F32) + from_b[z_, a].astype(F32) + from_a[z_].astype(F32)

        @pl.when(z_ == z)
        def _():
            part[0] = mine()

        @pl.when(jnp.logical_and(z_ > z, z == 0))
        def _():
            ps[j, c] = mine().astype(BF16)
            z_copy(z_, 1).start()

        @pl.when(jnp.logical_and(z_ < z, z == layers - 1))
        def _():
            ps[j, c] = mine().astype(BF16)
            z_copy(z_, 0).start()

    def stage_relay(t):
        z_ = target_layer(t)
        j = block_at(z_, b, a)

        def pass_on(up):
            z_copy(z_, up).wait_recv()
            ps[j, c] = (
                ps[j, c].astype(F32) + from_b[z_, a].astype(F32) + from_a[z_].astype(F32)
                + from_z[up, z_].astype(F32)
            ).astype(BF16)
            z_copy(z_, up).start()

        @pl.when(jnp.logical_and(z_ > z, z > 0))
        def _():
            pass_on(1)

        @pl.when(jnp.logical_and(z_ < z, z < layers - 1))
        def _():
            pass_on(0)

    for r in range(2):
        part_copy(r).wait_send()

    stages = max(layers + 1, folds + 3)
    for t in range(stages):
        if t < layers:
            stage_a(t)
        if 1 <= t <= folds + 2:
            weight_step(folds + t - 1)
        if t + 3 < layers:
            b_copy(target_layer(t + 3), 1 - a).start()
            b_copy(target_layer(t + 3), a).start()
        if 1 <= t <= layers:
            stage_z(t - 1)
        if t == 2:
            stage_relay(0)
        if 2 <= t <= layers:
            stage_relay(t - 1)
    w_last = copy_to(w_full.at[c], w_full.at[c], last_send.at[0], last_recv.at[0], d, other)
    w_last.start()

    @pl.when(z > 0)
    def _():
        z_copy(z, 1).wait_recv()
        part[0] += from_z[1, z].astype(F32)

    @pl.when(z < layers - 1)
    def _():
        z_copy(z, 0).wait_recv()
        part[0] += from_z[0, z].astype(F32)

    node = jnp.transpose(part[0]).astype(BF16)
    fg_half[c] = lax.dot_general(
        node, w_ref[...], (((1,), (1,)), ((), ())), preferred_element_type=F32
    ).astype(BF16)
    f_last = copy_to(fg_half.at[c], fg_half.at[c], last_send.at[1], last_recv.at[1], d, other)
    f_last.start()

    def fg_out(h):
        return pltpu.make_async_copy(
            fg_half.at[h], fg_hbm.at[pl.ds(pl.multiple_of(h * half, half), half)], out_sem.at[1 + h]
        )

    fg_out(c).start()

    copy_to(w_full.at[other], w_full.at[other], last_send.at[0], last_recv.at[0], d, other).wait_recv()
    for h in range(2):
        wg_ref[:, pl.ds(h * quarter, quarter)] = jnp.transpose(w_full[h]) * scaling
    wg_out = pltpu.make_async_copy(wg_ref, wg_hbm, out_sem.at[3])
    wg_out.start()

    def drain_p(j, carry):
        @pl.when(jnp.logical_and(owner(j) != c, j != d))
        def _():
            x_copy_p(j).wait_send()
            y_copy_p(j).wait_send()

        @pl.when(owner(j) == c)
        def _():
            p_copy(j).wait_send()

        return carry

    lax.fori_loop(0, domains, drain_p, 0)

    def drain(z_, carry):
        @pl.when(jnp.logical_and(z_ <= z, z < layers - 1))
        def _():
            x_copy_z(block_at(z_, b, a), z_, 1).wait_send()
            y_slab(z_, 1).wait_send()

        @pl.when(jnp.logical_and(z_ >= z, z > 0))
        def _():
            x_copy_z(block_at(z_, b, a), z_, 0).wait_send()
            y_slab(z_, 0).wait_send()

        x_copy_a(block_at(z_, b, a), z_).wait_send()
        a_copy(z_).wait_send()
        for a_ in range(2):
            x_copy_b(block_at(z_, b, a_), z_, a_).wait_send()
            b_copy(z_, a_).wait_send()

        @pl.when(z_ > z)
        def _():
            z_copy(z_, 1).wait_send()

        @pl.when(z_ < z)
        def _():
            z_copy(z_, 0).wait_send()

        return carry

    lax.fori_loop(0, layers, drain, 0)
    y_copy_a().wait_send()
    for a_ in range(2):
        y_copy_b(a_).wait_send()
    for f in range(folds):
        fold_copy(f).wait_send()
        unfold_copy(f).wait_send()
    for i in range(2):
        cross_copy(i).wait_send()
    copy_to(fg_half.at[other], fg_half.at[other], last_send.at[1], last_recv.at[1], d, other).wait_recv()
    fg_out(other).start()
    w_last.wait_send()
    f_last.wait_send()
    act_out.wait()
    wg_out.wait()
    for h in range(2):
        fg_out(h).wait()


def finish_kernel(act, fg, wg, act_out, fg_out, wg_out, act_v, fg_v, wg_v, sem):
    pairs = ((act, act_v, act_out), (fg, fg_v, fg_out), (wg, wg_v, wg_out))
    inward = [pltpu.make_async_copy(p[0], p[1], sem.at[0, i]) for i, p in enumerate(pairs)]
    outward = [pltpu.make_async_copy(p[1], p[2], sem.at[1, i]) for i, p in enumerate(pairs)]
    for copy in inward:
        copy.start()
    for first, second in zip(inward, outward):
        first.wait()
        second.start()
    for copy in outward:
        copy.wait()


def kernel_shards(features, weight, grad_out, tiles, tile_mask):
    domains = lax.axis_size("dom")
    layers = domains // 4
    folds = layers.bit_length() - 1
    sections = tiles.shape[1]
    rows, hidden = features.shape
    half, quarter = rows // 2, hidden // 2
    dma = pltpu.SemaphoreType.DMA
    out_shape = (
        jax.ShapeDtypeStruct((rows, hidden), BF16),
        jax.ShapeDtypeStruct((rows, hidden), BF16),
        jax.ShapeDtypeStruct((hidden, hidden), F32),
    )
    anywhere = [pl.BlockSpec(memory_space=pl.ANY)] * 3
    results = pl.pallas_call(
        functools.partial(layer_kernel, domains, float((rows * domains) ** (-0.5))),
        out_shape=out_shape,
        in_specs=[pl.BlockSpec(memory_space=pltpu.HBM)] * 4 + [pl.BlockSpec(memory_space=pltpu.SMEM)],
        out_specs=anywhere,
        scratch_shapes=[
            pltpu.VMEM((rows, hidden), BF16),
            pltpu.VMEM((hidden, hidden), F32),
            pltpu.VMEM(weight.shape, BF16),
            pltpu.VMEM((rows, hidden), BF16),
            pltpu.VMEM(tiles.shape[1:], BF16),
            pltpu.VMEM((domains, 2, half, hidden), BF16),
            pltpu.VMEM((domains, 2, hidden, half), BF16),
            pltpu.VMEM((layers, 2, hidden, half), BF16),
            pltpu.VMEM((layers, hidden, half), BF16),
            pltpu.VMEM((2, layers, hidden, half), BF16),
            pltpu.VMEM((2, half, hidden), F32),
            pltpu.VMEM((2, half, hidden), BF16),
            pltpu.VMEM((2, half, hidden), BF16),
            pltpu.VMEM((rows, hidden), BF16),
            pltpu.VMEM((hidden, rows), BF16),
            pltpu.VMEM((quarter, hidden), F32),
            pltpu.VMEM((folds, quarter // 2, hidden), F32),
            pltpu.VMEM((2, quarter // layers, hidden), F32),
            pltpu.VMEM((2, quarter // layers, hidden), F32),
            pltpu.VMEM((2, quarter, hidden), F32),
            pltpu.VMEM((2, half, hidden), BF16),
            dma((2,)), dma((3,)), dma((4,)),
            dma((domains,)), dma((domains,)),
            dma((2, layers)), dma((layers,)), dma((layers, 2)), dma((domains,)),
            dma((3,)), dma((4,)), dma((2, layers)), dma((layers,)), dma((domains,)), dma((domains,)),
            dma((2,)), dma((2,)),
            dma((domains,)), dma((domains,)),
            dma((layers, 2)), dma((layers, 2)),
            dma((layers,)), dma((layers,)),
            dma((layers,)), dma((2, layers)),
            dma((2 * folds + 2,)), dma((2 * folds + 2,)),
            dma((2,)), dma((2,)),
        ],
        compiler_params=pltpu.CompilerParams(
            collective_id=0, has_side_effects=True, vmem_limit_bytes=63 * 1024 * 1024
        ),
        cost_estimate=pl.CostEstimate(
            flops=4 * sections * rows * rows * hidden,
            bytes_accessed=2 * sections * rows * rows,
            transcendentals=rows * hidden,
        ),
    )(features, weight, grad_out, tiles, tile_mask)
    return pl.pallas_call(
        finish_kernel,
        out_shape=out_shape,
        in_specs=anywhere,
        out_specs=anywhere,
        scratch_shapes=[
            pltpu.VMEM((rows, hidden), BF16),
            pltpu.VMEM((rows, hidden), BF16),
            pltpu.VMEM((hidden, hidden), F32),
            dma((2, 3)),
        ],
        compiler_params=pltpu.CompilerParams(vmem_limit_bytes=63 * 1024 * 1024),
        cost_estimate=pl.CostEstimate(flops=0, bytes_accessed=6 * rows * hidden * 2, transcendentals=0),
    )(*results)


def solution(mesh):
    domains, replicas = mesh.shape["dom"], mesh.shape["rep"]
    paired = replicas == 2 and domains >= 8 and domains & (domains - 1) == 0
    placed = (P("dom", None), P(), P("dom", None), P("dom", "rep", None, None), P("dom", "rep"))
    return jax.shard_map(
        kernel_shards if paired else ring_shards,
        mesh=mesh,
        in_specs=placed,
        out_specs=(P("dom", None), P("dom", None), P()),
        check_vma=False,
    )
```
